32 devices in a mesh: wide: 16 (over z, y, x), narrow: 2 (over core).
Axes of the slice: x: 2, y: 2, z: 4, core: 2. Of those that a mesh axis runs over, the one named last changes fastest.
Arguments:
- char_ids: int32 [4096, 50], P('wide'), may hold values from 0 to 261
- char_mask: int32 [4096, 50], P('wide'), may hold values 0 or 1
- word_lengths: int32 [4096], P('wide'), may hold values from 1 to 50, as said below
- char_table: bfloat16 [262, 16], replicated, may hold values from -6 to 6
- conv_weight: bfloat16 [112, 2048], P(None, 'narrow'), may hold values from -0.5 to 0.5
- conv_bias: float32 [2048], P('narrow'), may hold values from -4 to 4
- highway_weight: bfloat16 [2, 2048, 2, 2048], P(None, 'wide', None, 'narrow'), may hold values from -0.125 to 0.125
- highway_bias: float32 [2, 2, 2048], P(None, None, 'narrow'), may hold values from -6 to 6
- proj_weight: bfloat16 [2048, 768], P('narrow', 'wide'), may hold values from -0.125 to 0.125
- qkv_weight: bfloat16 [768, 3, 768], P('wide', None, 'narrow'), may hold values from -0.21875 to 0.21875
- qv_bias: float32 [2, 768], P(None, 'narrow'), may hold values from -4 to 4
- out_weight: bfloat16 [768, 768], P('narrow', 'wide'), may hold values from -0.875 to 0.875
- up_weight: bfloat16 [768, 3072], P('wide', 'narrow'), may hold values from -0.21875 to 0.21875
- up_bias: float32 [3072], P('narrow'), may hold values from -4 to 4
- down_weight: bfloat16 [3072, 768], P('narrow', 'wide'), may hold values from -0.109375 to 0.109375
- vector_biases: float32 [5, 768], replicated, may hold values from -4 to 4
- norm_gains: float32 [2, 768], replicated, may hold values from 0.5 to 1.5
- cotangent: bfloat16 [4096, 768], P('wide'), may hold values from -6 to 6
Outputs:
- encoded: bfloat16 [4096, 768], P('wide')
- char_grad: float32 [262, 16], replicated
- conv_grad: float32 [112, 2048], P(None, 'narrow')
- conv_bias_grad: float32 [2048], P('narrow')
- highway_grad: float32 [2, 2048, 2, 2048], P(None, 'wide', None, 'narrow')
- highway_bias_grad: float32 [2, 2, 2048], P(None, None, 'narrow')
- proj_grad: float32 [2048, 768], P('narrow', 'wide')
- qkv_grad: float32 [768, 3, 768], P('wide', None, 'narrow')
- qv_bias_grad: float32 [2, 768], P(None, 'narrow')
- out_grad: float32 [768, 768], P('narrow', 'wide')
- up_grad: float32 [768, 3072], P('wide', 'narrow')
- up_bias_grad: float32 [3072], P('narrow')
- down_grad: float32 [3072, 768], P('narrow', 'wide')
- bias_grads: float32 [5, 768], replicated
- gain_grads: float32 [2, 768], replicated
The draws below stay inside these ranges and needn't reach their ends.
Inputs may be any that keep to these rules, and one draw needn't show every extreme that they name: `word_lengths`: in every sequence of 128 words some word has 50 characters; lengths are heavy-tailed.
All inputs are finite; a program needn't handle non-finite values. No bound on the sum of `char_mask` on one device may be relied on, other than what follows from the above.
Results may differ from the reference program's by a relative error of at most 0.014.
Values may be sent and summed in bfloat16 or wider, within the bound.
No kernel may reach another device: no remote copies, remote signals or barrier semaphores. Data moves between devices by JAX's collectives and lax.ppermute only.
A program may use at most 192 MiB of HBM per device.

```python
import math
import jax
import jax.numpy as jnp
import numpy as np
from jax import lax

D = 768
HEADS = 12
HEAD_DIM = 64
FF = 3072
FILTERS = 2048
CHAR_DIM = 16
CHAR_VOCAB = 262
CHARS_MAX = 50
TAPS = 7
HW_LAYERS = 2
LENGTH = 128
WORDS = 4096


def draw_word_lengths(key, part):
    key = jax.random.fold_in(key, 11)
    key_scale, key_value, key_place = jax.random.split(key, 3)
    exponent = jax.random.randint(key_scale, (WORDS,), 0, 7)
    spread = jnp.left_shift(jnp.ones((WORDS,), jnp.int32), exponent)
    lengths = 1 + jax.random.randint(key_value, (WORDS,), 0, spread)
    lengths = jnp.minimum(lengths, CHARS_MAX)
    sequences = WORDS // LENGTH
    place = jax.random.randint(key_place, (sequences,), 0, LENGTH)
    longest = jnp.arange(LENGTH)[None, :] == place[:, None]
    return jnp.where(longest, CHARS_MAX, lengths.reshape(sequences, LENGTH)).reshape(WORDS).astype(jnp.int32)


def set_ends(entries, stream_key, low, largest):
    spot = [jax.random.randint(jax.random.fold_in(stream_key, axis), (), 0, length) for axis, length in enumerate(entries.shape)]
    widest = entries.shape.index(max(entries.shape))
    next_to = spot[:widest] + [(spot[widest] + 1) % entries.shape[widest]] + spot[widest + 1:]
    return entries.at[tuple(spot)].set(low).at[tuple(next_to)].set(largest)


def shard_levels(rng, extent, cuts, least, largest):
    loudness, own = 1.0, jax.random.fold_in(rng, 6)
    for position, parts in cuts:
        draws = jnp.exp(jax.random.uniform(jax.random.fold_in(own, position), (parts,), jnp.float32, least / len(cuts), largest / len(cuts)))
        loudness = loudness * jnp.repeat(draws, extent[position] // parts).reshape([-1 if axis == position else 1 for axis in range(len(extent))])
    return loudness


def cumulative_ranks(amount, lean):
    loads = [(1 << 20) // math.isqrt(grade ** lean) + 1 for grade in range(1, amount + 1)]
    scale = 1 + sum(loads) // (1 << 30)
    return np.cumsum(np.array([max(1, weight // scale) for weight in loads]))


def skewed_ids(own_key, dims, count, lean):
    table = cumulative_ranks(count, lean)
    ticket = jax.random.randint(jax.random.fold_in(own_key, 1), dims, 0, int(table[count - 1]))
    standing = jnp.searchsorted(jnp.asarray(table, jnp.int32), ticket, side="right")
    return jax.random.permutation(jax.random.fold_in(own_key, 2), count)[standing].astype(jnp.int32)


def centred(own_key, extent, scale, most, cuts=(), kind=jnp.bfloat16):
    level = shard_levels(own_key, extent, cuts, -0.22, 0.18) if cuts else 1.0
    array = jax.random.normal(own_key, extent, jnp.float32) * scale * level
    return jnp.minimum(jnp.maximum(array, -most), most).astype(kind)


def setup_inputs(seed: int = 0) -> dict:
    splits = jax.random.split(jax.random.key(seed), 19)
    char_ids = set_ends(skewed_ids(splits[0], (WORDS, CHARS_MAX), CHAR_VOCAB, 2), jax.random.fold_in(splits[0], 3), 0, CHAR_VOCAB - 1).astype(jnp.int32)
    char_mask = set_ends((jax.random.randint(splits[1], (WORDS, CHARS_MAX), 0, 8) < 7).astype(jnp.int32), jax.random.fold_in(splits[1], 1), 0, 1)
    word_lengths = draw_word_lengths(jax.random.fold_in(splits[18], 71), 0)
    char_table = centred(splits[3], (CHAR_VOCAB, CHAR_DIM), 1.0, 6.0)
    conv_weight = centred(splits[4], (TAPS * CHAR_DIM, FILTERS), (TAPS * CHAR_DIM) ** -0.5, 0.5, ((1, 2),))
    conv_bias = centred(splits[5], (FILTERS,), 0.3, 4.0, ((0, 2),), jnp.float32)
    highway_weight = centred(splits[6], (HW_LAYERS, FILTERS, 2, FILTERS), FILTERS ** -0.5, 0.125, ((1, 16), (3, 2)))
    highway_bias = centred(splits[7], (HW_LAYERS, 2, FILTERS), 0.5, 6.0, ((2, 2),), jnp.float32)
    proj_weight = centred(splits[8], (FILTERS, D), FILTERS ** -0.5, 0.125, ((0, 2), (1, 16)))
    qkv_weight = centred(splits[9], (D, 3, D), D ** -0.5, 0.21875, ((0, 16), (2, 2)))
    qv_bias = centred(splits[10], (2, D), 0.3, 4.0, ((1, 2),), jnp.float32)
    out_weight = centred(splits[11], (D, D), (D // 16) ** -0.5, 0.875, ((0, 2), (1, 16)))
    up_weight = centred(splits[12], (D, FF), D ** -0.5, 0.21875, ((0, 16), (1, 2)))
    up_bias = centred(splits[13], (FF,), 0.3, 4.0, ((0, 2),), jnp.float32)
    down_weight = centred(splits[14], (FF, D), FF ** -0.5, 0.109375, ((0, 2), (1, 16)))
    vector_biases = centred(splits[15], (5, D), 0.3, 4.0, (), jnp.float32)
    norm_gains = jnp.clip(1.0 + 0.1 * jax.random.normal(splits[16], (2, D), jnp.float32), 0.5, 1.5)
    cotangent = centred(splits[17], (WORDS, D), 1.0, 6.0, ((0, 16),))
    return {"char_ids": char_ids, "char_mask": char_mask, "word_lengths": word_lengths, "char_table": char_table, "conv_weight": conv_weight, "conv_bias": conv_bias, "highway_weight": highway_weight, "highway_bias": highway_bias, "proj_weight": proj_weight, "qkv_weight": qkv_weight, "qv_bias": qv_bias, "out_weight": out_weight, "up_weight": up_weight, "up_bias": up_bias, "down_weight": down_weight, "vector_biases": vector_biases, "norm_gains": norm_gains, "cotangent": cotangent}


BOUNDS = ((1, 2), (3, 4), (7, 8), (15, 16), (31, 32), (63, 64))
EPSILON = 1e-06

@jax.custom_vjp
def low(v):
    return lax.optimization_barrier(v.astype(jnp.bfloat16)).astype(jnp.float32)

@jax.custom_vjp
def low_back(v):
    return v

def low_keep(v):
    return (low(v), None)

def low_pass(kept, grad):
    return (grad,)

def back_keep(v):
    return (v, None)

def back_low(kept, grad):
    return (low(grad),)
low.defvjp(low_keep, low_pass)
low_back.defvjp(back_keep, back_low)

def channel_widths(first_channel, count):
    channels = first_channel + jnp.arange(count, dtype=jnp.int32)
    widths = jnp.full((count,), TAPS, jnp.int32)
    for numerator, denominator in BOUNDS:
        widths = widths - (channels >= FILTERS * numerator // denominator).astype(jnp.int32)
    return widths

def tap_columns(embedded):
    char_slots = embedded.shape[1]
    padded = jnp.pad(embedded, ((0, 0), (0, TAPS - 1), (0, 0)))
    return jnp.concatenate([padded[:, offset:offset + char_slots, :] for offset in range(TAPS)], axis=-1)

def pool_windows(convolved, lengths, widths, chan_scale, conv_bias):
    shifted_in = convolved * chan_scale + conv_bias
    counts = jnp.maximum(lengths[:, None] - widths[None, :] + 1, 1)
    places = jnp.arange(convolved.shape[1], dtype=jnp.int32)
    valid = places[None, :, None] < counts[:, None, :]
    summit = lax.optimization_barrier(jnp.max(jnp.where(valid, shifted_in, -1e+30), axis=1))
    exponent = jnp.where(valid, shifted_in - summit[:, None, :], -80.0)
    weights = jnp.where(valid, jnp.exp(exponent), 0.0)
    totals = lax.optimization_barrier(jnp.sum(weights, axis=1))
    pooled = summit + jnp.log(totals) - jnp.log(counts.astype(jnp.float32))
    return (pooled, weights / totals[:, None, :])

def gelu_exact(values):
    return jax.nn.gelu(values, approximate=False)

def layer_norm(values, gain_row, bias_row):
    center = lax.optimization_barrier(jnp.mean(values, axis=-1, keepdims=True))
    spread = lax.optimization_barrier(jnp.mean(jnp.square(values - center), axis=-1, keepdims=True))
    return (values - center) * lax.rsqrt(spread + EPSILON) * gain_row + bias_row

def highway_mix(mixed_pre, carried):
    gate_value = jax.nn.sigmoid(mixed_pre[:, 1])
    return gate_value * carried + (1.0 - gate_value) * gelu_exact(mixed_pre[:, 0])

def forward_sequence(params, row_ids, row_alive, row_lengths):
    char_table, conv_weight, conv_bias, highway_weight, highway_bias, proj_weight, qkv_weight, qv_bias, out_weight, up_weight, up_bias, down_weight, vector_biases, norm_gains = params
    highest = lax.Precision.HIGHEST
    widths = channel_widths(0, FILTERS)
    tap_rows = jnp.arange(TAPS * CHAR_DIM, dtype=jnp.int32) // CHAR_DIM
    tap_mask = (tap_rows[:, None] < widths[None, :]).astype(jnp.float32)
    chan_scale = jnp.sqrt(TAPS / widths.astype(jnp.float32))
    embedded = char_table[row_ids] * row_alive[:, :, None]
    columns = tap_columns(embedded)
    convolved = low_back(jnp.einsum('wpt,tf->wpf', columns, conv_weight * tap_mask, precision=highest))
    pooled = pool_windows(convolved, row_lengths, widths, chan_scale, conv_bias)[0]
    current = low(gelu_exact(pooled))
    for layer_index in range(HW_LAYERS):
        mixed_pre = low_back(jnp.einsum('wi,igf->wgf', current, highway_weight[layer_index], precision=highest) + highway_bias[layer_index])
        current = low(highway_mix(mixed_pre, current))
    start_rows = low_back(jnp.dot(current, proj_weight, precision=highest) + vector_biases[0])
    start_low = low(start_rows)
    qkv_bias = jnp.stack([qv_bias[0], jnp.zeros_like(qv_bias[0]), qv_bias[1]])
    projected = low(low_back(jnp.einsum('wd,dgc->wgc', start_low, qkv_weight, precision=highest) + qkv_bias))
    word_count = projected.shape[0]
    query = projected[:, 0].reshape(word_count, HEADS, HEAD_DIM)
    keys_here = projected[:, 1].reshape(word_count, HEADS, HEAD_DIM)
    values_here = projected[:, 2].reshape(word_count, HEADS, HEAD_DIM)
    scores = low_back(jnp.einsum('qhe,khe->hqk', query, keys_here, precision=highest) * HEAD_DIM ** (-0.5))
    probs_low = low(jax.nn.softmax(scores, axis=-1))
    context = low(low_back(jnp.einsum('hqk,khe->qhe', probs_low, values_here, precision=highest).reshape(word_count, D)))
    attended = low_back(jnp.dot(context, out_weight, precision=highest) + vector_biases[1])
    normed_one = layer_norm(start_rows + attended, norm_gains[0], vector_biases[3])
    hidden_pre = low_back(jnp.dot(low(normed_one), up_weight, precision=highest) + up_bias)
    hidden_low = low(gelu_exact(hidden_pre))
    lowered = low_back(jnp.dot(hidden_low, down_weight, precision=highest) + vector_biases[2])
    return layer_norm(normed_one + lowered, norm_gains[1], vector_biases[4])

def reference(char_ids, char_mask, word_lengths, char_table, conv_weight, conv_bias, highway_weight, highway_bias, proj_weight, qkv_weight, qv_bias, out_weight, up_weight, up_bias, down_weight, vector_biases, norm_gains, cotangent):
    params = tuple((argument.astype(jnp.float32) for argument in (char_table, conv_weight, conv_bias, highway_weight, highway_bias, proj_weight, qkv_weight, qv_bias, out_weight, up_weight, up_bias, down_weight, vector_biases, norm_gains)))
    places = jnp.arange(CHARS_MAX, dtype=jnp.int32)
    alive = (char_mask * (places[None, :] < word_lengths[:, None]).astype(jnp.int32)).astype(jnp.float32)
    sequences = char_ids.shape[0] // LENGTH
    inputs = (char_ids.reshape(sequences, LENGTH, CHARS_MAX), alive.reshape(sequences, LENGTH, CHARS_MAX), word_lengths.reshape(sequences, LENGTH), cotangent.astype(jnp.float32).reshape(sequences, LENGTH, D))

    def one_sequence(running, pieces):
        row_ids, row_alive, row_lengths, row_cotangent = pieces
        outputs, pullback = jax.vjp(lambda weights: forward_sequence(weights, row_ids, row_alive, row_lengths), params)
        grads = pullback(row_cotangent)[0]
        return (jax.tree.map(jnp.add, running, grads), outputs.astype(jnp.bfloat16))
    totals, encoded = lax.scan(one_sequence, jax.tree.map(jnp.zeros_like, params), inputs)
    return (encoded.reshape(sequences * LENGTH, D), totals[0], totals[1], totals[2], totals[3], totals[4], totals[5], totals[6], totals[7], totals[8], totals[9], totals[10], totals[11], totals[12], totals[13])
```

```python
from functools import partial, reduce

import jax
import jax.numpy as jnp
from jax import lax
from jax.experimental import pallas as pl
from jax.experimental.pallas import tpu as pltpu
from jax.sharding import PartitionSpec as P

HEAD_DIM = 64
FILTERS = 2048
CHAR_DIM = 16
CHAR_VOCAB = 262
CHARS_MAX = 50
TAPS = 7
HW_LAYERS = 2
TILE = 16
CHUNK = 8
SLOTS = 64
IDS = 272
LANES = 128
BLOCK = 256
LOG2E = 1.4426950408889634
LENGTH = 128


BOUNDS = ((1, 2), (3, 4), (7, 8), (15, 16), (31, 32), (63, 64))
EPSILON = 1e-06


def channel_widths(first_channel, count):
    channels = first_channel + jnp.arange(count, dtype=jnp.int32)
    widths = jnp.full((count,), TAPS, jnp.int32)
    for numerator, denominator in BOUNDS:
        widths = widths - (channels >= FILTERS * numerator // denominator).astype(jnp.int32)
    return widths


def gelu_exact(values):
    return jax.nn.gelu(values, approximate=False)


def layer_norm(values, gain_row, bias_row):
    center = jnp.mean(values, axis=-1, keepdims=True)
    spread = jnp.mean(jnp.square(values - center), axis=-1, keepdims=True)
    return (values - center) * lax.rsqrt(spread + EPSILON) * gain_row + bias_row


def highway_mix(mixed_pre, carried):
    gate_value = jax.nn.sigmoid(mixed_pre[:, 1])
    return gate_value * carried + (1.0 - gate_value) * gelu_exact(mixed_pre[:, 0])


def word_order(lengths):
    words = lengths.shape[0]
    sequences = words // LENGTH
    spots = jnp.arange(words, dtype=jnp.int32)
    keys = lengths * LENGTH + (LENGTH - 1 - spots % LENGTH)
    same = spots[:, None] // LENGTH == spots[None, :] // LENGTH
    ranks = jnp.sum((same & (keys[None, :] > keys[:, None])).astype(jnp.int32), axis=1)
    places = ranks // 8 * (8 * sequences) + spots // LENGTH * 8 + ranks % 8
    return (places[None, :] == spots[:, None]).astype(jnp.float32)


def spot_chars(ids_row, table_t):
    ids = lax.broadcasted_iota(jnp.int32, (IDS, LANES), 0)
    marks = (ids == ids_row).astype(jnp.float32).astype(jnp.bfloat16)
    return jnp.dot(table_t, marks, preferred_element_type=jnp.float32).T.astype(jnp.bfloat16)


def tap_rows(table_ref, start, tile, tap_lanes):
    rows = pl.ds(pl.multiple_of(tile * TILE, TILE), TILE)
    taken = None
    for tap in range(TAPS):
        piece = table_ref[pl.ds(start + tap, CHUNK), rows, :] * tap_lanes[tap][None]
        taken = piece if taken is None else taken + piece
    return taken.reshape(CHUNK * TILE, LANES)


def window_counts(lens_ref, widths_ref, tile):
    rows = pl.ds(pl.multiple_of(tile * TILE, TILE), TILE)
    return jnp.maximum(lens_ref[rows, :1] - widths_ref[...] + 1.0, 1.0)


def pool_kernel(
    tile_ref, ids_ref, table_ref, lanes_ref, filters_ref, scale_ref, bias_ref, lens_ref, widths_ref,
    embed_ref, pooled_ref, shift_ref, conv_ref, count_ref, top_ref,
):
    channels = filters_ref.shape[1]
    chunks_all = SLOTS // CHUNK
    tap_lanes = [lanes_ref[tap : tap + 1, :].astype(jnp.bfloat16) for tap in range(TAPS)]
    blocks = [slice(first, first + BLOCK) for first in range(0, channels, BLOCK)]

    def one_tile(tile, _):
        rows = pl.ds(pl.multiple_of(tile * TILE, TILE), TILE)
        chunks = tile_ref[tile]

        def embed(chunk, _):
            found = spot_chars(ids_ref[pl.ds(tile * chunks_all + chunk, 1), :], table_ref[...])
            embed_ref[pl.ds(chunk * CHUNK, CHUNK), rows, :] = found.reshape(CHUNK, TILE, LANES)
            return 0

        lax.fori_loop(0, chunks, embed, 0)
        embed_ref[pl.ds(chunks * CHUNK, CHUNK), rows, :] = jnp.zeros(
            (CHUNK, TILE, LANES), jnp.bfloat16
        )
        count_ref[...] = window_counts(lens_ref, widths_ref, tile)
        top_ref[...] = jnp.full(top_ref.shape, -1e30, jnp.float32)

        def convolve(chunk, _):
            columns = tap_rows(embed_ref, chunk * CHUNK, tile, tap_lanes)
            first = (chunk * CHUNK).astype(jnp.float32)
            for block in blocks:
                convolved = jnp.dot(
                    columns, filters_ref[:, block], preferred_element_type=jnp.float32
                )
                conv_ref[chunk, :, block] = convolved
                counts = count_ref[:, block] - first
                top = top_ref[:, block]
                for place in range(CHUNK):
                    row = convolved[place * TILE : (place + 1) * TILE]
                    top = jnp.maximum(top, jnp.where(counts > float(place), row, -1e30))
                top_ref[:, block] = top
            return 0

        lax.fori_loop(0, chunks, convolve, 0)
        pooled_ref[rows, :] = jnp.zeros((TILE, channels), jnp.float32)

        def weigh(chunk, _):
            first = (chunk * CHUNK).astype(jnp.float32)
            for block in blocks:
                counts = count_ref[:, block] - first
                scale = scale_ref[:, block] * LOG2E
                offset = top_ref[:, block] * scale
                total = pooled_ref[rows, block]
                for place in range(CHUNK):
                    row = conv_ref[chunk, place * TILE : (place + 1) * TILE, block]
                    weight = jnp.exp2(row * scale - offset)
                    total = total + jnp.where(counts > float(place), weight, 0.0)
                pooled_ref[rows, block] = total
            return 0

        lax.fori_loop(0, chunks, weigh, 0)
        top = top_ref[...] * scale_ref[...]
        log_total = jnp.log(pooled_ref[rows, :])
        pooled_ref[rows, :] = top + bias_ref[...] + log_total - jnp.log(count_ref[...])
        shift_ref[rows, :] = (top + log_total) * -LOG2E
        return 0

    lax.fori_loop(0, tile_ref.shape[0], one_tile, 0)


def pool_back_kernel(
    tile_ref, ids_ref, lanes_ref, filters_ref, scale_ref, lens_ref, widths_ref, embed_ref, shift_ref,
    grad_ref, filter_grad_ref, char_grad_ref, conv_grad_ref, column_ref, count_ref,
):
    channels = filters_ref.shape[1]
    chunks_all = SLOTS // CHUNK
    tap_lanes = [lanes_ref[tap : tap + 1, :].astype(jnp.bfloat16) for tap in range(TAPS)]
    lane_taps = lax.broadcasted_iota(jnp.int32, (1, 1, LANES), 2) // CHAR_DIM
    blocks = [slice(first, first + BLOCK) for first in range(0, channels, BLOCK)]
    filter_grad_ref[...] = jnp.zeros(filter_grad_ref.shape, jnp.float32)
    char_grad_ref[...] = jnp.zeros(char_grad_ref.shape, jnp.float32)
    column_ref[:CHUNK] = jnp.zeros((CHUNK, TILE, LANES), jnp.float32)

    def one_tile(tile, _):
        rows = pl.ds(pl.multiple_of(tile * TILE, TILE), TILE)
        chunks = tile_ref[tile]
        count_ref[...] = window_counts(lens_ref, widths_ref, tile)

        def one_chunk(chunk, _):
            columns = tap_rows(embed_ref, chunk * CHUNK, tile, tap_lanes)
            columns_t = columns.astype(jnp.float32).T.astype(jnp.bfloat16)
            first = (chunk * CHUNK).astype(jnp.float32)
            grad_columns = None
            for block in blocks:
                filters = filters_ref[:, block]
                convolved = jnp.dot(columns, filters, preferred_element_type=jnp.float32)
                counts = count_ref[:, block] - first
                scale = scale_ref[:, block]
                scale2 = scale * LOG2E
                shift = shift_ref[rows, block]
                grad = grad_ref[rows, block] * scale
                for place in range(CHUNK):
                    row = convolved[place * TILE : (place + 1) * TILE]
                    share = jnp.exp2(row * scale2 + shift)
                    conv_grad_ref[place * TILE : (place + 1) * TILE, block] = jnp.where(
                        counts > float(place), share * grad, 0.0
                    ).astype(jnp.bfloat16)
                conv_grad = conv_grad_ref[:, block]
                filter_grad_ref[:, block] += jnp.dot(
                    columns_t, conv_grad, preferred_element_type=jnp.float32
                )
                piece = lax.dot_general(
                    conv_grad, filters, (((1,), (1,)), ((), ())), preferred_element_type=jnp.float32
                )
                grad_columns = piece if grad_columns is None else grad_columns + piece
            column_ref[pl.ds(chunk * CHUNK + CHUNK, CHUNK)] = grad_columns.reshape(
                CHUNK, TILE, LANES
            )
            return 0

        lax.fori_loop(0, chunks, one_chunk, 0)

        def fold(chunk, _):
            moved = None
            for tap in range(TAPS):
                piece = column_ref[pl.ds(chunk * CHUNK + CHUNK - tap, CHUNK)]
                moved = piece if moved is None else jnp.where(lane_taps == tap, piece, moved)
            moved = moved.reshape(CHUNK * TILE, LANES)
            high = moved.astype(jnp.bfloat16)
            low = (moved - high.astype(jnp.float32)).astype(jnp.bfloat16)
            ids = lax.broadcasted_iota(jnp.int32, (IDS, LANES), 0)
            ids_row = ids_ref[pl.ds(tile * chunks_all + chunk, 1), :]
            marks = (ids == ids_row).astype(jnp.float32).astype(jnp.bfloat16)
            char_grad_ref[...] += jnp.dot(
                marks, jnp.concatenate([high, low], axis=1), preferred_element_type=jnp.float32
            )
            return 0

        lax.fori_loop(0, chunks, fold, 0)
        return 0

    lax.fori_loop(0, tile_ref.shape[0], one_tile, 0)


def conv_calls(words, channels):
    vmem = pl.BlockSpec(memory_space=pltpu.VMEM)
    smem = pl.BlockSpec(memory_space=pltpu.SMEM)
    shape = partial(jax.ShapeDtypeStruct, dtype=jnp.float32)
    params = pltpu.CompilerParams(vmem_limit_bytes=40 * 1024 * 1024)
    pool = pl.pallas_call(
        pool_kernel,
        out_shape=[
            jax.ShapeDtypeStruct((SLOTS, words, LANES), jnp.bfloat16),
            shape((words, channels)),
            shape((words, channels)),
        ],
        in_specs=[smem] + [vmem] * 8,
        out_specs=[vmem] * 3,
        scratch_shapes=[
            pltpu.VMEM((SLOTS // CHUNK, CHUNK * TILE, channels), jnp.float32),
            pltpu.VMEM((TILE, channels), jnp.float32),
            pltpu.VMEM((TILE, channels), jnp.float32),
        ],
        compiler_params=params,
        cost_estimate=pl.CostEstimate(
            flops=5_000_000_000, bytes_accessed=8_000_000, transcendentals=5_000_000
        ),
    )
    back = pl.pallas_call(
        pool_back_kernel,
        out_shape=[shape((LANES, channels)), shape((IDS, 2 * LANES))],
        in_specs=[smem] + [vmem] * 9,
        out_specs=[vmem] * 2,
        scratch_shapes=[
            pltpu.VMEM((CHUNK * TILE, channels), jnp.bfloat16),
            pltpu.VMEM((SLOTS + CHUNK, TILE, LANES), jnp.float32),
            pltpu.VMEM((TILE, channels), jnp.float32),
        ],
        compiler_params=params,
        cost_estimate=pl.CostEstimate(
            flops=10_000_000_000, bytes_accessed=10_000_000, transcendentals=5_000_000
        ),
    )
    return pool, back


STEPS = {
    "x": [(i, i ^ 1) for i in range(16)],
    "y": [(i, i ^ 2) for i in range(16)],
    "z": [(i, (i + 4) % 16) for i in range(16)],
}
PLACE = {"z": 0, "y": 1, "x": 2}
CHIPS = 16
SWAP = [(0, 1), (1, 0)]


def step(value, axis):
    return lax.ppermute(value, "wide", STEPS[axis])


def swap(value):
    return lax.ppermute(value, "narrow", SWAP)


def joined(pieces):
    return pieces[0] if len(pieces) == 1 else jnp.concatenate(pieces, axis=0)


def blocks_after(axes):
    blocks = [(0, 0, 0)]
    for axis in axes:
        place = PLACE[axis]
        count = 4 if axis == "z" else 2
        blocks = [
            block[:place] + (away,) + block[place + 1 :] for away in range(count) for block in blocks
        ]
    return blocks


def owners(axes, here):
    z, y, x = here // 4, (here // 2) % 2, here % 2
    return jnp.stack(
        [
            ((z - dz) % 4) * 4 + (y + dy) % 2 * 2 + (x + dx) % 2
            for dz, dy, dx in blocks_after(axes)
        ]
    ).astype(jnp.int32)


def gather_blocks(shard, axes):
    pieces = [shard]
    for axis in axes:
        pieces = [joined(pieces)]
        for _ in range(3 if axis == "z" else 1):
            pieces.append(step(pieces[-1], axis))
    return pieces


def add(one, other):
    return one.astype(jnp.float32) + other.astype(jnp.float32)


def scatter_blocks(pieces, axes, dtype=jnp.bfloat16):
    for place in reversed(range(len(axes))):
        axis = axes[place]
        travelling = pieces[1].astype(dtype)
        for later in pieces[2:]:
            travelling = add(later, step(travelling, axis)).astype(dtype)
        total = add(pieces[0], step(travelling, axis))
        if place:
            count = 4 if axes[place - 1] == "z" else 2
            pieces = jnp.split(total.astype(dtype), count, axis=0)
    return total


def reorder(rows, old, new):
    height = rows.shape[0] // len(old)
    if old == new:
        return rows
    return joined([rows[old.index(block) * height :][:height] for block in new])


def pair_sum(partial_value):
    return partial_value + swap(partial_value)


def pair_grad_sum(partial_value):
    low = partial_value.astype(jnp.bfloat16)
    return add(low, swap(low))


def permute_kernel(order_ref, own_ref, other_ref, *out_refs):
    count = own_ref.shape[1] // 128
    for part, out_ref in enumerate(out_refs):
        for block in range(2 * count):
            source = order_ref[part, block]
            offset = pl.multiple_of((source % count) * 128, 128)
            target = slice(block * 128, block * 128 + 128)

            @pl.when(source < count)
            def _():
                out_ref[:, target] = own_ref[:, pl.ds(offset, 128)]

            @pl.when(source >= count)
            def _():
                out_ref[:, target] = other_ref[:, pl.ds(offset, 128)]


def permute_channels(order, own, other):
    shape = jax.ShapeDtypeStruct((own.shape[0], 2 * own.shape[1]), own.dtype)
    vmem = pl.BlockSpec(memory_space=pltpu.VMEM)
    return pl.pallas_call(
        permute_kernel,
        out_shape=[shape] * order.shape[0],
        in_specs=[pl.BlockSpec(memory_space=pltpu.SMEM), vmem, vmem],
        out_specs=[vmem] * order.shape[0],
    )(order, own, other)


def take_kernel(order_ref, rows_ref, out_ref):
    for block in range(out_ref.shape[0]):
        out_ref[block] = rows_ref[order_ref[block]]


def take_blocks(order, rows):
    blocks = rows.reshape(CHIPS, -1, rows.shape[1])
    vmem = pl.BlockSpec(memory_space=pltpu.VMEM)
    return pl.pallas_call(
        take_kernel,
        out_shape=jax.ShapeDtypeStruct(blocks.shape, blocks.dtype),
        in_specs=[pl.BlockSpec(memory_space=pltpu.SMEM), vmem],
        out_specs=vmem,
    )(order, blocks).reshape(rows.shape)


def unpermute_kernel(order_ref, first_ref, second_ref, own_ref, other_ref, total_ref):
    count = own_ref.shape[1] // 128
    for block in range(2 * count):
        offset = pl.multiple_of(order_ref[0, block] * 128, 128)
        total_ref[:, pl.ds(offset, 128)] = first_ref[:, block * 128 : block * 128 + 128]
    for block in range(2 * count):
        offset = pl.multiple_of(order_ref[1, block] * 128, 128)
        total_ref[:, pl.ds(offset, 128)] += second_ref[:, block * 128 : block * 128 + 128]
    own_ref[...] = total_ref[:, : count * 128]
    other_ref[...] = total_ref[:, count * 128 :].astype(other_ref.dtype)


def unpermute_sum(order, first, second):
    words, channels = first.shape
    vmem = pl.BlockSpec(memory_space=pltpu.VMEM)
    return pl.pallas_call(
        unpermute_kernel,
        out_shape=[
            jax.ShapeDtypeStruct((words, channels // 2), jnp.float32),
            jax.ShapeDtypeStruct((words, channels // 2), jnp.bfloat16),
        ],
        in_specs=[pl.BlockSpec(memory_space=pltpu.SMEM), vmem, vmem],
        out_specs=[vmem] * 2,
        scratch_shapes=[pltpu.VMEM((words, channels), jnp.float32)],
        compiler_params=pltpu.CompilerParams(vmem_limit_bytes=32 * 1024 * 1024),
    )(order, first, second)


FIRST_AXES = "xzy"
SECOND_AXES = "yzx"
HIGHWAY_AXES = (("xzy", "yzx"), ("zxy", "zyx"))
SMALL_AXES = "zxy"


def times_pieces(values, pieces):
    columns = jnp.split(values, len(pieces), axis=1)
    return reduce(
        jnp.add,
        [
            jnp.dot(column, piece, preferred_element_type=jnp.float32)
            for column, piece in zip(columns, pieces)
        ],
    )


def sum_over_wide(values, routed):
    if not routed:
        return lax.psum(values, "wide")
    flat = [value.reshape(-1) for value in values]
    flat = [jnp.pad(value, (0, -value.shape[0] % 128)).reshape(-1, 128) for value in flat]
    rows = jnp.concatenate(flat, axis=0)
    used = rows.shape[0]
    rows = jnp.pad(rows, ((0, -used % (8 * CHIPS)), (0, 0)))
    order = owners(SMALL_AXES, lax.axis_index("wide"))
    spots = jnp.arange(CHIPS, dtype=jnp.int32)
    places = jnp.sum(jnp.where(order[None, :] == spots[:, None], spots[None, :], 0), axis=1)
    rows = take_blocks(order, rows)
    own = scatter_blocks(jnp.split(rows, 2, axis=0), SMALL_AXES, jnp.float32)
    rows = take_blocks(places, joined(gather_blocks(own, SMALL_AXES)))
    totals = []
    first = 0
    for value, piece in zip(values, flat):
        totals.append(rows[first : first + piece.shape[0]].reshape(-1)[: value.size].reshape(value.shape))
        first += piece.shape[0]
    return totals


def per_device(
    char_ids,
    char_mask,
    word_lengths,
    char_table,
    conv_weight,
    conv_bias,
    highway_weight,
    highway_bias,
    proj_weight,
    qkv_weight,
    qv_bias,
    out_weight,
    up_weight,
    up_bias,
    down_weight,
    vector_biases,
    norm_gains,
    cotangent,
):
    f32 = jnp.float32
    bf16 = jnp.bfloat16
    own_filters = conv_weight.shape[1]
    widths = channel_widths(lax.axis_index("narrow") * own_filters, own_filters)
    tap_rows = jnp.arange(TAPS * CHAR_DIM, dtype=jnp.int32) // CHAR_DIM
    tap_mask = (tap_rows[:, None] < widths[None, :]).astype(bf16)
    tap_pad = ((0, LANES - TAPS * CHAR_DIM), (0, 0))
    masked_filters = jnp.pad(conv_weight * tap_mask, tap_pad)
    chan_scale = jnp.sqrt(TAPS / widths.astype(f32))
    word_count = char_ids.shape[0]
    seq_count = word_count // LENGTH
    places = jnp.arange(CHARS_MAX, dtype=jnp.int32)
    alive = (char_mask > 0) & (places[None, :] < word_lengths[:, None])
    picks = word_order(word_lengths)
    picks_low = picks.astype(bf16)
    told = jnp.concatenate(
        [jnp.where(alive, char_ids, -1), word_lengths[:, None]], axis=1
    ).astype(f32)
    told = jnp.dot(picks, told, precision=lax.Precision.HIGHEST)
    lens = told[:, CHARS_MAX:]
    tile_count = word_count // TILE
    longest = jnp.max(lens.astype(jnp.int32).reshape(tile_count, TILE), axis=1)
    tile_chunks = (longest + CHUNK - 1) // CHUNK
    spread_ids = jnp.pad(
        told[:, :CHARS_MAX].astype(jnp.int32),
        ((0, 0), (0, SLOTS - CHARS_MAX)),
        constant_values=-1,
    )
    spread_ids = spread_ids.reshape(tile_count, TILE, SLOTS // CHUNK, CHUNK)
    spread_ids = spread_ids.transpose(0, 2, 3, 1).reshape(-1, CHUNK * TILE)
    table_t = jnp.pad(
        jnp.tile(char_table.T, (TAPS, 1)), (tap_pad[0], (0, IDS - CHAR_VOCAB))
    )
    tap_lanes = (
        jnp.arange(LANES, dtype=jnp.int32)[None, :] // CHAR_DIM
        == jnp.arange(8, dtype=jnp.int32)[:, None]
    ).astype(f32)
    scale_row, bias_row = chan_scale[None, :], conv_bias[None, :]
    width_row = widths.astype(f32)[None, :]
    pool, pool_back = conv_calls(word_count, own_filters)
    embedded, pooled, pool_shift = pool(
        tile_chunks, spread_ids, table_t, tap_lanes, masked_filters, scale_row, bias_row, lens,
        width_row,
    )
    current = gelu_exact(pooled).astype(bf16)
    here = lax.axis_index("wide")
    core = lax.axis_index("narrow")
    routed = lax.axis_size("wide") == CHIPS
    width_proj, width_qkv, width_out = own_filters, 3 * qkv_weight.shape[2], out_weight.shape[0]
    width_up, width_down = up_weight.shape[1], down_weight.shape[0]
    feature_rows = qkv_weight.shape[0]
    first_rows = jnp.concatenate(
        [proj_weight.T, qkv_weight.reshape(feature_rows, width_qkv), out_weight.T], axis=1
    )
    second_rows = jnp.concatenate([up_weight, down_weight.T], axis=1)

    def whole_rows(shard, axes):
        if routed:
            return gather_blocks(shard, axes)
        return [lax.all_gather(shard, "wide", axis=0, tiled=True)]

    def own_rows(pieces, axes):
        if routed:
            return scatter_blocks(pieces, axes)
        return lax.psum_scatter(
            joined(pieces).astype(f32), "wide", scatter_dimension=0, tiled=True
        )

    def halves(rows):
        return jnp.split(rows, 2, axis=0) if routed else [rows]

    highway_full = [
        [whole_rows(highway_weight[layer, :, part], HIGHWAY_AXES[layer][part]) for part in range(2)]
        for layer in range(HW_LAYERS)
    ]
    first_full = joined(whole_rows(first_rows, FIRST_AXES))
    second_full = joined(whole_rows(second_rows, SECOND_AXES))
    if routed:
        second_full = reorder(second_full, blocks_after(SECOND_AXES), blocks_after(FIRST_AXES))
        feature_order = owners(FIRST_AXES, here)
    else:
        feature_order = jnp.arange(lax.axis_size("wide"), dtype=jnp.int32)
    proj_t, qkv_full, out_t = jnp.split(
        first_full, [width_proj, width_proj + width_qkv], axis=1
    )
    qkv_full = qkv_full.reshape(-1, 3, qkv_weight.shape[2])
    up_full, down_t = jnp.split(second_full, [width_up], axis=1)
    feature_count = proj_t.shape[0]
    feature_picks = (
        feature_order[:, None] == jnp.arange(feature_order.shape[0], dtype=jnp.int32)[None, :]
    ).astype(f32)
    feature_places = (
        feature_order[:, None] * feature_rows + jnp.arange(feature_rows, dtype=jnp.int32)[None, :]
    ).reshape(-1)
    feature_moves = (
        feature_places[:, None] == jnp.arange(feature_count, dtype=jnp.int32)[None, :]
    ).astype(bf16)

    def pick_features(rows, picks):
        blocked = rows.reshape(rows.shape[0], -1, feature_rows)
        return jnp.einsum(
            "kwr,bw->kbr", blocked, picks, precision=lax.Precision.HIGHEST
        ).reshape(rows.shape)

    vector_biases = pick_features(vector_biases, feature_picks)
    norm_gains = pick_features(norm_gains, feature_picks)
    grad_output = jnp.dot(cotangent, feature_moves.T, preferred_element_type=f32).astype(bf16)
    grad_output = jnp.dot(picks_low, grad_output, preferred_element_type=f32)
    kept_layers = []
    for layer_index in range(HW_LAYERS):
        if routed:
            order = jnp.stack([owners(axes, here) for axes in HIGHWAY_AXES[layer_index]])
            order = (order - core * (CHIPS // 2)) % CHIPS
            whole_input = permute_channels(order, current, swap(current))
        else:
            order = None
            whole_input = [lax.all_gather(current, "narrow", axis=1, tiled=True)] * 2
        mixed_pre = (
            jnp.stack(
                [
                    times_pieces(whole_input[part], highway_full[layer_index][part])
                    for part in range(2)
                ],
                axis=1,
            )
            + highway_bias[layer_index]
        )
        carried = current.astype(f32)
        kept_layers.append((whole_input, mixed_pre, carried, order))
        current = highway_mix(mixed_pre, carried).astype(bf16)
    start_rows = (
        pair_sum(jnp.dot(current, proj_t.T, preferred_element_type=f32)) + vector_biases[0]
    )
    start_low = start_rows.astype(bf16)
    qkv_bias = jnp.stack([qv_bias[0], jnp.zeros_like(qv_bias[0]), qv_bias[1]])
    projected = (
        jnp.einsum("wd,dgc->wgc", start_low, qkv_full, preferred_element_type=f32) + qkv_bias
    ).astype(bf16)
    heads_here = qkv_full.shape[2] // HEAD_DIM
    head_shape = (word_count, heads_here, HEAD_DIM)
    query = projected[:, 0].reshape(head_shape)
    keys_here = projected[:, 1].reshape(head_shape)
    values_here = projected[:, 2].reshape(head_shape)
    attn_scale = HEAD_DIM ** (-0.5)
    sequence = jnp.arange(word_count, dtype=jnp.int32) // 8 % seq_count
    together = (sequence[:, None] == sequence[None, :])[None]
    scores = jnp.einsum("qhe,khe->hqk", query, keys_here, preferred_element_type=f32) * attn_scale
    scores = jnp.where(together, scores, -1e30)
    weights = jnp.exp(scores - jnp.max(scores, axis=-1, keepdims=True))
    probs = weights / jnp.sum(weights, axis=-1, keepdims=True)
    probs_low = probs.astype(bf16)
    context = (
        jnp.einsum("hqk,khe->qhe", probs_low, values_here, preferred_element_type=f32)
        .reshape(word_count, -1)
        .astype(bf16)
    )
    attended = pair_sum(jnp.dot(context, out_t.T, preferred_element_type=f32)) + vector_biases[1]
    before_one = start_rows + attended
    normed_one = layer_norm(before_one, norm_gains[0], vector_biases[3])
    normed_low = normed_one.astype(bf16)
    hidden_pre = jnp.dot(normed_low, up_full, preferred_element_type=f32) + up_bias
    hidden_low = gelu_exact(hidden_pre).astype(bf16)
    lowered = (
        pair_sum(jnp.dot(hidden_low, down_t.T, preferred_element_type=f32)) + vector_biases[2]
    )
    before_two = normed_one + lowered
    encoded = layer_norm(before_two, norm_gains[1], vector_biases[4]).astype(bf16)
    encoded = jnp.dot(encoded, feature_moves, preferred_element_type=f32).astype(bf16)
    encoded = jnp.dot(picks_low.T, encoded, preferred_element_type=f32).astype(bf16)
    ln_two_back = jax.vjp(layer_norm, before_two, norm_gains[1], vector_biases[4])[1]
    grad_before_two, gain_two, bias_two = ln_two_back(grad_output)
    grad_lowered = grad_before_two.astype(bf16)
    down_grad_local = jnp.dot(grad_lowered.T, hidden_low, preferred_element_type=f32)
    bias_down = jnp.sum(grad_lowered.astype(f32), axis=0)
    grad_hidden = jnp.dot(grad_lowered, down_t, preferred_element_type=f32)
    grad_hidden_pre = jax.vjp(gelu_exact, hidden_pre)[1](grad_hidden)[0].astype(bf16)
    up_grad_local = jnp.dot(normed_low.T, grad_hidden_pre, preferred_element_type=f32)
    bias_up = jnp.sum(grad_hidden_pre.astype(f32), axis=0)
    grad_normed_one = grad_before_two + pair_grad_sum(
        jnp.dot(grad_hidden_pre, up_full.T, preferred_element_type=f32)
    )
    ln_one_back = jax.vjp(layer_norm, before_one, norm_gains[0], vector_biases[3])[1]
    grad_before_one, gain_one, bias_one = ln_one_back(grad_normed_one)
    grad_attended = grad_before_one.astype(bf16)
    out_grad_local = jnp.dot(grad_attended.T, context, preferred_element_type=f32)
    bias_attended = jnp.sum(grad_attended.astype(f32), axis=0)
    grad_context = (
        jnp.dot(grad_attended, out_t, preferred_element_type=f32)
        .astype(bf16)
        .reshape(head_shape)
    )
    grad_probs = jnp.einsum(
        "qhe,khe->hqk", grad_context, values_here, preferred_element_type=f32
    )
    grad_value = jnp.einsum("hqk,qhe->khe", probs_low, grad_context, preferred_element_type=f32)
    grad_scores = (
        probs * (grad_probs - jnp.sum(probs * grad_probs, axis=-1, keepdims=True))
    ).astype(bf16)
    grad_query = (
        jnp.einsum("hqk,khe->qhe", grad_scores, keys_here, preferred_element_type=f32) * attn_scale
    )
    grad_key = (
        jnp.einsum("hqk,qhe->khe", grad_scores, query, preferred_element_type=f32) * attn_scale
    )
    grad_projected = jnp.stack(
        [
            grad_query.reshape(word_count, -1),
            grad_key.reshape(word_count, -1),
            grad_value.reshape(word_count, -1),
        ],
        axis=1,
    ).astype(bf16)
    qkv_grad_local = jnp.einsum(
        "wd,wgc->dgc", start_low, grad_projected, preferred_element_type=f32
    )
    bias_qv = jnp.sum(grad_projected[:, 0::2].astype(f32), axis=0)
    grad_start = grad_before_one + pair_grad_sum(
        jnp.einsum("wgc,dgc->wd", grad_projected, qkv_full, preferred_element_type=f32)
    )
    grad_start_low = grad_start.astype(bf16)
    proj_grad_local = jnp.dot(grad_start_low.T, current, preferred_element_type=f32)
    bias_start = jnp.sum(grad_start_low.astype(f32), axis=0)
    grad_current = jnp.dot(grad_start_low, proj_t, preferred_element_type=f32)
    first_grad_local = jnp.concatenate(
        [proj_grad_local, qkv_grad_local.reshape(feature_count, width_qkv), out_grad_local], axis=1
    ).astype(bf16)
    second_grad_local = jnp.concatenate([up_grad_local, down_grad_local], axis=1).astype(bf16)
    if routed:
        second_grad_local = reorder(
            second_grad_local, blocks_after(FIRST_AXES), blocks_after(SECOND_AXES)
        )
    second_grad = own_rows(halves(second_grad_local), SECOND_AXES)
    first_grad = own_rows(halves(first_grad_local), FIRST_AXES)
    highway_grads = []
    highway_bias_grads = []
    for layer_index in reversed(range(HW_LAYERS)):
        whole_input, mixed_pre, carried, order = kept_layers[layer_index]
        mix_back = jax.vjp(highway_mix, mixed_pre, carried)[1]
        grad_mixed, grad_carried = mix_back(grad_current)
        grad_mixed_low = grad_mixed.astype(bf16)
        part_grads = []
        grad_whole = []
        for part in range(2):
            part_mixed = grad_mixed_low[:, part]
            pieces = highway_full[layer_index][part]
            part_grads.append(
                own_rows(
                    [
                        jnp.dot(columns.T, part_mixed, preferred_element_type=f32).astype(bf16)
                        for columns in jnp.split(whole_input[part], len(pieces), axis=1)
                    ],
                    HIGHWAY_AXES[layer_index][part],
                )
            )
            grad_whole.append(
                jnp.concatenate(
                    [
                        jnp.dot(part_mixed, piece.T, preferred_element_type=f32)
                        for piece in pieces
                    ],
                    axis=1,
                )
            )
        highway_grads.insert(0, jnp.stack(part_grads, axis=1))
        highway_bias_grads.insert(0, jnp.sum(grad_mixed_low.astype(f32), axis=0))
        if routed:
            grad_own, grad_other = unpermute_sum(order, *grad_whole)
            grad_current = grad_carried + add(grad_own, swap(grad_other))
        else:
            grad_current = grad_carried + lax.psum_scatter(
                add(*grad_whole).astype(bf16), "narrow", scatter_dimension=1, tiled=True
            ).astype(f32)
    highway_grad = jnp.stack(highway_grads)
    highway_bias_local = jnp.stack(highway_bias_grads)
    grad_pooled = jax.vjp(gelu_exact, pooled)[1](grad_current)[0]
    grad_filter, grad_marks = pool_back(
        tile_chunks, spread_ids, tap_lanes, masked_filters, scale_row, lens, width_row, embedded,
        pool_shift, grad_pooled,
    )
    grad_filter = grad_filter[: TAPS * CHAR_DIM]
    grad_conv_bias = jnp.sum(grad_pooled, axis=0)
    grad_marks = grad_marks[:CHAR_VOCAB, :LANES] + grad_marks[:CHAR_VOCAB, LANES:]
    grad_chars = jnp.sum(
        grad_marks[:, : TAPS * CHAR_DIM].reshape(CHAR_VOCAB, TAPS, CHAR_DIM), axis=1
    )
    grad_filter = grad_filter * tap_mask.astype(f32)
    proj_grad, qkv_grad, out_grad = jnp.split(
        first_grad, [width_proj, width_proj + width_qkv], axis=1
    )
    up_grad, down_grad = jnp.split(second_grad, [width_up], axis=1)
    proj_grad, out_grad, down_grad = proj_grad.T, out_grad.T, down_grad.T
    qkv_grad = qkv_grad.reshape(qkv_weight.shape)
    bias_local = pick_features(
        jnp.stack([bias_start, bias_attended, bias_down, bias_one, bias_two]), feature_picks.T
    )
    gain_local = pick_features(jnp.stack([gain_one, gain_two]), feature_picks.T)
    (
        conv_grad,
        conv_bias_grad,
        highway_bias_grad,
        qv_bias_grad,
        up_bias_grad,
        bias_grads,
        gain_grads,
        char_grad,
    ) = sum_over_wide(
        (
            grad_filter,
            grad_conv_bias,
            highway_bias_local,
            bias_qv,
            bias_up,
            bias_local,
            gain_local,
            pair_sum(grad_chars),
        ),
        routed,
    )
    return (
        encoded,
        char_grad,
        conv_grad,
        conv_bias_grad,
        highway_grad,
        highway_bias_grad,
        proj_grad,
        qkv_grad,
        qv_bias_grad,
        out_grad,
        up_grad,
        up_bias_grad,
        down_grad,
        bias_grads,
        gain_grads,
    )


def solution(mesh):
    placed = (
        P("wide", None),
        P("wide", None),
        P("wide"),
        P(),
        P(None, "narrow"),
        P("narrow"),
        P(None, "wide", None, "narrow"),
        P(None, None, "narrow"),
        P("narrow", "wide"),
        P("wide", None, "narrow"),
        P(None, "narrow"),
        P("narrow", "wide"),
        P("wide", "narrow"),
        P("narrow"),
        P("narrow", "wide"),
        P(),
        P(),
        P("wide", None),
    )
    return jax.shard_map(
        per_device,
        mesh=mesh,
        in_specs=placed,
        out_specs=(
            P("wide", None),
            P(),
            P(None, "narrow"),
            P("narrow"),
            P(None, "wide", None, "narrow"),
            P(None, None, "narrow"),
            P("narrow", "wide"),
            P("wide", None, "narrow"),
            P(None, "narrow"),
            P("narrow", "wide"),
            P("wide", "narrow"),
            P("narrow"),
            P("narrow", "wide"),
            P(),
            P(),
        ),
        check_vma=False,
    )
```

```python
from functools import partial, reduce

import jax
import jax.numpy as jnp
from jax import lax
from jax.experimental import pallas as pl
from jax.experimental.pallas import tpu as pltpu
from jax.sharding import PartitionSpec as P

HEAD_DIM = 64
FILTERS = 2048
CHAR_DIM = 16
CHAR_VOCAB = 262
CHARS_MAX = 50
TAPS = 7
HW_LAYERS = 2
TILE = 16
CHUNK = 8
SLOTS = 64
IDS = 272
LANES = 128
BLOCK = 256
LOG2E = 1.4426950408889634
LENGTH = 128


BOUNDS = ((1, 2), (3, 4), (7, 8), (15, 16), (31, 32), (63, 64))
EPSILON = 1e-06


def channel_widths(first_channel, count):
    channels = first_channel + jnp.arange(count, dtype=jnp.int32)
    widths = jnp.full((count,), TAPS, jnp.int32)
    for numerator, denominator in BOUNDS:
        widths = widths - (channels >= FILTERS * numerator // denominator).astype(jnp.int32)
    return widths


def gelu_exact(values):
    return jax.nn.gelu(values, approximate=False)


def layer_norm(values, gain_row, bias_row):
    center = jnp.mean(values, axis=-1, keepdims=True)
    spread = jnp.mean(jnp.square(values - center), axis=-1, keepdims=True)
    return (values - center) * lax.rsqrt(spread + EPSILON) * gain_row + bias_row


def highway_mix(mixed_pre, carried):
    gate_value = jax.nn.sigmoid(mixed_pre[:, 1])
    return gate_value * carried + (1.0 - gate_value) * gelu_exact(mixed_pre[:, 0])


def word_order(lengths):
    words = lengths.shape[0]
    sequences = words // LENGTH
    spots = jnp.arange(words, dtype=jnp.int32)
    keys = lengths * LENGTH + (LENGTH - 1 - spots % LENGTH)
    same = spots[:, None] // LENGTH == spots[None, :] // LENGTH
    ranks = jnp.sum((same & (keys[None, :] > keys[:, None])).astype(jnp.int32), axis=1)
    places = ranks // 8 * (8 * sequences) + spots // LENGTH * 8 + ranks % 8
    return (places[None, :] == spots[:, None]).astype(jnp.float32)


def spot_chars(ids_row, table_t):
    ids = lax.broadcasted_iota(jnp.int32, (IDS, LANES), 0)
    marks = (ids == ids_row).astype(jnp.float32).astype(jnp.bfloat16)
    return jnp.dot(table_t, marks, preferred_element_type=jnp.float32).T.astype(jnp.bfloat16)


def tap_rows(table_ref, start, tile, tap_lanes):
    rows = pl.ds(pl.multiple_of(tile * TILE, TILE), TILE)
    taken = None
    for tap in range(TAPS):
        piece = table_ref[pl.ds(start + tap, CHUNK), rows, :] * tap_lanes[tap][None]
        taken = piece if taken is None else taken + piece
    return taken.reshape(CHUNK * TILE, LANES)


def window_counts(lens_ref, widths_ref, tile):
    rows = pl.ds(pl.multiple_of(tile * TILE, TILE), TILE)
    return jnp.maximum(lens_ref[rows, :1] - widths_ref[...] + 1.0, 1.0)


def pool_kernel(
    tile_ref, ids_ref, table_ref, lanes_ref, filters_ref, scale_ref, bias_ref, lens_ref, widths_ref,
    embed_ref, pooled_ref, shift_ref, conv_ref, count_ref, top_ref,
):
    channels = filters_ref.shape[1]
    chunks_all = SLOTS // CHUNK
    tap_lanes = [lanes_ref[tap : tap + 1, :].astype(jnp.bfloat16) for tap in range(TAPS)]
    blocks = [slice(first, first + BLOCK) for first in range(0, channels, BLOCK)]

    def one_tile(tile, _):
        rows = pl.ds(pl.multiple_of(tile * TILE, TILE), TILE)
        chunks = tile_ref[tile]

        def embed(chunk, _):
            found = spot_chars(ids_ref[pl.ds(tile * chunks_all + chunk, 1), :], table_ref[...])
            embed_ref[pl.ds(chunk * CHUNK, CHUNK), rows, :] = found.reshape(CHUNK, TILE, LANES)
            return 0

        lax.fori_loop(0, chunks, embed, 0)
        embed_ref[pl.ds(chunks * CHUNK, CHUNK), rows, :] = jnp.zeros(
            (CHUNK, TILE, LANES), jnp.bfloat16
        )
        count_ref[...] = window_counts(lens_ref, widths_ref, tile)
        top_ref[...] = jnp.full(top_ref.shape, -1e30, jnp.float32)

        def convolve(chunk, _):
            columns = tap_rows(embed_ref, chunk * CHUNK, tile, tap_lanes)
            first = (chunk * CHUNK).astype(jnp.float32)
            for block in blocks:
                convolved = jnp.dot(
                    columns, filters_ref[:, block], preferred_element_type=jnp.float32
                )
                conv_ref[chunk, :, block] = convolved
                counts = count_ref[:, block] - first
                top = top_ref[:, block]
                for place in range(CHUNK):
                    row = convolved[place * TILE : (place + 1) * TILE]
                    top = jnp.maximum(top, jnp.where(counts > float(place), row, -1e30))
                top_ref[:, block] = top
            return 0

        lax.fori_loop(0, chunks, convolve, 0)
        pooled_ref[rows, :] = jnp.zeros((TILE, channels), jnp.float32)

        def weigh(chunk, _):
            first = (chunk * CHUNK).astype(jnp.float32)
            for block in blocks:
                counts = count_ref[:, block] - first
                scale = scale_ref[:, block] * LOG2E
                offset = top_ref[:, block] * scale
                total = pooled_ref[rows, block]
                for place in range(CHUNK):
                    row = conv_ref[chunk, place * TILE : (place + 1) * TILE, block]
                    weight = jnp.exp2(row * scale - offset)
                    total = total + jnp.where(counts > float(place), weight, 0.0)
                pooled_ref[rows, block] = total
            return 0

        lax.fori_loop(0, chunks, weigh, 0)
        top = top_ref[...] * scale_ref[...]
        log_total = jnp.log(pooled_ref[rows, :])
        pooled_ref[rows, :] = top + bias_ref[...] + log_total - jnp.log(count_ref[...])
        shift_ref[rows, :] = (top + log_total) * -LOG2E
        return 0

    lax.fori_loop(0, tile_ref.shape[0], one_tile, 0)


def pool_back_kernel(
    tile_ref, ids_ref, lanes_ref, filters_ref, scale_ref, lens_ref, widths_ref, embed_ref, shift_ref,
    grad_ref, filter_grad_ref, char_grad_ref, conv_grad_ref, column_ref, count_ref,
):
    channels = filters_ref.shape[1]
    chunks_all = SLOTS // CHUNK
    tap_lanes = [lanes_ref[tap : tap + 1, :].astype(jnp.bfloat16) for tap in range(TAPS)]
    lane_taps = lax.broadcasted_iota(jnp.int32, (1, 1, LANES), 2) // CHAR_DIM
    blocks = [slice(first, first + BLOCK) for first in range(0, channels, BLOCK)]
    filter_grad_ref[...] = jnp.zeros(filter_grad_ref.shape, jnp.float32)
    char_grad_ref[...] = jnp.zeros(char_grad_ref.shape, jnp.float32)
    column_ref[:CHUNK] = jnp.zeros((CHUNK, TILE, LANES), jnp.float32)

    def one_tile(tile, _):
        rows = pl.ds(pl.multiple_of(tile * TILE, TILE), TILE)
        chunks = tile_ref[tile]
        count_ref[...] = window_counts(lens_ref, widths_ref, tile)

        def one_chunk(chunk, _):
            columns = tap_rows(embed_ref, chunk * CHUNK, tile, tap_lanes)
            columns_t = columns.astype(jnp.float32).T.astype(jnp.bfloat16)
            first = (chunk * CHUNK).astype(jnp.float32)
            grad_columns = None
            for block in blocks:
                filters = filters_ref[:, block]
                convolved = jnp.dot(columns, filters, preferred_element_type=jnp.float32)
                counts = count_ref[:, block] - first
                scale = scale_ref[:, block]
                scale2 = scale * LOG2E
                shift = shift_ref[rows, block]
                grad = grad_ref[rows, block] * scale
                for place in range(CHUNK):
                    row = convolved[place * TILE : (place + 1) * TILE]
                    share = jnp.exp2(row * scale2 + shift)
                    conv_grad_ref[place * TILE : (place + 1) * TILE, block] = jnp.where(
                        counts > float(place), share * grad, 0.0
                    ).astype(jnp.bfloat16)
                conv_grad = conv_grad_ref[:, block]
                filter_grad_ref[:, block] += jnp.dot(
                    columns_t, conv_grad, preferred_element_type=jnp.float32
                )
                piece = lax.dot_general(
                    conv_grad, filters, (((1,), (1,)), ((), ())), preferred_element_type=jnp.float32
                )
                grad_columns = piece if grad_columns is None else grad_columns + piece
            column_ref[pl.ds(chunk * CHUNK + CHUNK, CHUNK)] = grad_columns.reshape(
                CHUNK, TILE, LANES
            )
            return 0

        lax.fori_loop(0, chunks, one_chunk, 0)

        def fold(chunk, _):
            moved = None
            for tap in range(TAPS):
                piece = column_ref[pl.ds(chunk * CHUNK + CHUNK - tap, CHUNK)]
                moved = piece if moved is None else jnp.where(lane_taps == tap, piece, moved)
            moved = moved.reshape(CHUNK * TILE, LANES)
            high = moved.astype(jnp.bfloat16)
            low = (moved - high.astype(jnp.float32)).astype(jnp.bfloat16)
            ids = lax.broadcasted_iota(jnp.int32, (IDS, LANES), 0)
            ids_row = ids_ref[pl.ds(tile * chunks_all + chunk, 1), :]
            marks = (ids == ids_row).astype(jnp.float32).astype(jnp.bfloat16)
            char_grad_ref[...] += jnp.dot(
                marks, jnp.concatenate([high, low], axis=1), preferred_element_type=jnp.float32
            )
            return 0

        lax.fori_loop(0, chunks, fold, 0)
        return 0

    lax.fori_loop(0, tile_ref.shape[0], one_tile, 0)


def conv_calls(words, channels):
    vmem = pl.BlockSpec(memory_space=pltpu.VMEM)
    smem = pl.BlockSpec(memory_space=pltpu.SMEM)
    shape = partial(jax.ShapeDtypeStruct, dtype=jnp.float32)
    params = pltpu.CompilerParams(vmem_limit_bytes=40 * 1024 * 1024)
    pool = pl.pallas_call(
        pool_kernel,
        out_shape=[
            jax.ShapeDtypeStruct((SLOTS, words, LANES), jnp.bfloat16),
            shape((words, channels)),
            shape((words, channels)),
        ],
        in_specs=[smem] + [vmem] * 8,
        out_specs=[vmem] * 3,
        scratch_shapes=[
            pltpu.VMEM((SLOTS // CHUNK, CHUNK * TILE, channels), jnp.float32),
            pltpu.VMEM((TILE, channels), jnp.float32),
            pltpu.VMEM((TILE, channels), jnp.float32),
        ],
        compiler_params=params,
        cost_estimate=pl.CostEstimate(
            flops=5_000_000_000, bytes_accessed=8_000_000, transcendentals=5_000_000
        ),
    )
    back = pl.pallas_call(
        pool_back_kernel,
        out_shape=[shape((LANES, channels)), shape((IDS, 2 * LANES))],
        in_specs=[smem] + [vmem] * 9,
        out_specs=[vmem] * 2,
        scratch_shapes=[
            pltpu.VMEM((CHUNK * TILE, channels), jnp.bfloat16),
            pltpu.VMEM((SLOTS + CHUNK, TILE, LANES), jnp.float32),
            pltpu.VMEM((TILE, channels), jnp.float32),
        ],
        compiler_params=params,
        cost_estimate=pl.CostEstimate(
            flops=10_000_000_000, bytes_accessed=10_000_000, transcendentals=5_000_000
        ),
    )
    return pool, back


STEPS = {
    "x": [(i, i ^ 1) for i in range(16)],
    "y": [(i, i ^ 2) for i in range(16)],
    "z": [(i, (i + 4) % 16) for i in range(16)],
    "near": [(i, i ^ 4) for i in range(16)],
    "far": [(i, i ^ 8) for i in range(16)],
}
CHIPS = 16
SWAP = [(0, 1), (1, 0)]


def step(value, axis):
    return lax.ppermute(value, "wide", STEPS[axis])


def swap(value):
    return lax.ppermute(value, "narrow", SWAP)


def joined(pieces):
    return pieces[0] if len(pieces) == 1 else jnp.concatenate(pieces, axis=0)


def add(one, other):
    return one.astype(jnp.float32) + other.astype(jnp.float32)


FIRST = {"a": "x", "b": "y"}
LAST = {"a": "y", "b": "x"}


def moves_of(kind):
    moves = {}
    if kind == "Q":
        for turn in (1, 2, 3):
            moves["z", turn] = ("z", 2, [("z", turn - 1)] if turn > 1 else [])
    for part in "ab":
        if kind == "P":
            moves[part, "first"] = (FIRST[part], 1, [])
            for turn in (1, 2, 3):
                before = (part, "z", turn - 1) if turn > 1 else (part, "first")
                moves[part, "z", turn] = ("z", 2, [before])
            for half in (0, 1):
                moves[part, "last", half] = (LAST[part], 4, [(part, "z", 1 + 2 * half)])
        else:
            for half in (0, 1):
                moves[part, "first", half] = (FIRST[part], 2, [("z", 1 + 2 * half)])
                moves[part, "last", half] = (LAST[part], 4, [(part, "first", half)])
    return moves


def back_moves_of(kind):
    moves = {}
    for part in "ab":
        for half in (0, 1):
            moves[part, "last", half] = (LAST[part], 4, [])
        if kind == "P":
            moves[part, "z", 1] = ("z", 2, [(part, "last", 0)])
            moves[part, "z", 2] = ("z", 2, [(part, "z", 1), (part, "last", 1)])
            moves[part, "z", 3] = ("z", 2, [(part, "z", 2)])
            moves[part, "first"] = (FIRST[part], 1, [(part, "z", 3)])
        else:
            for half in (0, 1):
                moves[part, "first", half] = (FIRST[part], 2, [(part, "last", half)])
    if kind == "Q":
        moves["z", 1] = ("z", 2, [("a", "first", 0), ("b", "first", 0)])
        moves["z", 2] = ("z", 2, [("z", 1), ("a", "first", 1), ("b", "first", 1)])
        moves["z", 3] = ("z", 2, [("z", 2)])
    return moves


def ordered_moves(moves, ready, lag=0.5):
    ended, free, order = {}, {"x": 0.0, "y": 0.0, "z": 0.0}, []
    ranks = {name: rank for rank, name in enumerate(moves)}
    waiting = dict(moves)
    while waiting:
        best = None
        for name, (axis, size, needs) in waiting.items():
            if all(need in ended for need in needs):
                start = max([ready.get(name[0], 0.0), free[axis]] + [ended[need] + lag for need in needs])
                if best is None or (start, ranks[name]) < best[:2]:
                    best = (start, ranks[name], name)
        start, _, name = best
        axis, size, _ = waiting.pop(name)
        ended[name] = free[axis] = start + size
        order.append(name)
    return order


class Links:
    def __init__(self):
        self.sent = {"x": [], "y": [], "z": []}

    def send(self, value, axis, way=None):
        sent = self.sent[axis]
        if len(sent) > 1:
            value, _ = lax.optimization_barrier((value, sent[-2]))
        sent.append(step(value, way or axis))
        return sent[-1]


def blocks_of(kind, part):
    blocks = []
    for last in (0, 1):
        for half in (0, 1):
            turns = (2 * half, 2 * half + 1)
            if kind == "P":
                pairs = [(turn, first) for turn in turns for first in (0, 1)]
            else:
                pairs = [(turn, first) for first in (0, 1) for turn in turns]
            for turn, first in pairs:
                blocks.append((turn, first, last) if part == "b" else (turn, last, first))
    return blocks


def owners(blocks, here):
    z, y, x = here // 4, (here // 2) % 2, here % 2
    return jnp.stack(
        [((z - dz) % 4) * 4 + (y + dy) % 2 * 2 + (x + dx) % 2 for dz, dy, dx in blocks]
    ).astype(jnp.int32)


def gather_matrices(shards, kinds):
    moves = {}
    for name, kind in kinds.items():
        for move, (axis, size, needs) in moves_of(kind).items():
            moves[(name,) + move] = (axis, size, [(name,) + need for need in needs])
    links, got, sent = Links(), {}, {}
    for move in ordered_moves(moves, {}):
        name, kind = move[0], kinds[move[0]]
        parts = dict(zip("ab", shards[name]))
        if kind == "P":
            part, stage = move[1:3]
            if stage == "first":
                value = parts[part]
            elif stage == "z":
                if move[3] == 1:
                    sent[name, part, "pair"] = joined([parts[part], got[name, part, "first"]])
                    value = sent[name, part, "pair"]
                else:
                    value = got[name, part, "z", move[3] - 1]
            else:
                pairs = [sent[name, part, "pair"]] + [got[name, part, "z", turn] for turn in (1, 2, 3) if turn <= 1 + 2 * move[3]]
                value = joined(pairs[2 * move[3] :])
        elif move[1] == "z":
            value = joined_lanes(shards[name]) if move[2] == 1 else got[name, "z", move[2] - 1]
        else:
            part, stage, half = move[1:]
            if stage == "first":
                width = parts["a"].shape[1]
                lanes = slice(0, width) if part == "a" else slice(width, None)
                rows = [
                    got[name, "z", turn][:, lanes] if turn else parts[part]
                    for turn in (2 * half, 2 * half + 1)
                ]
                value = joined(rows)
            else:
                value = joined([sent[name, part, "first", half], got[name, part, "first", half]])
        sent[move] = value
        got[move] = links.send(value, moves[move][0])
    full = {
        (name, part): [held[name, part, "last", half] for held in (sent, got) for half in (0, 1)]
        for name in kinds
        for part in "ab"
    }
    return full, got


def joined_lanes(pieces):
    return jnp.concatenate(pieces, axis=1)


SMALL_MOVES = {
    ("small", "x"): ("x", 1, []),
    ("small", "y"): ("y", 1, [("small", "x")]),
    ("small", "near"): ("z", 1, [("small", "y")]),
    ("small", "far"): ("z", 2, [("small", "near")]),
}


def scatter_matrices(grads, kinds, small, ready):
    low = jnp.bfloat16
    moves = {}
    for name, kind in kinds.items():
        for move, (axis, size, needs) in back_moves_of(kind).items():
            moves[(name,) + move] = (axis, size, [(name,) + need for need in needs])
    moves = {**SMALL_MOVES, **moves}
    links, got, held = Links(), {}, {}

    def kept(name, part, half):
        key = (name, part, half)
        if key not in held:
            held[key] = add(grads[name, part][half], got[name, part, "last", half]).astype(low)
        return held[key]

    def pair(name, part, turn):
        rows = kept(name, part, turn // 2)
        height = rows.shape[0] // 2
        return rows[(turn % 2) * height :][:height]

    def both(name, turn):
        rows = []
        for part in "ab":
            half = turn // 2
            key = (name, part, "both", half)
            if key not in held:
                own = kept(name, part, half)
                held[key] = add(own[: own.shape[0] // 2], got[name, part, "first", half])
            height = held[key].shape[0] // 2
            rows.append(held[key][(turn % 2) * height :][:height])
        return joined_lanes(rows)

    for move in ordered_moves(moves, ready):
        if move in SMALL_MOVES:
            small = small.astype(low)
            small = add(small, links.send(small, moves[move][0], move[1]))
            continue
        name, kind = move[0], kinds[move[0]]
        if "last" in move:
            value = grads[name, move[1]][2 + move[3]]
        elif kind == "P" and move[2] == "z":
            part, turn = move[1], move[3]
            value = pair(name, part, turn)
            if turn > 1:
                value = add(value, got[name, part, "z", turn - 1]).astype(low)
        elif kind == "P":
            part = move[1]
            total = add(pair(name, part, 0), got[name, part, "z", 3])
            held[name, part, "own"] = total[: total.shape[0] // 2]
            value = total[total.shape[0] // 2 :].astype(low)
        elif move[1] == "z":
            turn = move[2]
            value = both(name, turn)
            if turn > 1:
                value = add(value, got[name, "z", turn - 1])
            value = value.astype(low)
        else:
            part, half = move[1], move[3]
            own = kept(name, part, half)
            value = own[own.shape[0] // 2 :]
        got[move] = links.send(value, moves[move][0])
    sums = {}
    for name, kind in kinds.items():
        if kind == "P":
            sums[name] = joined_lanes(
                [add(held[name, part, "own"], got[name, part, "first"]) for part in "ab"]
            )
        else:
            sums[name] = add(both(name, 0), got[name, "z", 3])
    return sums, small


def moved_blocks(buffers, old, new, count):
    rows, width = buffers[0].shape
    height = rows * len(buffers) // len(old)
    per_source, per_target = len(old) // len(buffers), len(new) // count

    def kernel(*refs):
        sources, targets = refs[: len(buffers)], refs[len(buffers) :]
        for spot, block in enumerate(new):
            place = old.index(block)
            source, target = sources[place // per_source], targets[spot // per_target]
            first, place = spot % per_target * height, place % per_source * height
            target[first : first + height] = source[place : place + height]

    vmem = pl.BlockSpec(memory_space=pltpu.VMEM)
    return pl.pallas_call(
        kernel,
        out_shape=[jax.ShapeDtypeStruct((height * per_target, width), buffers[0].dtype)] * count,
        in_specs=[vmem] * len(buffers),
        out_specs=[vmem] * count,
        compiler_params=pltpu.CompilerParams(vmem_limit_bytes=24 * 1024 * 1024),
    )(*buffers)


def pair_sum(partial_value):
    return partial_value + swap(partial_value)


def pair_grad_sum(partial_value):
    low = partial_value.astype(jnp.bfloat16)
    return add(low, swap(low))


def permute_kernel(order_ref, own_ref, other_ref, *out_refs):
    count = own_ref.shape[1] // 128
    for part, out_ref in enumerate(out_refs):
        for block in range(2 * count):
            source = order_ref[part, block]
            offset = pl.multiple_of((source % count) * 128, 128)
            target = slice(block * 128, block * 128 + 128)

            @pl.when(source < count)
            def _():
                out_ref[:, target] = own_ref[:, pl.ds(offset, 128)]

            @pl.when(source >= count)
            def _():
                out_ref[:, target] = other_ref[:, pl.ds(offset, 128)]


def permute_channels(order, own, other):
    shape = jax.ShapeDtypeStruct((own.shape[0], 2 * own.shape[1]), own.dtype)
    vmem = pl.BlockSpec(memory_space=pltpu.VMEM)
    return pl.pallas_call(
        permute_kernel,
        out_shape=[shape] * order.shape[0],
        in_specs=[pl.BlockSpec(memory_space=pltpu.SMEM), vmem, vmem],
        out_specs=[vmem] * order.shape[0],
    )(order, own, other)


def unpermute_kernel(order_ref, first_ref, second_ref, own_ref, other_ref, total_ref):
    count = own_ref.shape[1] // 128
    for block in range(2 * count):
        offset = pl.multiple_of(order_ref[0, block] * 128, 128)
        total_ref[:, pl.ds(offset, 128)] = first_ref[:, block * 128 : block * 128 + 128]
    for block in range(2 * count):
        offset = pl.multiple_of(order_ref[1, block] * 128, 128)
        total_ref[:, pl.ds(offset, 128)] += second_ref[:, block * 128 : block * 128 + 128]
    own_ref[...] = total_ref[:, : count * 128]
    other_ref[...] = total_ref[:, count * 128 :].astype(other_ref.dtype)


def unpermute_sum(order, first, second):
    words, channels = first.shape
    vmem = pl.BlockSpec(memory_space=pltpu.VMEM)
    return pl.pallas_call(
        unpermute_kernel,
        out_shape=[
            jax.ShapeDtypeStruct((words, channels // 2), jnp.float32),
            jax.ShapeDtypeStruct((words, channels // 2), jnp.bfloat16),
        ],
        in_specs=[pl.BlockSpec(memory_space=pltpu.SMEM), vmem, vmem],
        out_specs=[vmem] * 2,
        scratch_shapes=[pltpu.VMEM((words, channels), jnp.float32)],
        compiler_params=pltpu.CompilerParams(vmem_limit_bytes=32 * 1024 * 1024),
    )(order, first, second)


READY = {"highway1": 12.0, "highway0": 16.0, "small": 24.0}
CONV_AFTER = [("highway0", "b", "z", 1)]
GATHER_KINDS = {"highway0": "P", "highway1": "Q", "encoder": "P"}
SCATTER_KINDS = {"encoder": "P", "highway1": "P", "highway0": "Q"}


def times_pieces(values, pieces):
    columns = jnp.split(values, len(pieces), axis=1)
    return reduce(
        jnp.add,
        [
            jnp.dot(column, piece, preferred_element_type=jnp.float32)
            for column, piece in zip(columns, pieces)
        ],
    )


def packed(values):
    width = 1024
    flat = [value.reshape(-1) for value in values]
    flat = [jnp.pad(value, (0, -value.shape[0] % width)).reshape(-1, width) for value in flat]
    rows = jnp.concatenate(flat, axis=0)
    return jnp.pad(rows, ((0, -rows.shape[0] % 16), (0, 0)))


def unpacked(rows, values):
    totals = []
    first = 0
    for value in values:
        count = -(-value.size // rows.shape[1])
        taken = rows[first : first + count].reshape(-1)
        totals.append(taken[: value.size].reshape(value.shape))
        first += count
    return totals


def per_device(
    char_ids,
    char_mask,
    word_lengths,
    char_table,
    conv_weight,
    conv_bias,
    highway_weight,
    highway_bias,
    proj_weight,
    qkv_weight,
    qv_bias,
    out_weight,
    up_weight,
    up_bias,
    down_weight,
    vector_biases,
    norm_gains,
    cotangent,
):
    f32 = jnp.float32
    bf16 = jnp.bfloat16
    own_filters = conv_weight.shape[1]
    widths = channel_widths(lax.axis_index("narrow") * own_filters, own_filters)
    tap_rows = jnp.arange(TAPS * CHAR_DIM, dtype=jnp.int32) // CHAR_DIM
    tap_mask = (tap_rows[:, None] < widths[None, :]).astype(bf16)
    tap_pad = ((0, LANES - TAPS * CHAR_DIM), (0, 0))
    masked_filters = jnp.pad(conv_weight * tap_mask, tap_pad)
    chan_scale = jnp.sqrt(TAPS / widths.astype(f32))
    word_count = char_ids.shape[0]
    seq_count = word_count // LENGTH
    places = jnp.arange(CHARS_MAX, dtype=jnp.int32)
    alive = (char_mask > 0) & (places[None, :] < word_lengths[:, None])
    picks = word_order(word_lengths)
    picks_low = picks.astype(bf16)
    told = jnp.concatenate(
        [jnp.where(alive, char_ids, -1), word_lengths[:, None]], axis=1
    ).astype(f32)
    told = jnp.dot(picks, told, precision=lax.Precision.HIGHEST)
    lens = told[:, CHARS_MAX:]
    tile_count = word_count // TILE
    longest = jnp.max(lens.astype(jnp.int32).reshape(tile_count, TILE), axis=1)
    tile_chunks = (longest + CHUNK - 1) // CHUNK
    spread_ids = jnp.pad(
        told[:, :CHARS_MAX].astype(jnp.int32),
        ((0, 0), (0, SLOTS - CHARS_MAX)),
        constant_values=-1,
    )
    spread_ids = spread_ids.reshape(tile_count, TILE, SLOTS // CHUNK, CHUNK)
    spread_ids = spread_ids.transpose(0, 2, 3, 1).reshape(-1, CHUNK * TILE)
    table_t = jnp.pad(
        jnp.tile(char_table.T, (TAPS, 1)), (tap_pad[0], (0, IDS - CHAR_VOCAB))
    )
    tap_lanes = (
        jnp.arange(LANES, dtype=jnp.int32)[None, :] // CHAR_DIM
        == jnp.arange(8, dtype=jnp.int32)[:, None]
    ).astype(f32)
    scale_row, bias_row = chan_scale[None, :], conv_bias[None, :]
    width_row = widths.astype(f32)[None, :]
    pool, pool_back = conv_calls(word_count, own_filters)
    here = lax.axis_index("wide")
    core = lax.axis_index("narrow")
    routed = lax.axis_size("wide") == CHIPS
    width_proj, width_qkv, width_out = own_filters, 3 * qkv_weight.shape[2], out_weight.shape[0]
    width_up, width_down = up_weight.shape[1], down_weight.shape[0]
    feature_rows = qkv_weight.shape[0]
    first_rows = jnp.concatenate(
        [proj_weight.T, qkv_weight.reshape(feature_rows, width_qkv), out_weight.T], axis=1
    )
    second_rows = jnp.concatenate([up_weight, down_weight.T], axis=1)

    def whole_rows(shard):
        return lax.all_gather(shard, "wide", axis=0, tiled=True)

    def own_rows(terms):
        return lax.psum_scatter(terms.astype(f32), "wide", scatter_dimension=0, tiled=True)

    arrived = {}

    def after(value, moves):
        ended = [arrived[move] for move in moves if move in arrived]
        return lax.optimization_barrier((value, *ended))[0] if ended else value

    if routed:
        full, arrived = gather_matrices(
            {
                "highway0": [highway_weight[0, :, part] for part in range(2)],
                "highway1": [highway_weight[1, :, part] for part in range(2)],
                "encoder": [first_rows, second_rows],
            },
            GATHER_KINDS,
        )
        highway_full = [
            [full[f"highway{layer}", part] for part in "ab"] for layer in range(HW_LAYERS)
        ]
        gathered_blocks = {part: blocks_of(GATHER_KINDS["encoder"], part) for part in "ab"}
        scattered_blocks = {part: blocks_of(SCATTER_KINDS["encoder"], part) for part in "ab"}
        features = gathered_blocks["a"]
        first_full, second_full = [
            moved_blocks(full["encoder", part], gathered_blocks[part], features, 1)[0]
            for part in "ab"
        ]
        feature_order = owners(features, here)
    else:
        highway_full = [
            [[whole_rows(highway_weight[layer, :, part])] for part in range(2)]
            for layer in range(HW_LAYERS)
        ]
        first_full, second_full = whole_rows(first_rows), whole_rows(second_rows)
        feature_order = jnp.arange(lax.axis_size("wide"), dtype=jnp.int32)
    embedded, pooled, pool_shift = pool(
        after(tile_chunks, CONV_AFTER), spread_ids, table_t, tap_lanes, masked_filters, scale_row, bias_row, lens,
        width_row,
    )
    current = gelu_exact(pooled).astype(bf16)
    proj_t, qkv_full, out_t = jnp.split(
        first_full, [width_proj, width_proj + width_qkv], axis=1
    )
    up_full, down_t = jnp.split(second_full, [width_up], axis=1)
    feature_count = proj_t.shape[0]
    feature_picks = (
        feature_order[:, None] == jnp.arange(feature_order.shape[0], dtype=jnp.int32)[None, :]
    ).astype(f32)
    feature_places = (
        feature_order[:, None] * feature_rows + jnp.arange(feature_rows, dtype=jnp.int32)[None, :]
    ).reshape(-1)
    feature_moves = (
        feature_places[:, None] == jnp.arange(feature_count, dtype=jnp.int32)[None, :]
    ).astype(bf16)

    def pick_features(rows, picks):
        blocked = rows.reshape(rows.shape[0], -1, feature_rows)
        return jnp.einsum(
            "kwr,bw->kbr", blocked, picks, precision=lax.Precision.HIGHEST
        ).reshape(rows.shape)

    vector_biases = pick_features(vector_biases, feature_picks)
    norm_gains = pick_features(norm_gains, feature_picks)
    grad_output = jnp.dot(cotangent, feature_moves.T, preferred_element_type=f32).astype(bf16)
    grad_output = jnp.dot(picks_low, grad_output, preferred_element_type=f32)
    kept_layers = []
    for layer_index in range(HW_LAYERS):
        if routed:
            name = f"highway{layer_index}"
            orders = {}
            for kind in (GATHER_KINDS[name], SCATTER_KINDS[name]):
                order = jnp.stack([owners(blocks_of(kind, part), here) for part in "ab"])
                orders[kind] = (order - core * (CHIPS // 2)) % CHIPS
            order = orders[GATHER_KINDS[name]]
            whole_input = permute_channels(
                jnp.concatenate(list(orders.values())), current, swap(current)
            )
            grad_input = whole_input[-2:]
        else:
            order = None
            whole_input = [lax.all_gather(current, "narrow", axis=1, tiled=True)] * 2
            grad_input = whole_input
        mixed_pre = (
            jnp.stack(
                [
                    times_pieces(whole_input[part], highway_full[layer_index][part])
                    for part in range(2)
                ],
                axis=1,
            )
            + highway_bias[layer_index]
        )
        carried = current.astype(f32)
        kept_layers.append((grad_input, mixed_pre, carried, order))
        current = highway_mix(mixed_pre, carried).astype(bf16)
    start_rows = (
        pair_sum(jnp.dot(current, proj_t.T, preferred_element_type=f32)) + vector_biases[0]
    )
    start_low = start_rows.astype(bf16)
    qkv_bias = jnp.concatenate([qv_bias[0], jnp.zeros_like(qv_bias[0]), qv_bias[1]])
    projected = (
        jnp.dot(start_low, qkv_full, preferred_element_type=f32) + qkv_bias
    ).astype(bf16)
    head_shape = (word_count, -1, HEAD_DIM)
    query, keys_here, values_here = [
        part.reshape(head_shape) for part in jnp.split(projected, 3, axis=1)
    ]
    attn_scale = HEAD_DIM ** (-0.5)
    sequence = jnp.arange(word_count, dtype=jnp.int32) // 8 % seq_count
    together = (sequence[:, None] == sequence[None, :])[None]
    scores = jnp.einsum("qhe,khe->hqk", query, keys_here, preferred_element_type=f32) * attn_scale
    scores = jnp.where(together, scores, -1e30)
    weights = jnp.exp(scores - jnp.max(scores, axis=-1, keepdims=True))
    probs = weights / jnp.sum(weights, axis=-1, keepdims=True)
    probs_low = probs.astype(bf16)
    context = (
        jnp.einsum("hqk,khe->qhe", probs_low, values_here, preferred_element_type=f32)
        .reshape(word_count, -1)
        .astype(bf16)
    )
    attended = pair_sum(jnp.dot(context, out_t.T, preferred_element_type=f32)) + vector_biases[1]
    before_one = start_rows + attended
    normed_one = layer_norm(before_one, norm_gains[0], vector_biases[3])
    normed_low = normed_one.astype(bf16)
    hidden_pre = jnp.dot(normed_low, up_full, preferred_element_type=f32) + up_bias
    hidden_low = gelu_exact(hidden_pre).astype(bf16)
    lowered = (
        pair_sum(jnp.dot(hidden_low, down_t.T, preferred_element_type=f32)) + vector_biases[2]
    )
    before_two = normed_one + lowered
    encoded = layer_norm(before_two, norm_gains[1], vector_biases[4]).astype(bf16)
    encoded = jnp.dot(encoded, feature_moves, preferred_element_type=f32).astype(bf16)
    encoded = jnp.dot(picks_low.T, encoded, preferred_element_type=f32).astype(bf16)
    ln_two_back = jax.vjp(layer_norm, before_two, norm_gains[1], vector_biases[4])[1]
    grad_before_two, gain_two, bias_two = ln_two_back(grad_output)
    grad_lowered = grad_before_two.astype(bf16)
    down_grad_local = jnp.dot(grad_lowered.T, hidden_low, preferred_element_type=f32)
    bias_down = jnp.sum(grad_lowered.astype(f32), axis=0)
    grad_hidden = jnp.dot(grad_lowered, down_t, preferred_element_type=f32)
    grad_hidden_pre = jax.vjp(gelu_exact, hidden_pre)[1](grad_hidden)[0].astype(bf16)
    up_grad_local = jnp.dot(normed_low.T, grad_hidden_pre, preferred_element_type=f32)
    bias_up = jnp.sum(grad_hidden_pre.astype(f32), axis=0)
    grad_normed_one = grad_before_two + pair_grad_sum(
        jnp.dot(grad_hidden_pre, up_full.T, preferred_element_type=f32)
    )
    ln_one_back = jax.vjp(layer_norm, before_one, norm_gains[0], vector_biases[3])[1]
    grad_before_one, gain_one, bias_one = ln_one_back(grad_normed_one)
    grad_attended = grad_before_one.astype(bf16)
    out_grad_local = jnp.dot(grad_attended.T, context, preferred_element_type=f32)
    bias_attended = jnp.sum(grad_attended.astype(f32), axis=0)
    grad_context = (
        jnp.dot(grad_attended, out_t, preferred_element_type=f32)
        .astype(bf16)
        .reshape(head_shape)
    )
    grad_probs = jnp.einsum(
        "qhe,khe->hqk", grad_context, values_here, preferred_element_type=f32
    )
    grad_value = jnp.einsum("hqk,qhe->khe", probs_low, grad_context, preferred_element_type=f32)
    grad_scores = (
        probs * (grad_probs - jnp.sum(probs * grad_probs, axis=-1, keepdims=True))
    ).astype(bf16)
    grad_query = (
        jnp.einsum("hqk,khe->qhe", grad_scores, keys_here, preferred_element_type=f32) * attn_scale
    )
    grad_key = (
        jnp.einsum("hqk,qhe->khe", grad_scores, query, preferred_element_type=f32) * attn_scale
    )
    grad_projected = jnp.concatenate(
        [grad.reshape(word_count, -1).astype(bf16) for grad in (grad_query, grad_key, grad_value)],
        axis=1,
    )
    qkv_grad_local = jnp.dot(start_low.T, grad_projected, preferred_element_type=f32)
    bias_qkv = jnp.sum(grad_projected.astype(f32), axis=0).reshape(3, -1)
    bias_qv = bias_qkv[0::2]
    grad_start = grad_before_one + pair_grad_sum(
        jnp.dot(grad_projected, qkv_full.T, preferred_element_type=f32)
    )
    grad_start_low = grad_start.astype(bf16)
    proj_grad_local = jnp.dot(grad_start_low.T, current, preferred_element_type=f32)
    bias_start = jnp.sum(grad_start_low.astype(f32), axis=0)
    grad_current = jnp.dot(grad_start_low, proj_t, preferred_element_type=f32)
    first_grad_local = jnp.concatenate(
        [proj_grad_local, qkv_grad_local, out_grad_local], axis=1
    ).astype(bf16)
    second_grad_local = jnp.concatenate([up_grad_local, down_grad_local], axis=1).astype(bf16)
    terms = {}
    if routed:
        for part, local in (("a", first_grad_local), ("b", second_grad_local)):
            terms["encoder", part] = moved_blocks([local], features, scattered_blocks[part], 4)
    highway_grads = []
    highway_bias_grads = []
    for layer_index in reversed(range(HW_LAYERS)):
        grad_input, mixed_pre, carried, order = kept_layers[layer_index]
        mix_back = jax.vjp(highway_mix, mixed_pre, carried)[1]
        grad_mixed, grad_carried = mix_back(grad_current)
        grad_mixed_low = grad_mixed.astype(bf16)
        part_grads = []
        grad_whole = []
        for part in range(2):
            part_mixed = grad_mixed_low[:, part]
            pieces = highway_full[layer_index][part]
            part_grads.append(
                [
                    jnp.dot(columns.T, part_mixed, preferred_element_type=f32).astype(bf16)
                    for columns in jnp.split(grad_input[part], len(pieces), axis=1)
                ]
            )
            grad_whole.append(
                jnp.concatenate(
                    [
                        jnp.dot(part_mixed, piece.T, preferred_element_type=f32)
                        for piece in pieces
                    ],
                    axis=1,
                )
            )
        if routed:
            terms.update(zip([(f"highway{layer_index}", part) for part in "ab"], part_grads))
        else:
            highway_grads.insert(
                0, jnp.stack([own_rows(joined(pieces)) for pieces in part_grads], axis=1)
            )
        highway_bias_grads.insert(0, jnp.sum(grad_mixed_low.astype(f32), axis=0))
        if routed:
            grad_own, grad_other = unpermute_sum(order, *grad_whole)
            grad_current = grad_carried + add(grad_own, swap(grad_other))
        else:
            grad_current = grad_carried + lax.psum_scatter(
                add(*grad_whole).astype(bf16), "narrow", scatter_dimension=1, tiled=True
            ).astype(f32)
    highway_bias_local = jnp.stack(highway_bias_grads)
    grad_pooled = jax.vjp(gelu_exact, pooled)[1](grad_current)[0]
    grad_filter, grad_marks = pool_back(
        tile_chunks, spread_ids, tap_lanes, masked_filters, scale_row, lens, width_row, embedded,
        pool_shift, grad_pooled,
    )
    grad_filter = grad_filter[: TAPS * CHAR_DIM]
    grad_conv_bias = jnp.sum(grad_pooled, axis=0)
    grad_marks = grad_marks[:CHAR_VOCAB, :LANES] + grad_marks[:CHAR_VOCAB, LANES:]
    grad_chars = jnp.sum(
        grad_marks[:, : TAPS * CHAR_DIM].reshape(CHAR_VOCAB, TAPS, CHAR_DIM), axis=1
    )
    grad_filter = grad_filter * tap_mask.astype(f32)
    bias_local = pick_features(
        jnp.stack([bias_start, bias_attended, bias_down, bias_one, bias_two]), feature_picks.T
    )
    gain_local = pick_features(jnp.stack([gain_one, gain_two]), feature_picks.T)
    locals_small = (
        grad_filter,
        grad_conv_bias,
        highway_bias_local,
        bias_qv,
        bias_up,
        bias_local,
        gain_local,
        pair_sum(grad_chars),
    )
    if routed:
        sums, small = scatter_matrices(terms, SCATTER_KINDS, packed(locals_small), READY)
        small_sums = unpacked(small, locals_small)
        highway_grads = [
            sums[f"highway{layer}"].reshape(highway_weight.shape[1:]) for layer in range(HW_LAYERS)
        ]
        first_grad, second_grad = jnp.split(sums["encoder"], [first_rows.shape[1]], axis=1)
    else:
        first_grad, second_grad = own_rows(first_grad_local), own_rows(second_grad_local)
        small_sums = lax.psum(locals_small, "wide")
    highway_grad = jnp.stack(highway_grads)
    proj_grad, qkv_grad, out_grad = jnp.split(
        first_grad, [width_proj, width_proj + width_qkv], axis=1
    )
    up_grad, down_grad = jnp.split(second_grad, [width_up], axis=1)
    proj_grad, out_grad, down_grad = proj_grad.T, out_grad.T, down_grad.T
    qkv_grad = qkv_grad.reshape(qkv_weight.shape)
    (
        conv_grad,
        conv_bias_grad,
        highway_bias_grad,
        qv_bias_grad,
        up_bias_grad,
        bias_grads,
        gain_grads,
        char_grad,
    ) = small_sums
    return (
        encoded,
        char_grad,
        conv_grad,
        conv_bias_grad,
        highway_grad,
        highway_bias_grad,
        proj_grad,
        qkv_grad,
        qv_bias_grad,
        out_grad,
        up_grad,
        up_bias_grad,
        down_grad,
        bias_grads,
        gain_grads,
    )


def solution(mesh):
    placed = (
        P("wide", None),
        P("wide", None),
        P("wide"),
        P(),
        P(None, "narrow"),
        P("narrow"),
        P(None, "wide", None, "narrow"),
        P(None, None, "narrow"),
        P("narrow", "wide"),
        P("wide", None, "narrow"),
        P(None, "narrow"),
        P("narrow", "wide"),
        P("wide", "narrow"),
        P("narrow"),
        P("narrow", "wide"),
        P(),
        P(),
        P("wide", None),
    )
    return jax.shard_map(
        per_device,
        mesh=mesh,
        in_specs=placed,
        out_specs=(
            P("wide", None),
            P(),
            P(None, "narrow"),
            P("narrow"),
            P(None, "wide", None, "narrow"),
            P(None, None, "narrow"),
            P("narrow", "wide"),
            P("wide", None, "narrow"),
            P(None, "narrow"),
            P("narrow", "wide"),
            P("wide", "narrow"),
            P("narrow"),
            P("narrow", "wide"),
            P(),
            P(),
        ),
        check_vma=False,
    )
```

```python
import math
from functools import partial

import jax
import jax.numpy as jnp
from jax import lax
from jax.experimental import pallas as pl
from jax.experimental.pallas import tpu as pltpu
from jax.sharding import PartitionSpec as P

HEAD_DIM = 64
FILTERS = 2048
CHAR_DIM = 16
CHAR_VOCAB = 262
CHARS_MAX = 50
TAPS = 7
HW_LAYERS = 2
TILE = 16
CHUNK = 8
SLOTS = 64
IDS = 272
LANES = 128
BLOCK = 256
LOG2E = 1.4426950408889634
LENGTH = 128


BOUNDS = ((1, 2), (3, 4), (7, 8), (15, 16), (31, 32), (63, 64))
EPSILON = 1e-06


def channel_widths(first_channel, count):
    channels = first_channel + jnp.arange(count, dtype=jnp.int32)
    widths = jnp.full((count,), TAPS, jnp.int32)
    for numerator, denominator in BOUNDS:
        widths = widths - (channels >= FILTERS * numerator // denominator).astype(jnp.int32)
    return widths


def gelu_exact(values):
    return jax.nn.gelu(values, approximate=False)


def layer_norm(values, gain_row, bias_row):
    center = jnp.mean(values, axis=-1, keepdims=True)
    spread = jnp.mean(jnp.square(values - center), axis=-1, keepdims=True)
    return (values - center) * lax.rsqrt(spread + EPSILON) * gain_row + bias_row


def word_order(lengths):
    words = lengths.shape[0]
    sequences = words // LENGTH
    spots = jnp.arange(words, dtype=jnp.int32)
    keys = lengths * LENGTH + (LENGTH - 1 - spots % LENGTH)
    same = spots[:, None] // LENGTH == spots[None, :] // LENGTH
    ranks = jnp.sum((same & (keys[None, :] > keys[:, None])).astype(jnp.int32), axis=1)
    places = ranks // 8 * (8 * sequences) + spots // LENGTH * 8 + ranks % 8
    return (places[None, :] == spots[:, None]).astype(jnp.float32)


def spot_chars(ids_row, table_t):
    ids = lax.broadcasted_iota(jnp.int32, (IDS, LANES), 0)
    marks = (ids == ids_row).astype(jnp.float32).astype(jnp.bfloat16)
    return jnp.dot(table_t, marks, preferred_element_type=jnp.float32).T.astype(jnp.bfloat16)


def tap_rows(table_ref, start, tile, tap_lanes):
    rows = pl.ds(pl.multiple_of(tile * TILE, TILE), TILE)
    taken = None
    for tap in range(TAPS):
        piece = table_ref[pl.ds(start + tap, CHUNK), rows, :] * tap_lanes[tap][None]
        taken = piece if taken is None else taken + piece
    return taken.reshape(CHUNK * TILE, LANES)


def window_counts(lens_ref, widths_ref, tile):
    rows = pl.ds(pl.multiple_of(tile * TILE, TILE), TILE)
    return jnp.maximum(lens_ref[rows, :1] - widths_ref[...] + 1.0, 1.0)


def pool_kernel(
    tile_ref, ids_ref, table_ref, lanes_ref, filters_ref, scale_ref, bias_ref, lens_ref, widths_ref,
    embed_ref, pooled_ref, shift_ref, conv_ref, count_ref, top_ref,
):
    channels = filters_ref.shape[1]
    chunks_all = SLOTS // CHUNK
    tap_lanes = [lanes_ref[tap : tap + 1, :].astype(jnp.bfloat16) for tap in range(TAPS)]
    blocks = [slice(first, first + BLOCK) for first in range(0, channels, BLOCK)]

    def one_tile(tile, _):
        rows = pl.ds(pl.multiple_of(tile * TILE, TILE), TILE)
        chunks = tile_ref[tile]

        def embed(chunk, _):
            found = spot_chars(ids_ref[pl.ds(tile * chunks_all + chunk, 1), :], table_ref[...])
            embed_ref[pl.ds(chunk * CHUNK, CHUNK), rows, :] = found.reshape(CHUNK, TILE, LANES)
            return 0

        lax.fori_loop(0, chunks, embed, 0)
        embed_ref[pl.ds(chunks * CHUNK, CHUNK), rows, :] = jnp.zeros(
            (CHUNK, TILE, LANES), jnp.bfloat16
        )
        count_ref[...] = window_counts(lens_ref, widths_ref, tile)
        top_ref[...] = jnp.full(top_ref.shape, -1e30, jnp.float32)

        def convolve(chunk, _):
            columns = tap_rows(embed_ref, chunk * CHUNK, tile, tap_lanes)
            first = (chunk * CHUNK).astype(jnp.float32)
            for block in blocks:
                convolved = jnp.dot(
                    columns, filters_ref[:, block], preferred_element_type=jnp.float32
                )
                conv_ref[chunk, :, block] = convolved
                counts = count_ref[:, block] - first
                top = top_ref[:, block]
                for place in range(CHUNK):
                    row = convolved[place * TILE : (place + 1) * TILE]
                    top = jnp.maximum(top, jnp.where(counts > float(place), row, -1e30))
                top_ref[:, block] = top
            return 0

        lax.fori_loop(0, chunks, convolve, 0)
        pooled_ref[rows, :] = jnp.zeros((TILE, channels), jnp.float32)

        def weigh(chunk, _):
            first = (chunk * CHUNK).astype(jnp.float32)
            for block in blocks:
                counts = count_ref[:, block] - first
                scale = scale_ref[:, block] * LOG2E
                offset = top_ref[:, block] * scale
                total = pooled_ref[rows, block]
                for place in range(CHUNK):
                    row = conv_ref[chunk, place * TILE : (place + 1) * TILE, block]
                    weight = jnp.exp2(row * scale - offset)
                    total = total + jnp.where(counts > float(place), weight, 0.0)
                pooled_ref[rows, block] = total
            return 0

        lax.fori_loop(0, chunks, weigh, 0)
        top = top_ref[...] * scale_ref[...]
        log_total = jnp.log(pooled_ref[rows, :])
        pooled_ref[rows, :] = top + bias_ref[...] + log_total - jnp.log(count_ref[...])
        shift_ref[rows, :] = (top + log_total) * -LOG2E
        return 0

    lax.fori_loop(0, tile_ref.shape[0], one_tile, 0)


def pool_back_kernel(
    tile_ref, ids_ref, lanes_ref, filters_ref, scale_ref, lens_ref, widths_ref, embed_ref, shift_ref,
    grad_ref, filter_before_ref, char_before_ref, filter_grad_ref, char_grad_ref, conv_grad_ref,
    column_ref, count_ref,
):
    channels = filters_ref.shape[1]
    chunks_all = SLOTS // CHUNK
    tap_lanes = [lanes_ref[tap : tap + 1, :].astype(jnp.bfloat16) for tap in range(TAPS)]
    lane_taps = lax.broadcasted_iota(jnp.int32, (1, 1, LANES), 2) // CHAR_DIM
    blocks = [slice(first, first + BLOCK) for first in range(0, channels, BLOCK)]
    filter_grad_ref[...] = filter_before_ref[...]
    char_grad_ref[...] = char_before_ref[...]
    column_ref[:CHUNK] = jnp.zeros((CHUNK, TILE, LANES), jnp.float32)

    def one_tile(tile, _):
        rows = pl.ds(pl.multiple_of(tile * TILE, TILE), TILE)
        chunks = tile_ref[tile]
        count_ref[...] = window_counts(lens_ref, widths_ref, tile)

        def one_chunk(chunk, _):
            columns = tap_rows(embed_ref, chunk * CHUNK, tile, tap_lanes)
            columns_t = columns.astype(jnp.float32).T.astype(jnp.bfloat16)
            first = (chunk * CHUNK).astype(jnp.float32)
            grad_columns = None
            for block in blocks:
                filters = filters_ref[:, block]
                convolved = jnp.dot(columns, filters, preferred_element_type=jnp.float32)
                counts = count_ref[:, block] - first
                scale = scale_ref[:, block]
                scale2 = scale * LOG2E
                shift = shift_ref[rows, block]
                grad = grad_ref[rows, block] * scale
                for place in range(CHUNK):
                    row = convolved[place * TILE : (place + 1) * TILE]
                    share = jnp.exp2(row * scale2 + shift)
                    conv_grad_ref[place * TILE : (place + 1) * TILE, block] = jnp.where(
                        counts > float(place), share * grad, 0.0
                    ).astype(jnp.bfloat16)
                conv_grad = conv_grad_ref[:, block]
                filter_grad_ref[:, block] += jnp.dot(
                    columns_t, conv_grad, preferred_element_type=jnp.float32
                )
                piece = lax.dot_general(
                    conv_grad, filters, (((1,), (1,)), ((), ())), preferred_element_type=jnp.float32
                )
                grad_columns = piece if grad_columns is None else grad_columns + piece
            column_ref[pl.ds(chunk * CHUNK + CHUNK, CHUNK)] = grad_columns.reshape(
                CHUNK, TILE, LANES
            )
            return 0

        lax.fori_loop(0, chunks, one_chunk, 0)

        def fold(chunk, _):
            moved = None
            for tap in range(TAPS):
                piece = column_ref[pl.ds(chunk * CHUNK + CHUNK - tap, CHUNK)]
                moved = piece if moved is None else jnp.where(lane_taps == tap, piece, moved)
            moved = moved.reshape(CHUNK * TILE, LANES)
            high = moved.astype(jnp.bfloat16)
            low = (moved - high.astype(jnp.float32)).astype(jnp.bfloat16)
            ids = lax.broadcasted_iota(jnp.int32, (IDS, LANES), 0)
            ids_row = ids_ref[pl.ds(tile * chunks_all + chunk, 1), :]
            marks = (ids == ids_row).astype(jnp.float32).astype(jnp.bfloat16)
            char_grad_ref[...] += jnp.dot(
                marks, jnp.concatenate([high, low], axis=1), preferred_element_type=jnp.float32
            )
            return 0

        lax.fori_loop(0, chunks, fold, 0)
        return 0

    lax.fori_loop(0, tile_ref.shape[0], one_tile, 0)


def conv_calls(words, channels):
    vmem = pl.BlockSpec(memory_space=pltpu.VMEM)
    smem = pl.BlockSpec(memory_space=pltpu.SMEM)
    shape = partial(jax.ShapeDtypeStruct, dtype=jnp.float32)
    params = pltpu.CompilerParams(vmem_limit_bytes=40 * 1024 * 1024)
    pool = pl.pallas_call(
        pool_kernel,
        out_shape=[
            jax.ShapeDtypeStruct((SLOTS, words, LANES), jnp.bfloat16),
            shape((words, channels)),
            shape((words, channels)),
        ],
        in_specs=[smem] + [vmem] * 8,
        out_specs=[vmem] * 3,
        scratch_shapes=[
            pltpu.VMEM((SLOTS // CHUNK, CHUNK * TILE, channels), jnp.float32),
            pltpu.VMEM((TILE, channels), jnp.float32),
            pltpu.VMEM((TILE, channels), jnp.float32),
        ],
        compiler_params=params,
        cost_estimate=pl.CostEstimate(
            flops=2_000_000_000, bytes_accessed=8_000_000, transcendentals=5_000_000
        ),
    )
    back = pl.pallas_call(
        pool_back_kernel,
        out_shape=[shape((LANES, channels)), shape((IDS, 2 * LANES))],
        in_specs=[smem] + [vmem] * 11,
        out_specs=[vmem] * 2,
        scratch_shapes=[
            pltpu.VMEM((CHUNK * TILE, channels), jnp.bfloat16),
            pltpu.VMEM((SLOTS + CHUNK, TILE, LANES), jnp.float32),
            pltpu.VMEM((TILE, channels), jnp.float32),
        ],
        compiler_params=params,
        cost_estimate=pl.CostEstimate(
            flops=4_000_000_000, bytes_accessed=10_000_000, transcendentals=5_000_000
        ),
    )
    return pool, back


STEPS = {
    "x": [(i, i ^ 1) for i in range(16)],
    "y": [(i, i ^ 2) for i in range(16)],
    "z": [(i, (i + 4) % 16) for i in range(16)],
    "near": [(i, i ^ 4) for i in range(16)],
    "far": [(i, i ^ 8) for i in range(16)],
}
CHIPS = 16
SWAP = [(0, 1), (1, 0)]


def step(value, axis):
    return lax.ppermute(value, "wide", STEPS[axis])


def swap(value):
    return lax.ppermute(value, "narrow", SWAP)


def joined(pieces):
    return pieces[0] if len(pieces) == 1 else jnp.concatenate(pieces, axis=0)


def add(one, other):
    return one.astype(jnp.float32) + other.astype(jnp.float32)


FIRST = {"a": "x", "b": "y"}
LAST = {"a": "y", "b": "x"}
TURNS = (1, 2, 3)
SMALL_MOVES = {
    ("small", "x"): ("x", 1, []),
    ("small", "y"): ("y", 1, [("small", "x")]),
    ("small", "near"): ("z", 1, [("small", "y")]),
    ("small", "far"): ("z", 2, [("small", "near")]),
}


def moves_of(kind):
    moves = {}
    if kind == "Q":
        for turn in TURNS:
            moves["z", turn] = ("z", 2, [("z", turn - 1)] if turn > 1 else [])
    for part in "ab":
        if kind == "P":
            moves[part, "first"] = (FIRST[part], 1, [])
            for turn in TURNS:
                before = (part, "z", turn - 1) if turn > 1 else (part, "first")
                moves[part, "z", turn] = ("z", 2, [before])
            for half in (0, 1):
                moves[part, "last", half] = (LAST[part], 4, [(part, "z", 1 + 2 * half)])
        else:
            for half in (0, 1):
                moves[part, "first", half] = (FIRST[part], 2, [("z", 1 + 2 * half)])
                moves[part, "last", half] = (LAST[part], 4, [(part, "first", half)])
    return moves


def back_moves_of(kind):
    moves = {}
    for part in "ab":
        for half in (0, 1):
            moves[part, "last", half] = (LAST[part], 4, [])
        if kind == "P":
            moves[part, "z", 1] = ("z", 2, [(part, "last", 0)])
            moves[part, "z", 2] = ("z", 2, [(part, "z", 1), (part, "last", 1)])
            moves[part, "z", 3] = ("z", 2, [(part, "z", 2)])
            moves[part, "first"] = (FIRST[part], 1, [(part, "z", 3)])
        else:
            for half in (0, 1):
                moves[part, "first", half] = (FIRST[part], 2, [(part, "last", half)])
    if kind == "Q":
        moves["z", 1] = ("z", 2, [("a", "first", 0), ("b", "first", 0)])
        moves["z", 2] = ("z", 2, [("z", 1), ("a", "first", 1), ("b", "first", 1)])
        moves["z", 3] = ("z", 2, [("z", 2)])
    return moves


class Schedule:
    def __init__(self, kinds, moves_of_kind, ready, extra, ranks, lag=0.7):
        moves = dict(extra)
        for name, kind in kinds.items():
            for move, (axis, load, needs) in moves_of_kind(kind).items():
                moves[(name,) + move] = (axis, load, [(name,) + need for need in needs])
        self.moves, self.got, self.sent = moves, {}, {"x": [], "y": [], "z": []}
        self.values = {}
        users = {move: [] for move in moves}
        for move, (_, _, needs) in moves.items():
            for need in needs:
                users[need].append(move)
        tails = {}

        def tail(move):
            if move not in tails:
                tails[move] = moves[move][1] + lag + max(map(tail, users[move]), default=0.0)
            return tails[move]

        places = {move: place for place, move in enumerate(moves)}
        free, waiting = {"x": 0.0, "y": 0.0, "z": 0.0}, dict(moves)
        self.starts, self.ends = {}, {}
        while waiting:
            best = None
            for move, (axis, load, needs) in waiting.items():
                if all(need in self.ends for need in needs):
                    start = max(
                        [ready.get(move[:2], ready.get(move[0], 0.0)), free[axis]]
                        + [self.ends[need] + lag for need in needs]
                    )
                    rank = ranks.get(move[:2], ranks.get(move[0], 0))
                    key = (start, rank - tail(move), places[move])
                    if best is None or key < best[0]:
                        best = (key, start, move)
            _, start, move = best
            axis, load, _ = waiting.pop(move)
            self.starts[move] = start
            self.ends[move] = free[axis] = start + load
        self.order = list(self.starts)

    def after(self, value, time):
        known = []
        for axis in "xyz":
            for times, arrays in ((self.ends, self.got), (self.starts, self.values)):
                past = [m for m in arrays if self.moves[m][0] == axis and times[m] <= time]
                if past:
                    known.append(arrays[max(past, key=times.get)])
        return lax.optimization_barrier((value, *known))[0] if known else value

    def after_all(self, value, *names):
        return self.after(
            value, max(end for move, end in self.ends.items() if move[: len(names)] == names)
        )

    def send(self, move, value, way):
        axis = self.moves[move][0]
        sent = self.sent[axis]
        if len(sent) > 1:
            value = lax.optimization_barrier((value, sent[-2]))[0]
        value = self.after(value, self.starts[move] - SLACK)
        self.values[move] = value
        self.got[move] = step(value, way)
        sent.append(self.got[move])
        return self.got[move]


def blocks_of(kind, part):
    blocks = []
    for last in (0, 1):
        for half in (0, 1):
            turns = (2 * half, 2 * half + 1)
            if kind == "P":
                pairs = [(turn, first) for turn in turns for first in (0, 1)]
            else:
                pairs = [(turn, first) for first in (0, 1) for turn in turns]
            for turn, first in pairs:
                blocks.append((turn, first, last) if part == "b" else (turn, last, first))
    return blocks


def owners(blocks, here):
    z, y, x = here // 4, (here // 2) % 2, here % 2
    return jnp.stack(
        [((z - dz) % 4) * 4 + (y + dy) % 2 * 2 + (x + dx) % 2 for dz, dy, dx in blocks]
    ).astype(jnp.int32)


def gather_matrices(shards, kinds):
    plan = Schedule(kinds, moves_of, {}, {}, GATHER_RANKS)
    got, sent = plan.got, {}
    for move in plan.order:
        name, kind = move[0], kinds[move[0]]
        parts = dict(zip("ab", shards[name]))
        way = plan.moves[move][0]
        if "z" in move:
            turn = move[-1]
            if turn > 1:
                value = got[move[:-1] + (turn - 1,)]
            elif kind == "P":
                part = move[1]
                value = joined([parts[part], got[name, part, "first"]])
                sent[name, part, "pair"] = value
            else:
                value = joined_lanes(shards[name])
        else:
            part, stage = move[1:3]
            turns = (2 * move[3], 2 * move[3] + 1) if len(move) == 4 else ()
            if kind == "P" and stage == "first":
                value = parts[part]
            elif kind == "P":
                value = joined(
                    [got[name, part, "z", turn] if turn else sent[name, part, "pair"] for turn in turns]
                )
            elif stage == "first":
                width = parts["a"].shape[1]
                lanes = slice(0, width) if part == "a" else slice(width, None)
                value = joined(
                    [got[name, "z", turn][:, lanes] if turn else parts[part] for turn in turns]
                )
            else:
                value = joined([sent[name, part, "first", move[3]], got[name, part, "first", move[3]]])
        sent[move] = value
        plan.send(move, value, way)
    full = {
        (name, part): [held[name, part, "last", half] for held in (sent, got) for half in (0, 1)]
        for name in kinds
        for part in "ab"
    }
    return full, plan


def joined_lanes(pieces):
    return jnp.concatenate(pieces, axis=1)


class Scatter:
    def __init__(self, kinds, ready):
        self.kinds, self.terms, self.held, self.small = kinds, {}, {}, None
        self.plan = Schedule(kinds, back_moves_of, ready, SMALL_MOVES, SCATTER_RANKS)
        self.left = list(self.plan.order)

    def kept(self, name, part, half):
        key = (name, part, half)
        if key not in self.held:
            got = self.plan.got[name, part, "last", half]
            self.held[key] = add(self.terms[name, part][half], got).astype(jnp.bfloat16)
        return self.held[key]

    def pair(self, name, part, turn):
        rows = self.kept(name, part, turn // 2)
        height = rows.shape[0] // 2
        return rows[(turn % 2) * height :][:height]

    def crossed(self, name, part, turn):
        half = turn // 2
        key = (name, part, "crossed", half)
        if key not in self.held:
            own = self.kept(name, part, half)
            got = self.plan.got[name, part, "first", half]
            self.held[key] = add(own[: own.shape[0] // 2], got).astype(jnp.bfloat16)
        height = self.held[key].shape[0] // 2
        return self.held[key][(turn % 2) * height :][:height]

    def both(self, name, turn):
        return joined_lanes([self.crossed(name, part, turn) for part in "ab"])

    def advance(self, time):
        got = self.plan.got
        while self.left and self.plan.starts[self.left[0]] < time:
            move = self.left.pop(0)
            name, way = move[0], self.plan.moves[move][0]
            if name == "small":
                small = self.small.astype(jnp.bfloat16)
                self.small = add(small, self.plan.send(move, small, move[1]))
                continue
            kind = self.kinds[name]
            if "last" in move:
                value = self.terms[name, move[1]][2 + move[3]]
            elif "z" in move:
                turn = move[-1]
                value = self.pair(name, move[1], turn) if kind == "P" else self.both(name, turn)
                if turn > 1:
                    value = add(value, got[move[:-1] + (turn - 1,)]).astype(jnp.bfloat16)
            elif kind == "P":
                part = move[1]
                total = add(self.pair(name, part, 0), got[name, part, "z", 3])
                self.held[name, part, "own"] = total[: total.shape[0] // 2]
                value = total[total.shape[0] // 2 :].astype(jnp.bfloat16)
            else:
                own = self.kept(name, move[1], move[3])
                value = own[own.shape[0] // 2 :]
            self.plan.send(move, value, way)

    def sums(self):
        got = self.plan.got
        sums = {}
        for name, kind in self.kinds.items():
            if kind == "P":
                sums[name] = joined_lanes(
                    [add(self.held[name, part, "own"], got[name, part, "first"]) for part in "ab"]
                )
            else:
                sums[name] = add(self.both(name, 0), got[name, "z", 3])
        return sums, self.small


def moved_blocks(buffers, old, new, count):
    rows, width = buffers[0].shape
    height = rows * len(buffers) // len(old)
    per_source, per_target = len(old) // len(buffers), len(new) // count

    def kernel(*refs):
        sources, targets = refs[: len(buffers)], refs[len(buffers) :]
        for spot, block in enumerate(new):
            place = old.index(block)
            source, target = sources[place // per_source], targets[spot // per_target]
            first, place = spot % per_target * height, place % per_source * height
            target[first : first + height] = source[place : place + height]

    vmem = pl.BlockSpec(memory_space=pltpu.VMEM)
    return pl.pallas_call(
        kernel,
        out_shape=[jax.ShapeDtypeStruct((height * per_target, width), buffers[0].dtype)] * count,
        in_specs=[vmem] * len(buffers),
        out_specs=[vmem] * count,
        compiler_params=pltpu.CompilerParams(vmem_limit_bytes=24 * 1024 * 1024),
    )(*buffers)


def pair_sum(partial_value):
    return partial_value + swap(partial_value)


def pair_grad_sum(partial_value):
    low = partial_value.astype(jnp.bfloat16)
    return add(low, swap(low))


def permute_kernel(order_ref, own_ref, other_ref, a_ref, b_ref, a_t_ref, b_t_ref, both_ref):
    half = own_ref.shape[1]
    both_ref[:, :half] = own_ref[...]
    both_ref[:, half:] = other_ref[...]
    for block in range(2 * half // LANES):
        target = slice(block * LANES, block * LANES + LANES)
        for row, out_ref in enumerate((a_ref, b_ref, a_t_ref, b_t_ref)):
            offset = pl.multiple_of(order_ref[row, block] * LANES, LANES)
            taken = both_ref[:, pl.ds(offset, LANES)]
            if row < 2:
                out_ref[:, target] = taken
            else:
                out_ref[target, :] = taken.astype(jnp.float32).T.astype(taken.dtype)


def permute_channels(orders, own, other):
    words, channels = own.shape[0], 2 * own.shape[1]
    vmem = pl.BlockSpec(memory_space=pltpu.VMEM)
    return pl.pallas_call(
        permute_kernel,
        out_shape=[jax.ShapeDtypeStruct((words, channels), own.dtype)] * 2
        + [jax.ShapeDtypeStruct((channels, words), own.dtype)] * 2,
        in_specs=[pl.BlockSpec(memory_space=pltpu.SMEM), vmem, vmem],
        out_specs=[vmem] * 4,
        scratch_shapes=[pltpu.VMEM((words, channels), own.dtype)],
        compiler_params=pltpu.CompilerParams(vmem_limit_bytes=24 * 1024 * 1024),
    )(orders, own, other)


def normal_share(values):
    return 0.5 * (1.0 + lax.erf(values * 0.5**0.5))


def load_all(sources, targets, sems):
    return [
        pltpu.make_async_copy(source, targets.at[place], sems.at[place])
        for place, source in enumerate(sources)
    ]


ROWS = 32


def mix_kernel(count, a_ref, b_ref, own_ref, bias_ref, *refs):
    sources = refs[: 2 * count]
    change_ref, gate_ref, next_ref, held, sems = refs[2 * count :]
    copies = load_all(sources, held, sems)
    for copy in copies:
        copy.start()
    width = a_ref.shape[1] // count
    for part, (values_ref, out_ref) in enumerate(((a_ref, change_ref), (b_ref, gate_ref))):
        for place in range(count):
            copies[part * count + place].wait()
            product = jnp.dot(
                values_ref[:, place * width : (place + 1) * width],
                held[part * count + place],
                preferred_element_type=jnp.float32,
            )
            if place:
                out_ref[...] += product
            else:
                out_ref[...] = product + bias_ref[part : part + 1, :]

    def rows_of(step, _):
        rows = pl.ds(pl.multiple_of(step * ROWS, ROWS), ROWS)
        change, gate = change_ref[rows, :], jax.nn.sigmoid(gate_ref[rows, :])
        carried = own_ref[rows, :].astype(jnp.float32)
        mixed = gate * carried + (1.0 - gate) * (change * normal_share(change))
        next_ref[rows, :] = mixed.astype(next_ref.dtype)
        return 0

    lax.fori_loop(0, a_ref.shape[0] // ROWS, rows_of, 0)


def mix_layer(values, own, bias, pieces):
    words, channels = own.shape
    count = len(pieces) // 2
    vmem, anywhere = [pl.BlockSpec(memory_space=space) for space in (pltpu.VMEM, pl.ANY)]
    full = jax.ShapeDtypeStruct((words, channels), jnp.float32)
    return pl.pallas_call(
        partial(mix_kernel, count),
        out_shape=[full, full, jax.ShapeDtypeStruct((words, channels), own.dtype)],
        in_specs=[vmem] * 4 + [anywhere] * len(pieces),
        out_specs=[vmem] * 3,
        scratch_shapes=[
            pltpu.VMEM((len(pieces),) + pieces[0].shape, own.dtype),
            pltpu.SemaphoreType.DMA((len(pieces),)),
        ],
        compiler_params=pltpu.CompilerParams(vmem_limit_bytes=40 * 1024 * 1024),
        cost_estimate=pl.CostEstimate(
            flops=4_300_000_000, bytes_accessed=16_000_000, transcendentals=1_000_000
        ),
    )(*values, own, bias, *pieces)


def mix_back_kernel(count, order_ref, grad_ref, change_ref, gate_ref, carried_ref, *refs):
    sources = refs[: 2 * count]
    (
        grad_change_ref, grad_gate_ref, grad_carried_ref, bias_ref, own_ref, other_ref,
        total_ref, held, sems,
    ) = refs[2 * count :]
    copies = load_all(sources, held, sems)
    for copy in copies:
        copy.start()
    words, channels = grad_ref.shape
    bias_ref[...] = jnp.zeros(bias_ref.shape, jnp.float32)

    def rows_of(step, _):
        rows = pl.ds(pl.multiple_of(step * ROWS, ROWS), ROWS)
        grad, change = grad_ref[rows, :], change_ref[rows, :]
        gate = jax.nn.sigmoid(gate_ref[rows, :])
        share = normal_share(change)
        slope = share + change * jnp.exp(change * change * -0.5) * (0.5 / math.pi) ** 0.5
        rest = grad * (1.0 - gate)
        grad_change = (rest * slope).astype(jnp.bfloat16)
        grad_gate = rest * gate * (carried_ref[rows, :].astype(jnp.float32) - change * share)
        grad_gate = grad_gate.astype(jnp.bfloat16)
        grad_change_ref[rows, :] = grad_change
        grad_gate_ref[rows, :] = grad_gate
        grad_carried_ref[rows, :] = grad * gate
        for part, piece in enumerate((grad_change, grad_gate)):
            bias_ref[part : part + 1, :] += jnp.sum(
                piece.astype(jnp.float32), axis=0, keepdims=True
            )
        return 0

    lax.fori_loop(0, words // ROWS, rows_of, 0)
    blocks = 2 * channels // LANES // count
    for part, values_ref in enumerate((grad_change_ref, grad_gate_ref)):
        for place in range(count):
            copies[part * count + place].wait()
            product = lax.dot_general(
                values_ref[...],
                held[part * count + place],
                (((1,), (1,)), ((), ())),
                preferred_element_type=jnp.float32,
            )
            for block in range(blocks):
                source = order_ref[part, place * blocks + block]
                lanes = pl.ds(pl.multiple_of(source * LANES, LANES), LANES)
                piece = product[:, block * LANES : (block + 1) * LANES]
                if part:
                    total_ref[:, lanes] += piece
                else:
                    total_ref[:, lanes] = piece
    own_ref[...] = total_ref[:, :channels] + grad_carried_ref[...]
    other_ref[...] = total_ref[:, channels:].astype(other_ref.dtype)


def mix_layer_back(order, grad, change, gate, carried, pieces):
    words, channels = grad.shape
    count = len(pieces) // 2
    vmem, anywhere = [pl.BlockSpec(memory_space=space) for space in (pltpu.VMEM, pl.ANY)]
    low = jax.ShapeDtypeStruct((words, channels), jnp.bfloat16)
    full = jax.ShapeDtypeStruct((words, channels), jnp.float32)
    results = pl.pallas_call(
        partial(mix_back_kernel, count),
        out_shape=[low, low, full, jax.ShapeDtypeStruct((2, channels), jnp.float32), full, low],
        in_specs=[pl.BlockSpec(memory_space=pltpu.SMEM)] + [vmem] * 4 + [anywhere] * len(pieces),
        out_specs=[vmem] * 6,
        scratch_shapes=[
            pltpu.VMEM((words, 2 * channels), jnp.float32),
            pltpu.VMEM((len(pieces),) + pieces[0].shape, jnp.bfloat16),
            pltpu.SemaphoreType.DMA((len(pieces),)),
        ],
        compiler_params=pltpu.CompilerParams(vmem_limit_bytes=40 * 1024 * 1024),
        cost_estimate=pl.CostEstimate(
            flops=4_300_000_000, bytes_accessed=16_000_000, transcendentals=1_000_000
        ),
    )(order, grad, change, gate, carried, *pieces)
    return results[:2], results[3], results[4], results[5]


def outer_kernel(count, a_t_ref, b_t_ref, grad_a_ref, grad_b_ref, *refs):
    out_refs, (held, sems) = refs[: 2 * count], refs[2 * count :]
    height = a_t_ref.shape[0] // count
    copies = []
    for part, (rows_ref, grad_ref) in enumerate(((a_t_ref, grad_a_ref), (b_t_ref, grad_b_ref))):
        for place in range(count):
            spot = part * count + place
            held[spot] = jnp.dot(
                rows_ref[place * height : (place + 1) * height, :],
                grad_ref[...],
                preferred_element_type=jnp.float32,
            ).astype(held.dtype)
            copies.append(pltpu.make_async_copy(held.at[spot], out_refs[spot], sems.at[spot]))
            copies[-1].start()
    for copy in copies:
        copy.wait()


def outer_products(rows, grads, count):
    channels, width = rows[0].shape[0], grads[0].shape[1]
    shape = (channels // count, width)
    vmem, anywhere = [pl.BlockSpec(memory_space=space) for space in (pltpu.VMEM, pl.ANY)]
    results = pl.pallas_call(
        partial(outer_kernel, count),
        out_shape=[jax.ShapeDtypeStruct(shape, jnp.bfloat16)] * (2 * count),
        in_specs=[vmem] * 4,
        out_specs=[anywhere] * (2 * count),
        scratch_shapes=[
            pltpu.VMEM((2 * count,) + shape, jnp.bfloat16),
            pltpu.SemaphoreType.DMA((2 * count,)),
        ],
        compiler_params=pltpu.CompilerParams(vmem_limit_bytes=32 * 1024 * 1024),
        cost_estimate=pl.CostEstimate(
            flops=4_300_000_000, bytes_accessed=11_000_000, transcendentals=0
        ),
    )(*rows, *grads)
    return results[:count], results[count:]


SLACK = 4.0
GATHER_KINDS = {"highway0": "Q", "highway1": "P", "encoder": "P"}
GATHER_RANKS = {"highway0": -8.0, ("encoder", "b"): 6.0}
SCATTER_KINDS = {"encoder": "P", "highway1": "Q", "highway0": "Q"}
READY = {
    ("encoder", "b"): 0.0,
    ("encoder", "a"): 5.0,
    "highway1": 9.0,
    "highway0": 13.0,
    "small": 30.0,
}
SCATTER_RANKS = {"encoder": -20.0, "highway1": -10.0}
BACK_TIMES = (9.0, 4.9)
POOL_TIMES = (4.0, 6.0, 8.0, 10.0, 12.0, 14.0)
POOL_BACK_TIMES = (15.0, 17.5, 20.0, 22.5, 25.0, 27.0)
POOL_CUTS = (0, 1, 2, 3, 5, 8)


def packed(values):
    width = 1024
    flat = [value.reshape(-1) for value in values]
    flat = [jnp.pad(value, (0, -value.shape[0] % width)).reshape(-1, width) for value in flat]
    rows = jnp.concatenate(flat, axis=0)
    return jnp.pad(rows, ((0, -rows.shape[0] % 16), (0, 0)))


def unpacked(rows, values):
    totals = []
    first = 0
    for value in values:
        count = -(-value.size // rows.shape[1])
        taken = rows[first : first + count].reshape(-1)
        totals.append(taken[: value.size].reshape(value.shape))
        first += count
    return totals


def per_device(
    char_ids,
    char_mask,
    word_lengths,
    char_table,
    conv_weight,
    conv_bias,
    highway_weight,
    highway_bias,
    proj_weight,
    qkv_weight,
    qv_bias,
    out_weight,
    up_weight,
    up_bias,
    down_weight,
    vector_biases,
    norm_gains,
    cotangent,
):
    f32 = jnp.float32
    bf16 = jnp.bfloat16
    own_filters = conv_weight.shape[1]
    widths = channel_widths(lax.axis_index("narrow") * own_filters, own_filters)
    tap_rows = jnp.arange(TAPS * CHAR_DIM, dtype=jnp.int32) // CHAR_DIM
    tap_mask = (tap_rows[:, None] < widths[None, :]).astype(bf16)
    tap_pad = ((0, LANES - TAPS * CHAR_DIM), (0, 0))
    masked_filters = jnp.pad(conv_weight * tap_mask, tap_pad)
    chan_scale = jnp.sqrt(TAPS / widths.astype(f32))
    word_count = char_ids.shape[0]
    seq_count = word_count // LENGTH
    places = jnp.arange(CHARS_MAX, dtype=jnp.int32)
    alive = (char_mask > 0) & (places[None, :] < word_lengths[:, None])
    picks = word_order(word_lengths)
    picks_low = picks.astype(bf16)
    told = jnp.concatenate(
        [jnp.where(alive, char_ids, -1), word_lengths[:, None]], axis=1
    ).astype(f32)
    told = jnp.dot(picks, told, precision=lax.Precision.HIGHEST)
    lens = told[:, CHARS_MAX:]
    tile_count = word_count // TILE
    longest = jnp.max(lens.astype(jnp.int32).reshape(tile_count, TILE), axis=1)
    tile_chunks = (longest + CHUNK - 1) // CHUNK
    spread_ids = jnp.pad(
        told[:, :CHARS_MAX].astype(jnp.int32),
        ((0, 0), (0, SLOTS - CHARS_MAX)),
        constant_values=-1,
    )
    spread_ids = spread_ids.reshape(tile_count, TILE, SLOTS // CHUNK, CHUNK)
    spread_ids = spread_ids.transpose(0, 2, 3, 1).reshape(-1, CHUNK * TILE)
    table_t = jnp.pad(
        jnp.tile(char_table.T, (TAPS, 1)), (tap_pad[0], (0, IDS - CHAR_VOCAB))
    )
    tap_lanes = (
        jnp.arange(LANES, dtype=jnp.int32)[None, :] // CHAR_DIM
        == jnp.arange(8, dtype=jnp.int32)[:, None]
    ).astype(f32)
    scale_row, bias_row = chan_scale[None, :], conv_bias[None, :]
    width_row = widths.astype(f32)[None, :]
    here = lax.axis_index("wide")
    core = lax.axis_index("narrow")
    routed = lax.axis_size("wide") == CHIPS
    width_proj, width_qkv, width_out = own_filters, 3 * qkv_weight.shape[2], out_weight.shape[0]
    width_up, width_down = up_weight.shape[1], down_weight.shape[0]
    feature_rows = qkv_weight.shape[0]
    first_rows = jnp.concatenate(
        [proj_weight.T, qkv_weight.reshape(feature_rows, width_qkv), out_weight.T], axis=1
    )
    second_rows = jnp.concatenate([up_weight, down_weight.T], axis=1)

    def whole_rows(shard):
        return lax.all_gather(shard, "wide", axis=0, tiled=True)

    def own_rows(terms):
        return lax.psum_scatter(terms.astype(f32), "wide", scatter_dimension=0, tiled=True)

    if routed:
        full, gather_plan = gather_matrices(
            {
                "highway0": [highway_weight[0, :, part] for part in range(2)],
                "highway1": [highway_weight[1, :, part] for part in range(2)],
                "encoder": [first_rows, second_rows],
            },
            GATHER_KINDS,
        )
        highway_full = [
            [full[f"highway{layer}", part] for part in "ab"] for layer in range(HW_LAYERS)
        ]
        gathered_blocks = {part: blocks_of(GATHER_KINDS["encoder"], part) for part in "ab"}
        scattered_blocks = {part: blocks_of(SCATTER_KINDS["encoder"], part) for part in "ab"}
        features = gathered_blocks["a"]
        first_full, second_full = [
            moved_blocks(
                [gather_plan.after_all(full["encoder", part][0], "encoder", part)]
                + full["encoder", part][1:],
                gathered_blocks[part],
                features,
                1,
            )[0]
            for part in "ab"
        ]
        feature_order = owners(features, here)
    else:
        highway_full = [
            [[whole_rows(highway_weight[layer, :, part])] for part in range(2)]
            for layer in range(HW_LAYERS)
        ]
        first_full, second_full = whole_rows(first_rows), whole_rows(second_rows)
        feature_order = jnp.arange(lax.axis_size("wide"), dtype=jnp.int32)
    cuts = [cut * tile_count // 16 for cut in POOL_CUTS] + [tile_count]
    pool_pieces = []
    for first, last, time in zip(cuts, cuts[1:], POOL_TIMES):
        rows = slice(first * TILE, last * TILE)
        id_rows = slice(first * (SLOTS // CHUNK), last * (SLOTS // CHUNK))
        chunks = tile_chunks[first:last]
        if routed:
            chunks = gather_plan.after(chunks, time)
        pool, pool_back = conv_calls((last - first) * TILE, own_filters)
        results = pool(
            chunks, spread_ids[id_rows], table_t, tap_lanes, masked_filters, scale_row, bias_row,
            lens[rows], width_row,
        )
        pool_pieces.append((rows, id_rows, first, last, pool_back, results))
    pooled = joined([results[1] for *_, results in pool_pieces])
    current = gelu_exact(pooled).astype(bf16)
    proj_t, qkv_full, out_t = jnp.split(
        first_full, [width_proj, width_proj + width_qkv], axis=1
    )
    up_full, down_t = jnp.split(second_full, [width_up], axis=1)
    feature_count = proj_t.shape[0]
    feature_picks = (
        feature_order[:, None] == jnp.arange(feature_order.shape[0], dtype=jnp.int32)[None, :]
    ).astype(f32)
    feature_places = (
        feature_order[:, None] * feature_rows + jnp.arange(feature_rows, dtype=jnp.int32)[None, :]
    ).reshape(-1)
    feature_moves = (
        feature_places[:, None] == jnp.arange(feature_count, dtype=jnp.int32)[None, :]
    ).astype(bf16)

    def pick_features(rows, picks):
        blocked = rows.reshape(rows.shape[0], -1, feature_rows)
        return jnp.einsum(
            "kwr,bw->kbr", blocked, picks, precision=lax.Precision.HIGHEST
        ).reshape(rows.shape)

    vector_biases = pick_features(vector_biases, feature_picks)
    norm_gains = pick_features(norm_gains, feature_picks)
    grad_output = jnp.dot(cotangent, feature_moves.T, preferred_element_type=f32).astype(bf16)
    grad_output = jnp.dot(picks_low, grad_output, preferred_element_type=f32)
    kept_layers = []
    block_count = 2 * own_filters // LANES
    for layer_index in range(HW_LAYERS):
        name = f"highway{layer_index}"
        orders = [jnp.arange(block_count, dtype=jnp.int32)] * 4
        if routed:
            orders = [
                owners(blocks_of(kinds[name], part), here)
                for kinds in (GATHER_KINDS, SCATTER_KINDS)
                for part in "ab"
            ]
        order = (jnp.stack(orders) - core * (block_count // 2)) % block_count
        *whole_input, rows_a, rows_b = permute_channels(order, current, swap(current))
        if routed:
            whole_input[0] = gather_plan.after_all(whole_input[0], name)
        pieces = highway_full[layer_index][0] + highway_full[layer_index][1]
        change, gate, mixed = mix_layer(whole_input, current, highway_bias[layer_index], pieces)
        kept_layers.append((order[:2], change, gate, current, pieces, (rows_a, rows_b)))
        current = mixed
    start_rows = (
        pair_sum(jnp.dot(current, proj_t.T, preferred_element_type=f32)) + vector_biases[0]
    )
    start_low = start_rows.astype(bf16)
    qkv_bias = jnp.concatenate([qv_bias[0], jnp.zeros_like(qv_bias[0]), qv_bias[1]])
    projected = (
        jnp.dot(start_low, qkv_full, preferred_element_type=f32) + qkv_bias
    ).astype(bf16)
    head_shape = (word_count, -1, HEAD_DIM)
    query, keys_here, values_here = [
        part.reshape(head_shape) for part in jnp.split(projected, 3, axis=1)
    ]
    attn_scale = HEAD_DIM ** (-0.5)
    sequence = jnp.arange(word_count, dtype=jnp.int32) // 8 % seq_count
    together = (sequence[:, None] == sequence[None, :])[None]
    scores = jnp.einsum("qhe,khe->hqk", query, keys_here, preferred_element_type=f32) * attn_scale
    scores = jnp.where(together, scores, -1e30)
    weights = jnp.exp(scores - jnp.max(scores, axis=-1, keepdims=True))
    probs = weights / jnp.sum(weights, axis=-1, keepdims=True)
    probs_low = probs.astype(bf16)
    context = (
        jnp.einsum("hqk,khe->qhe", probs_low, values_here, preferred_element_type=f32)
        .reshape(word_count, -1)
        .astype(bf16)
    )
    attended = pair_sum(jnp.dot(context, out_t.T, preferred_element_type=f32)) + vector_biases[1]
    before_one = start_rows + attended
    normed_one = layer_norm(before_one, norm_gains[0], vector_biases[3])
    normed_low = normed_one.astype(bf16)
    hidden_pre = jnp.dot(normed_low, up_full, preferred_element_type=f32) + up_bias
    hidden_low = gelu_exact(hidden_pre).astype(bf16)
    lowered = (
        pair_sum(jnp.dot(hidden_low, down_t.T, preferred_element_type=f32)) + vector_biases[2]
    )
    before_two = normed_one + lowered
    encoded = layer_norm(before_two, norm_gains[1], vector_biases[4]).astype(bf16)
    encoded = jnp.dot(encoded, feature_moves, preferred_element_type=f32).astype(bf16)
    encoded = jnp.dot(picks_low.T, encoded, preferred_element_type=f32).astype(bf16)
    if routed:
        scatter = Scatter(SCATTER_KINDS, READY)
    ln_two_back = jax.vjp(layer_norm, before_two, norm_gains[1], vector_biases[4])[1]
    grad_before_two, gain_two, bias_two = ln_two_back(grad_output)
    grad_lowered = grad_before_two.astype(bf16)
    down_grad_local = jnp.dot(grad_lowered.T, hidden_low, preferred_element_type=f32)
    bias_down = jnp.sum(grad_lowered.astype(f32), axis=0)
    grad_hidden = jnp.dot(grad_lowered, down_t, preferred_element_type=f32)
    grad_hidden_pre = jax.vjp(gelu_exact, hidden_pre)[1](grad_hidden)[0].astype(bf16)
    up_grad_local = jnp.dot(normed_low.T, grad_hidden_pre, preferred_element_type=f32)
    bias_up = jnp.sum(grad_hidden_pre.astype(f32), axis=0)
    grad_normed_one = grad_before_two + pair_grad_sum(
        jnp.dot(grad_hidden_pre, up_full.T, preferred_element_type=f32)
    )
    ln_one_back = jax.vjp(layer_norm, before_one, norm_gains[0], vector_biases[3])[1]
    grad_before_one, gain_one, bias_one = ln_one_back(grad_normed_one)
    grad_attended = grad_before_one.astype(bf16)
    out_grad_local = jnp.dot(grad_attended.T, context, preferred_element_type=f32)
    bias_attended = jnp.sum(grad_attended.astype(f32), axis=0)
    grad_context = (
        jnp.dot(grad_attended, out_t, preferred_element_type=f32)
        .astype(bf16)
        .reshape(head_shape)
    )
    grad_probs = jnp.einsum(
        "qhe,khe->hqk", grad_context, values_here, preferred_element_type=f32
    )
    grad_value = jnp.einsum("hqk,qhe->khe", probs_low, grad_context, preferred_element_type=f32)
    grad_scores = (
        probs * (grad_probs - jnp.sum(probs * grad_probs, axis=-1, keepdims=True))
    ).astype(bf16)
    grad_query = (
        jnp.einsum("hqk,khe->qhe", grad_scores, keys_here, preferred_element_type=f32) * attn_scale
    )
    grad_key = (
        jnp.einsum("hqk,qhe->khe", grad_scores, query, preferred_element_type=f32) * attn_scale
    )
    grad_projected = jnp.concatenate(
        [grad.reshape(word_count, -1).astype(bf16) for grad in (grad_query, grad_key, grad_value)],
        axis=1,
    )
    qkv_grad_local = jnp.dot(start_low.T, grad_projected, preferred_element_type=f32)
    bias_qkv = jnp.sum(grad_projected.astype(f32), axis=0).reshape(3, -1)
    bias_qv = bias_qkv[0::2]
    grad_start = grad_before_one + pair_grad_sum(
        jnp.dot(grad_projected, qkv_full.T, preferred_element_type=f32)
    )
    grad_start_low = grad_start.astype(bf16)
    proj_grad_local = jnp.dot(grad_start_low.T, current, preferred_element_type=f32)
    bias_start = jnp.sum(grad_start_low.astype(f32), axis=0)
    grad_current = jnp.dot(grad_start_low, proj_t, preferred_element_type=f32)
    first_grad_local = jnp.concatenate(
        [proj_grad_local, qkv_grad_local, out_grad_local], axis=1
    ).astype(bf16)
    second_grad_local = jnp.concatenate([up_grad_local, down_grad_local], axis=1).astype(bf16)
    if routed:
        for part, local in (("a", first_grad_local), ("b", second_grad_local)):
            scatter.terms["encoder", part] = moved_blocks([local], features, scattered_blocks[part], 4)
    highway_grads = []
    highway_bias_grads = []
    for layer_index in reversed(range(HW_LAYERS)):
        order, change, gate, carried, pieces, rows = kept_layers[layer_index]
        if routed:
            scatter.advance(READY[f"highway{layer_index}"])
            grad_current = scatter.plan.after(grad_current, BACK_TIMES[layer_index])
        part_grads, bias_sums, grad_own, grad_other = mix_layer_back(
            order, grad_current, change, gate, carried, pieces
        )
        terms = outer_products(rows, part_grads, len(pieces) // 2)
        if routed:
            scatter.terms.update(zip([(f"highway{layer_index}", part) for part in "ab"], terms))
        else:
            highway_grads.insert(0, jnp.stack([own_rows(joined(part)) for part in terms], axis=1))
        highway_bias_grads.insert(0, bias_sums)
        grad_current = add(grad_own, swap(grad_other))
    highway_bias_local = jnp.stack(highway_bias_grads)
    grad_pooled = jax.vjp(gelu_exact, pooled)[1](grad_current)[0]
    grad_filter = jnp.zeros((LANES, own_filters), f32)
    grad_marks = jnp.zeros((IDS, 2 * LANES), f32)
    for (rows, id_rows, first, last, pool_back, results), time in zip(pool_pieces, POOL_BACK_TIMES):
        chunks = tile_chunks[first:last]
        if routed:
            scatter.advance(time)
            chunks = scatter.plan.after(chunks, time - 1.0)
        grad_filter, grad_marks = pool_back(
            chunks, spread_ids[id_rows], tap_lanes, masked_filters, scale_row, lens[rows], width_row,
            results[0], results[2], grad_pooled[rows], grad_filter, grad_marks,
        )
    grad_filter = grad_filter[: TAPS * CHAR_DIM]
    grad_conv_bias = jnp.sum(grad_pooled, axis=0)
    grad_marks = grad_marks[:CHAR_VOCAB, :LANES] + grad_marks[:CHAR_VOCAB, LANES:]
    grad_chars = jnp.sum(
        grad_marks[:, : TAPS * CHAR_DIM].reshape(CHAR_VOCAB, TAPS, CHAR_DIM), axis=1
    )
    grad_filter = grad_filter * tap_mask.astype(f32)
    bias_local = pick_features(
        jnp.stack([bias_start, bias_attended, bias_down, bias_one, bias_two]), feature_picks.T
    )
    gain_local = pick_features(jnp.stack([gain_one, gain_two]), feature_picks.T)
    locals_small = (
        grad_filter,
        grad_conv_bias,
        highway_bias_local,
        bias_qv,
        bias_up,
        bias_local,
        gain_local,
        pair_sum(grad_chars),
    )
    if routed:
        scatter.small = packed(locals_small)
        scatter.advance(float("inf"))
        sums, small = scatter.sums()
        small_sums = unpacked(small, locals_small)
        highway_grads = [
            sums[f"highway{layer}"].reshape(highway_weight.shape[1:]) for layer in range(HW_LAYERS)
        ]
        first_grad, second_grad = jnp.split(sums["encoder"], [first_rows.shape[1]], axis=1)
    else:
        first_grad, second_grad = own_rows(first_grad_local), own_rows(second_grad_local)
        small_sums = lax.psum(locals_small, "wide")
    highway_grad = jnp.stack(highway_grads)
    proj_grad, qkv_grad, out_grad = jnp.split(
        first_grad, [width_proj, width_proj + width_qkv], axis=1
    )
    up_grad, down_grad = jnp.split(second_grad, [width_up], axis=1)
    proj_grad, out_grad, down_grad = proj_grad.T, out_grad.T, down_grad.T
    qkv_grad = qkv_grad.reshape(qkv_weight.shape)
    (
        conv_grad,
        conv_bias_grad,
        highway_bias_grad,
        qv_bias_grad,
        up_bias_grad,
        bias_grads,
        gain_grads,
        char_grad,
    ) = small_sums
    return (
        encoded,
        char_grad,
        conv_grad,
        conv_bias_grad,
        highway_grad,
        highway_bias_grad,
        proj_grad,
        qkv_grad,
        qv_bias_grad,
        out_grad,
        up_grad,
        up_bias_grad,
        down_grad,
        bias_grads,
        gain_grads,
    )


def solution(mesh):
    placed = (
        P("wide", None),
        P("wide", None),
        P("wide"),
        P(),
        P(None, "narrow"),
        P("narrow"),
        P(None, "wide", None, "narrow"),
        P(None, None, "narrow"),
        P("narrow", "wide"),
        P("wide", None, "narrow"),
        P(None, "narrow"),
        P("narrow", "wide"),
        P("wide", "narrow"),
        P("narrow"),
        P("narrow", "wide"),
        P(),
        P(),
        P("wide", None),
    )
    return jax.shard_map(
        per_device,
        mesh=mesh,
        in_specs=placed,
        out_specs=(
            P("wide", None),
            P(),
            P(None, "narrow"),
            P("narrow"),
            P(None, "wide", None, "narrow"),
            P(None, None, "narrow"),
            P("narrow", "wide"),
            P("wide", None, "narrow"),
            P(None, "narrow"),
            P("narrow", "wide"),
            P("wide", "narrow"),
            P("narrow"),
            P("narrow", "wide"),
            P(),
            P(),
        ),
        check_vma=False,
    )
```

```python
import math
from functools import partial

import jax
import jax.numpy as jnp
from jax import lax
from jax.experimental import pallas as pl
from jax.experimental.pallas import tpu as pltpu
from jax.sharding import PartitionSpec as P

HEAD_DIM = 64
FILTERS = 2048
CHAR_DIM = 16
CHAR_VOCAB = 262
CHARS_MAX = 50
TAPS = 7
HW_LAYERS = 2
TILE = 16
CHUNK = 8
SLOTS = 64
IDS = 272
LANES = 128
BLOCK = 256
LOG2E = 1.4426950408889634
LENGTH = 128


BOUNDS = ((1, 2), (3, 4), (7, 8), (15, 16), (31, 32), (63, 64))
EPSILON = 1e-06


def channel_widths(first_channel, count):
    channels = first_channel + jnp.arange(count, dtype=jnp.int32)
    widths = jnp.full((count,), TAPS, jnp.int32)
    for numerator, denominator in BOUNDS:
        widths = widths - (channels >= FILTERS * numerator // denominator).astype(jnp.int32)
    return widths


def gelu_exact(values):
    return jax.nn.gelu(values, approximate=False)


def layer_norm(values, gain_row, bias_row):
    center = jnp.mean(values, axis=-1, keepdims=True)
    spread = jnp.mean(jnp.square(values - center), axis=-1, keepdims=True)
    return (values - center) * lax.rsqrt(spread + EPSILON) * gain_row + bias_row


def word_order(lengths):
    words = lengths.shape[0]
    sequences = words // LENGTH
    spots = jnp.arange(words, dtype=jnp.int32)
    keys = lengths * LENGTH + (LENGTH - 1 - spots % LENGTH)
    same = spots[:, None] // LENGTH == spots[None, :] // LENGTH
    ranks = jnp.sum((same & (keys[None, :] > keys[:, None])).astype(jnp.int32), axis=1)
    places = ranks // 8 * (8 * sequences) + spots // LENGTH * 8 + ranks % 8
    return (places[None, :] == spots[:, None]).astype(jnp.float32)


def spot_chars(ids_row, table_t):
    ids = lax.broadcasted_iota(jnp.int32, (IDS, LANES), 0)
    marks = (ids == ids_row).astype(jnp.float32).astype(jnp.bfloat16)
    return jnp.dot(table_t, marks, preferred_element_type=jnp.float32).T.astype(jnp.bfloat16)


def tap_rows(table_ref, start, tile, tap_lanes):
    rows = pl.ds(pl.multiple_of(tile * TILE, TILE), TILE)
    taken = None
    for tap in range(TAPS):
        piece = table_ref[pl.ds(start + tap, CHUNK), rows, :] * tap_lanes[tap][None]
        taken = piece if taken is None else taken + piece
    return taken.reshape(CHUNK * TILE, LANES)


def window_counts(lens_ref, widths_ref, tile):
    rows = pl.ds(pl.multiple_of(tile * TILE, TILE), TILE)
    return jnp.maximum(lens_ref[rows, :1] - widths_ref[...] + 1.0, 1.0)


def pool_kernel(
    tile_ref, ids_ref, table_ref, lanes_ref, filters_ref, scale_ref, bias_ref, lens_ref, widths_ref,
    embed_ref, pooled_ref, shift_ref, conv_ref, count_ref, top_ref,
):
    channels = filters_ref.shape[1]
    chunks_all = SLOTS // CHUNK
    tap_lanes = [lanes_ref[tap : tap + 1, :].astype(jnp.bfloat16) for tap in range(TAPS)]
    blocks = [slice(first, first + BLOCK) for first in range(0, channels, BLOCK)]

    def one_tile(tile, _):
        rows = pl.ds(pl.multiple_of(tile * TILE, TILE), TILE)
        chunks = tile_ref[tile]

        def embed(chunk, _):
            found = spot_chars(ids_ref[pl.ds(tile * chunks_all + chunk, 1), :], table_ref[...])
            embed_ref[pl.ds(chunk * CHUNK, CHUNK), rows, :] = found.reshape(CHUNK, TILE, LANES)
            return 0

        lax.fori_loop(0, chunks, embed, 0)
        embed_ref[pl.ds(chunks * CHUNK, CHUNK), rows, :] = jnp.zeros(
            (CHUNK, TILE, LANES), jnp.bfloat16
        )
        count_ref[...] = window_counts(lens_ref, widths_ref, tile)
        top_ref[...] = jnp.full(top_ref.shape, -1e30, jnp.float32)

        def convolve(chunk, _):
            columns = tap_rows(embed_ref, chunk * CHUNK, tile, tap_lanes)
            first = (chunk * CHUNK).astype(jnp.float32)
            for block in blocks:
                convolved = jnp.dot(
                    columns, filters_ref[:, block], preferred_element_type=jnp.float32
                )
                conv_ref[chunk, :, block] = convolved
                counts = count_ref[:, block] - first
                top = top_ref[:, block]
                for place in range(CHUNK):
                    row = convolved[place * TILE : (place + 1) * TILE]
                    top = jnp.maximum(top, jnp.where(counts > float(place), row, -1e30))
                top_ref[:, block] = top
            return 0

        lax.fori_loop(0, chunks, convolve, 0)
        pooled_ref[rows, :] = jnp.zeros((TILE, channels), jnp.float32)

        def weigh(chunk, _):
            first = (chunk * CHUNK).astype(jnp.float32)
            for block in blocks:
                counts = count_ref[:, block] - first
                scale = scale_ref[:, block] * LOG2E
                offset = top_ref[:, block] * scale
                total = pooled_ref[rows, block]
                for place in range(CHUNK):
                    row = conv_ref[chunk, place * TILE : (place + 1) * TILE, block]
                    weight = jnp.exp2(row * scale - offset)
                    total = total + jnp.where(counts > float(place), weight, 0.0)
                pooled_ref[rows, block] = total
            return 0

        lax.fori_loop(0, chunks, weigh, 0)
        top = top_ref[...] * scale_ref[...]
        log_total = jnp.log(pooled_ref[rows, :])
        pooled_ref[rows, :] = top + bias_ref[...] + log_total - jnp.log(count_ref[...])
        shift_ref[rows, :] = (top + log_total) * -LOG2E
        return 0

    lax.fori_loop(0, tile_ref.shape[0], one_tile, 0)


def pool_back_kernel(
    tile_ref, ids_ref, lanes_ref, filters_ref, scale_ref, lens_ref, widths_ref, embed_ref, shift_ref,
    grad_ref, filter_before_ref, char_before_ref, filter_grad_ref, char_grad_ref, conv_grad_ref,
    column_ref, count_ref,
):
    channels = filters_ref.shape[1]
    chunks_all = SLOTS // CHUNK
    tap_lanes = [lanes_ref[tap : tap + 1, :].astype(jnp.bfloat16) for tap in range(TAPS)]
    lane_taps = lax.broadcasted_iota(jnp.int32, (1, 1, LANES), 2) // CHAR_DIM
    blocks = [slice(first, first + BLOCK) for first in range(0, channels, BLOCK)]
    filter_grad_ref[...] = filter_before_ref[...]
    char_grad_ref[...] = char_before_ref[...]
    column_ref[:CHUNK] = jnp.zeros((CHUNK, TILE, LANES), jnp.float32)

    def one_tile(tile, _):
        rows = pl.ds(pl.multiple_of(tile * TILE, TILE), TILE)
        chunks = tile_ref[tile]
        count_ref[...] = window_counts(lens_ref, widths_ref, tile)

        def one_chunk(chunk, _):
            columns = tap_rows(embed_ref, chunk * CHUNK, tile, tap_lanes)
            columns_t = columns.astype(jnp.float32).T.astype(jnp.bfloat16)
            first = (chunk * CHUNK).astype(jnp.float32)
            grad_columns = None
            for block in blocks:
                filters = filters_ref[:, block]
                convolved = jnp.dot(columns, filters, preferred_element_type=jnp.float32)
                counts = count_ref[:, block] - first
                scale = scale_ref[:, block]
                scale2 = scale * LOG2E
                shift = shift_ref[rows, block]
                grad = grad_ref[rows, block] * scale
                for place in range(CHUNK):
                    row = convolved[place * TILE : (place + 1) * TILE]
                    share = jnp.exp2(row * scale2 + shift)
                    conv_grad_ref[place * TILE : (place + 1) * TILE, block] = jnp.where(
                        counts > float(place), share * grad, 0.0
                    ).astype(jnp.bfloat16)
                conv_grad = conv_grad_ref[:, block]
                filter_grad_ref[:, block] += jnp.dot(
                    columns_t, conv_grad, preferred_element_type=jnp.float32
                )
                piece = lax.dot_general(
                    conv_grad, filters, (((1,), (1,)), ((), ())), preferred_element_type=jnp.float32
                )
                grad_columns = piece if grad_columns is None else grad_columns + piece
            column_ref[pl.ds(chunk * CHUNK + CHUNK, CHUNK)] = grad_columns.reshape(
                CHUNK, TILE, LANES
            )
            return 0

        lax.fori_loop(0, chunks, one_chunk, 0)

        def fold(chunk, _):
            moved = None
            for tap in range(TAPS):
                piece = column_ref[pl.ds(chunk * CHUNK + CHUNK - tap, CHUNK)]
                moved = piece if moved is None else jnp.where(lane_taps == tap, piece, moved)
            moved = moved.reshape(CHUNK * TILE, LANES)
            high = moved.astype(jnp.bfloat16)
            low = (moved - high.astype(jnp.float32)).astype(jnp.bfloat16)
            ids = lax.broadcasted_iota(jnp.int32, (IDS, LANES), 0)
            ids_row = ids_ref[pl.ds(tile * chunks_all + chunk, 1), :]
            marks = (ids == ids_row).astype(jnp.float32).astype(jnp.bfloat16)
            char_grad_ref[...] += jnp.dot(
                marks, jnp.concatenate([high, low], axis=1), preferred_element_type=jnp.float32
            )
            return 0

        lax.fori_loop(0, chunks, fold, 0)
        return 0

    lax.fori_loop(0, tile_ref.shape[0], one_tile, 0)


def conv_calls(words, channels):
    vmem = pl.BlockSpec(memory_space=pltpu.VMEM)
    smem = pl.BlockSpec(memory_space=pltpu.SMEM)
    shape = partial(jax.ShapeDtypeStruct, dtype=jnp.float32)
    params = pltpu.CompilerParams(vmem_limit_bytes=40 * 1024 * 1024)
    pool = pl.pallas_call(
        pool_kernel,
        out_shape=[
            jax.ShapeDtypeStruct((SLOTS, words, LANES), jnp.bfloat16),
            shape((words, channels)),
            shape((words, channels)),
        ],
        in_specs=[smem] + [vmem] * 8,
        out_specs=[vmem] * 3,
        scratch_shapes=[
            pltpu.VMEM((SLOTS // CHUNK, CHUNK * TILE, channels), jnp.float32),
            pltpu.VMEM((TILE, channels), jnp.float32),
            pltpu.VMEM((TILE, channels), jnp.float32),
        ],
        compiler_params=params,
        cost_estimate=pl.CostEstimate(
            flops=2_000_000_000, bytes_accessed=8_000_000, transcendentals=5_000_000
        ),
    )
    back = pl.pallas_call(
        pool_back_kernel,
        out_shape=[shape((LANES, channels)), shape((IDS, 2 * LANES))],
        in_specs=[smem] + [vmem] * 11,
        out_specs=[vmem] * 2,
        scratch_shapes=[
            pltpu.VMEM((CHUNK * TILE, channels), jnp.bfloat16),
            pltpu.VMEM((SLOTS + CHUNK, TILE, LANES), jnp.float32),
            pltpu.VMEM((TILE, channels), jnp.float32),
        ],
        compiler_params=params,
        cost_estimate=pl.CostEstimate(
            flops=4_000_000_000, bytes_accessed=10_000_000, transcendentals=5_000_000
        ),
    )
    return pool, back


STEPS = {
    "x": [(i, i ^ 1) for i in range(16)],
    "y": [(i, i ^ 2) for i in range(16)],
    "z": [(i, (i + 4) % 16) for i in range(16)],
    "near": [(i, i ^ 4) for i in range(16)],
    "far": [(i, i ^ 8) for i in range(16)],
}
CHIPS = 16
SWAP = [(0, 1), (1, 0)]


def step(value, axis):
    return lax.ppermute(value, "wide", STEPS[axis])


def swap(value):
    return lax.ppermute(value, "narrow", SWAP)


def joined(pieces):
    return pieces[0] if len(pieces) == 1 else jnp.concatenate(pieces, axis=0)


def add(one, other):
    return one.astype(jnp.float32) + other.astype(jnp.float32)


FIRST = {"a": "x", "b": "y"}
LAST = {"a": "y", "b": "x"}
TURNS = (1, 2, 3)
SMALL_MOVES = {
    ("small", "x"): ("x", 1, []),
    ("small", "y"): ("y", 1, [("small", "x")]),
    ("small", "near"): ("z", 1, [("small", "y")]),
    ("small", "far"): ("z", 2, [("small", "near")]),
}


def moves_of(kind):
    moves = {}
    if kind == "Q":
        for turn in TURNS:
            moves["z", turn] = ("z", 2, [("z", turn - 1)] if turn > 1 else [])
    for part in "ab":
        if kind == "P":
            moves[part, "first"] = (FIRST[part], 1, [])
            for turn in TURNS:
                before = (part, "z", turn - 1) if turn > 1 else (part, "first")
                moves[part, "z", turn] = ("z", 2, [before])
            for half in (0, 1):
                moves[part, "last", half] = (LAST[part], 4, [(part, "z", 1 + 2 * half)])
        else:
            for half in (0, 1):
                moves[part, "first", half] = (FIRST[part], 2, [("z", 1 + 2 * half)])
                moves[part, "last", half] = (LAST[part], 4, [(part, "first", half)])
    return moves


def back_moves_of(kind):
    moves = {}
    for part in "ab":
        for half in (0, 1):
            moves[part, "last", half] = (LAST[part], 4, [])
        if kind == "P":
            moves[part, "z", 1] = ("z", 2, [(part, "last", 0)])
            moves[part, "z", 2] = ("z", 2, [(part, "z", 1), (part, "last", 1)])
            moves[part, "z", 3] = ("z", 2, [(part, "z", 2)])
            moves[part, "first"] = (FIRST[part], 1, [(part, "z", 3)])
        else:
            for half in (0, 1):
                moves[part, "first", half] = (FIRST[part], 2, [(part, "last", half)])
    if kind == "Q":
        moves["z", 1] = ("z", 2, [("a", "first", 0), ("b", "first", 0)])
        moves["z", 2] = ("z", 2, [("z", 1), ("a", "first", 1), ("b", "first", 1)])
        moves["z", 3] = ("z", 2, [("z", 2)])
    return moves


class Schedule:
    def __init__(self, kinds, moves_of_kind, ready, extra, ranks, lag=0.7):
        moves = dict(extra)
        for name, kind in kinds.items():
            for move, (axis, load, needs) in moves_of_kind(kind).items():
                moves[(name,) + move] = (axis, load, [(name,) + need for need in needs])
        self.moves, self.got, self.sent = moves, {}, {"x": [], "y": [], "z": []}
        self.values = {}
        users = {move: [] for move in moves}
        for move, (_, _, needs) in moves.items():
            for need in needs:
                users[need].append(move)
        tails = {}

        def tail(move):
            if move not in tails:
                tails[move] = moves[move][1] + lag + max(map(tail, users[move]), default=0.0)
            return tails[move]

        places = {move: place for place, move in enumerate(moves)}
        free, waiting = {"x": 0.0, "y": 0.0, "z": 0.0}, dict(moves)
        self.starts, self.ends = {}, {}
        while waiting:
            best = None
            for move, (axis, load, needs) in waiting.items():
                if all(need in self.ends for need in needs):
                    start = max(
                        [ready.get(move[:2], ready.get(move[0], 0.0)), free[axis]]
                        + [self.ends[need] + lag for need in needs]
                    )
                    rank = ranks.get(move[:2], ranks.get(move[0], 0))
                    key = (start, rank - tail(move), places[move])
                    if best is None or key < best[0]:
                        best = (key, start, move)
            _, start, move = best
            axis, load, _ = waiting.pop(move)
            self.starts[move] = start
            self.ends[move] = free[axis] = start + load
        self.order = list(self.starts)

    def after(self, value, time):
        known = []
        for axis in "xyz":
            for times, arrays in ((self.ends, self.got), (self.starts, self.values)):
                past = [m for m in arrays if self.moves[m][0] == axis and times[m] <= time]
                if past:
                    known.append(arrays[max(past, key=times.get)])
        return lax.optimization_barrier((value, *known))[0] if known else value

    def after_all(self, value, *names):
        return self.after(
            value, max(end for move, end in self.ends.items() if move[: len(names)] == names)
        )

    def send(self, move, value, way):
        axis = self.moves[move][0]
        sent = self.sent[axis]
        if len(sent) > 1:
            value = lax.optimization_barrier((value, sent[-2]))[0]
        value = self.after(value, self.starts[move] - SLACK)
        self.values[move] = value
        self.got[move] = step(value, way)
        sent.append(self.got[move])
        return self.got[move]


def blocks_of(kind, part):
    blocks = []
    for last in (0, 1):
        for half in (0, 1):
            turns = (2 * half, 2 * half + 1)
            if kind == "P":
                pairs = [(turn, first) for turn in turns for first in (0, 1)]
            else:
                pairs = [(turn, first) for first in (0, 1) for turn in turns]
            for turn, first in pairs:
                blocks.append((turn, first, last) if part == "b" else (turn, last, first))
    return blocks


def owners(blocks, here):
    z, y, x = here // 4, (here // 2) % 2, here % 2
    return jnp.stack(
        [((z - dz) % 4) * 4 + (y + dy) % 2 * 2 + (x + dx) % 2 for dz, dy, dx in blocks]
    ).astype(jnp.int32)


def gather_matrices(shards, kinds):
    plan = Schedule(kinds, moves_of, {}, {}, GATHER_RANKS)
    got, sent = plan.got, {}
    for move in plan.order:
        name, kind = move[0], kinds[move[0]]
        parts = dict(zip("ab", shards[name]))
        way = plan.moves[move][0]
        if "z" in move:
            turn = move[-1]
            if turn > 1:
                value = got[move[:-1] + (turn - 1,)]
            elif kind == "P":
                part = move[1]
                value = joined([parts[part], got[name, part, "first"]])
                sent[name, part, "pair"] = value
            else:
                value = joined_lanes(shards[name])
        else:
            part, stage = move[1:3]
            turns = (2 * move[3], 2 * move[3] + 1) if len(move) == 4 else ()
            if kind == "P" and stage == "first":
                value = parts[part]
            elif kind == "P":
                value = joined(
                    [got[name, part, "z", turn] if turn else sent[name, part, "pair"] for turn in turns]
                )
            elif stage == "first":
                width = parts["a"].shape[1]
                lanes = slice(0, width) if part == "a" else slice(width, None)
                value = joined(
                    [got[name, "z", turn][:, lanes] if turn else parts[part] for turn in turns]
                )
            else:
                value = joined([sent[name, part, "first", move[3]], got[name, part, "first", move[3]]])
        sent[move] = value
        plan.send(move, value, way)
    full = {
        (name, part): [held[name, part, "last", half] for held in (sent, got) for half in (0, 1)]
        for name in kinds
        for part in "ab"
    }
    return full, plan


def joined_lanes(pieces):
    return jnp.concatenate(pieces, axis=1)


class Scatter:
    def __init__(self, kinds, ready):
        self.kinds, self.terms, self.held, self.small = kinds, {}, {}, None
        self.plan = Schedule(kinds, back_moves_of, ready, SMALL_MOVES, SCATTER_RANKS)
        self.left = list(self.plan.order)

    def kept(self, name, part, half):
        key = (name, part, half)
        if key not in self.held:
            got = self.plan.got[name, part, "last", half]
            self.held[key] = add(self.terms[name, part][half], got).astype(jnp.bfloat16)
        return self.held[key]

    def pair(self, name, part, turn):
        rows = self.kept(name, part, turn // 2)
        height = rows.shape[0] // 2
        return rows[(turn % 2) * height :][:height]

    def crossed(self, name, part, turn):
        half = turn // 2
        key = (name, part, "crossed", half)
        if key not in self.held:
            own = self.kept(name, part, half)
            got = self.plan.got[name, part, "first", half]
            self.held[key] = add(own[: own.shape[0] // 2], got).astype(jnp.bfloat16)
        height = self.held[key].shape[0] // 2
        return self.held[key][(turn % 2) * height :][:height]

    def both(self, name, turn):
        return joined_lanes([self.crossed(name, part, turn) for part in "ab"])

    def advance(self, time):
        got = self.plan.got
        while self.left and self.plan.starts[self.left[0]] < time:
            move = self.left.pop(0)
            name, way = move[0], self.plan.moves[move][0]
            if name == "small":
                small = self.small.astype(jnp.bfloat16)
                self.small = add(small, self.plan.send(move, small, move[1]))
                continue
            kind = self.kinds[name]
            if "last" in move:
                value = self.terms[name, move[1]][2 + move[3]]
            elif "z" in move:
                turn = move[-1]
                value = self.pair(name, move[1], turn) if kind == "P" else self.both(name, turn)
                if turn > 1:
                    value = add(value, got[move[:-1] + (turn - 1,)]).astype(jnp.bfloat16)
            elif kind == "P":
                part = move[1]
                total = add(self.pair(name, part, 0), got[name, part, "z", 3])
                self.held[name, part, "own"] = total[: total.shape[0] // 2]
                value = total[total.shape[0] // 2 :].astype(jnp.bfloat16)
            else:
                own = self.kept(name, move[1], move[3])
                value = own[own.shape[0] // 2 :]
            self.plan.send(move, value, way)

    def sums(self):
        got = self.plan.got
        sums = {}
        for name, kind in self.kinds.items():
            if kind == "P":
                sums[name] = joined_lanes(
                    [add(self.held[name, part, "own"], got[name, part, "first"]) for part in "ab"]
                )
            else:
                sums[name] = add(self.both(name, 0), got[name, "z", 3])
        return sums, self.small


def moved_blocks(buffers, old, new, count):
    rows, width = buffers[0].shape
    height = rows * len(buffers) // len(old)
    per_source, per_target = len(old) // len(buffers), len(new) // count

    def kernel(*refs):
        sources, targets = refs[: len(buffers)], refs[len(buffers) :]
        for spot, block in enumerate(new):
            place = old.index(block)
            source, target = sources[place // per_source], targets[spot // per_target]
            first, place = spot % per_target * height, place % per_source * height
            target[first : first + height] = source[place : place + height]

    vmem = pl.BlockSpec(memory_space=pltpu.VMEM)
    return pl.pallas_call(
        kernel,
        out_shape=[jax.ShapeDtypeStruct((height * per_target, width), buffers[0].dtype)] * count,
        in_specs=[vmem] * len(buffers),
        out_specs=[vmem] * count,
        compiler_params=pltpu.CompilerParams(vmem_limit_bytes=24 * 1024 * 1024),
    )(*buffers)


def pair_sum(partial_value):
    return partial_value + swap(partial_value)


def pair_grad_sum(partial_value):
    low = partial_value.astype(jnp.bfloat16)
    return add(low, swap(low))


def permute_kernel(order_ref, own_ref, other_ref, a_ref, b_ref, a_t_ref, b_t_ref, both_ref):
    half = own_ref.shape[1]
    both_ref[:, :half] = own_ref[...]
    both_ref[:, half:] = other_ref[...]
    for block in range(2 * half // LANES):
        target = slice(block * LANES, block * LANES + LANES)
        for row, out_ref in enumerate((a_ref, b_ref, a_t_ref, b_t_ref)):
            offset = pl.multiple_of(order_ref[row, block] * LANES, LANES)
            taken = both_ref[:, pl.ds(offset, LANES)]
            if row < 2:
                out_ref[:, target] = taken
            else:
                out_ref[target, :] = taken.astype(jnp.float32).T.astype(taken.dtype)


def permute_channels(orders, own, other):
    words, channels = own.shape[0], 2 * own.shape[1]
    vmem = pl.BlockSpec(memory_space=pltpu.VMEM)
    return pl.pallas_call(
        permute_kernel,
        out_shape=[jax.ShapeDtypeStruct((words, channels), own.dtype)] * 2
        + [jax.ShapeDtypeStruct((channels, words), own.dtype)] * 2,
        in_specs=[pl.BlockSpec(memory_space=pltpu.SMEM), vmem, vmem],
        out_specs=[vmem] * 4,
        scratch_shapes=[pltpu.VMEM((words, channels), own.dtype)],
        compiler_params=pltpu.CompilerParams(vmem_limit_bytes=24 * 1024 * 1024),
    )(orders, own, other)


def normal_share(values):
    return 0.5 * (1.0 + lax.erf(values * 0.5**0.5))


def load_all(sources, targets, sems):
    return [
        pltpu.make_async_copy(source, targets.at[place], sems.at[place])
        for place, source in enumerate(sources)
    ]


ROWS = 32


def mix_kernel(count, a_ref, b_ref, own_ref, bias_ref, *refs):
    sources = refs[: 2 * count]
    change_ref, gate_ref, next_ref, held, sems = refs[2 * count :]
    copies = load_all(sources, held, sems)
    for copy in copies:
        copy.start()
    width = a_ref.shape[1] // count
    for part, (values_ref, out_ref) in enumerate(((a_ref, change_ref), (b_ref, gate_ref))):
        for place in range(count):
            copies[part * count + place].wait()
            product = jnp.dot(
                values_ref[:, place * width : (place + 1) * width],
                held[part * count + place],
                preferred_element_type=jnp.float32,
            )
            if place:
                out_ref[...] += product
            else:
                out_ref[...] = product + bias_ref[part : part + 1, :]

    def rows_of(step, _):
        rows = pl.ds(pl.multiple_of(step * ROWS, ROWS), ROWS)
        change, gate = change_ref[rows, :], jax.nn.sigmoid(gate_ref[rows, :])
        carried = own_ref[rows, :].astype(jnp.float32)
        mixed = gate * carried + (1.0 - gate) * (change * normal_share(change))
        next_ref[rows, :] = mixed.astype(next_ref.dtype)
        return 0

    lax.fori_loop(0, a_ref.shape[0] // ROWS, rows_of, 0)


def mix_layer(values, own, bias, pieces):
    words, channels = own.shape
    count = len(pieces) // 2
    vmem, anywhere = [pl.BlockSpec(memory_space=space) for space in (pltpu.VMEM, pl.ANY)]
    full = jax.ShapeDtypeStruct((words, channels), jnp.float32)
    return pl.pallas_call(
        partial(mix_kernel, count),
        out_shape=[full, full, jax.ShapeDtypeStruct((words, channels), own.dtype)],
        in_specs=[vmem] * 4 + [anywhere] * len(pieces),
        out_specs=[vmem] * 3,
        scratch_shapes=[
            pltpu.VMEM((len(pieces),) + pieces[0].shape, own.dtype),
            pltpu.SemaphoreType.DMA((len(pieces),)),
        ],
        compiler_params=pltpu.CompilerParams(vmem_limit_bytes=40 * 1024 * 1024),
        cost_estimate=pl.CostEstimate(
            flops=4_300_000_000, bytes_accessed=16_000_000, transcendentals=1_000_000
        ),
    )(*values, own, bias, *pieces)


def mix_back_kernel(count, order_ref, grad_ref, change_ref, gate_ref, carried_ref, *refs):
    sources = refs[: 2 * count]
    (
        grad_change_ref, grad_gate_ref, grad_carried_ref, bias_ref, own_ref, other_ref,
        total_ref, held, sems,
    ) = refs[2 * count :]
    copies = load_all(sources, held, sems)
    for copy in copies:
        copy.start()
    words, channels = grad_ref.shape
    bias_ref[...] = jnp.zeros(bias_ref.shape, jnp.float32)

    def rows_of(step, _):
        rows = pl.ds(pl.multiple_of(step * ROWS, ROWS), ROWS)
        grad, change = grad_ref[rows, :], change_ref[rows, :]
        gate = jax.nn.sigmoid(gate_ref[rows, :])
        share = normal_share(change)
        slope = share + change * jnp.exp(change * change * -0.5) * (0.5 / math.pi) ** 0.5
        rest = grad * (1.0 - gate)
        grad_change = (rest * slope).astype(jnp.bfloat16)
        grad_gate = rest * gate * (carried_ref[rows, :].astype(jnp.float32) - change * share)
        grad_gate = grad_gate.astype(jnp.bfloat16)
        grad_change_ref[rows, :] = grad_change
        grad_gate_ref[rows, :] = grad_gate
        grad_carried_ref[rows, :] = grad * gate
        for part, piece in enumerate((grad_change, grad_gate)):
            bias_ref[part : part + 1, :] += jnp.sum(
                piece.astype(jnp.float32), axis=0, keepdims=True
            )
        return 0

    lax.fori_loop(0, words // ROWS, rows_of, 0)
    blocks = 2 * channels // LANES // count
    for part, values_ref in enumerate((grad_change_ref, grad_gate_ref)):
        for place in range(count):
            copies[part * count + place].wait()
            product = lax.dot_general(
                values_ref[...],
                held[part * count + place],
                (((1,), (1,)), ((), ())),
                preferred_element_type=jnp.float32,
            )
            for block in range(blocks):
                source = order_ref[part, place * blocks + block]
                lanes = pl.ds(pl.multiple_of(source * LANES, LANES), LANES)
                piece = product[:, block * LANES : (block + 1) * LANES]
                if part:
                    total_ref[:, lanes] += piece
                else:
                    total_ref[:, lanes] = piece
    own_ref[...] = total_ref[:, :channels] + grad_carried_ref[...]
    other_ref[...] = total_ref[:, channels:].astype(other_ref.dtype)


def mix_layer_back(order, grad, change, gate, carried, pieces):
    words, channels = grad.shape
    count = len(pieces) // 2
    vmem, anywhere = [pl.BlockSpec(memory_space=space) for space in (pltpu.VMEM, pl.ANY)]
    low = jax.ShapeDtypeStruct((words, channels), jnp.bfloat16)
    full = jax.ShapeDtypeStruct((words, channels), jnp.float32)
    results = pl.pallas_call(
        partial(mix_back_kernel, count),
        out_shape=[low, low, full, jax.ShapeDtypeStruct((2, channels), jnp.float32), full, low],
        in_specs=[pl.BlockSpec(memory_space=pltpu.SMEM)] + [vmem] * 4 + [anywhere] * len(pieces),
        out_specs=[vmem] * 6,
        scratch_shapes=[
            pltpu.VMEM((words, 2 * channels), jnp.float32),
            pltpu.VMEM((len(pieces),) + pieces[0].shape, jnp.bfloat16),
            pltpu.SemaphoreType.DMA((len(pieces),)),
        ],
        compiler_params=pltpu.CompilerParams(vmem_limit_bytes=40 * 1024 * 1024),
        cost_estimate=pl.CostEstimate(
            flops=4_300_000_000, bytes_accessed=16_000_000, transcendentals=1_000_000
        ),
    )(order, grad, change, gate, carried, *pieces)
    return results[:2], results[3], results[4], results[5]


def outer_kernel(count, a_t_ref, b_t_ref, grad_a_ref, grad_b_ref, *refs):
    out_refs, (held, sems) = refs[: 2 * count], refs[2 * count :]
    height = a_t_ref.shape[0] // count
    copies = []
    for part, (rows_ref, grad_ref) in enumerate(((a_t_ref, grad_a_ref), (b_t_ref, grad_b_ref))):
        for place in range(count):
            spot = part * count + place
            held[spot] = jnp.dot(
                rows_ref[place * height : (place + 1) * height, :],
                grad_ref[...],
                preferred_element_type=jnp.float32,
            ).astype(held.dtype)
            copies.append(pltpu.make_async_copy(held.at[spot], out_refs[spot], sems.at[spot]))
            copies[-1].start()
    for copy in copies:
        copy.wait()


def outer_products(rows, grads, count):
    channels, width = rows[0].shape[0], grads[0].shape[1]
    shape = (channels // count, width)
    vmem, anywhere = [pl.BlockSpec(memory_space=space) for space in (pltpu.VMEM, pl.ANY)]
    results = pl.pallas_call(
        partial(outer_kernel, count),
        out_shape=[jax.ShapeDtypeStruct(shape, jnp.bfloat16)] * (2 * count),
        in_specs=[vmem] * 4,
        out_specs=[anywhere] * (2 * count),
        scratch_shapes=[
            pltpu.VMEM((2 * count,) + shape, jnp.bfloat16),
            pltpu.SemaphoreType.DMA((2 * count,)),
        ],
        compiler_params=pltpu.CompilerParams(vmem_limit_bytes=32 * 1024 * 1024),
        cost_estimate=pl.CostEstimate(
            flops=4_300_000_000, bytes_accessed=11_000_000, transcendentals=0
        ),
    )(*rows, *grads)
    return results[:count], results[count:]


SLACK = 4.0
GATHER_KINDS = {"highway0": "Q", "highway1": "P", "encoder": "P"}
GATHER_RANKS = {"highway0": -8.0, ("encoder", "b"): 6.0}
SCATTER_KINDS = {"encoder": "P", "highway1": "Q", "highway0": "Q"}
READY = {
    ("encoder", "b"): 0.0,
    ("encoder", "a"): 5.0,
    "highway1": 9.0,
    "highway0": 13.0,
    "small": 30.0,
}
SCATTER_RANKS = {"encoder": -20.0, "highway1": -10.0}
BACK_TIMES = (9.0, 4.9)
POOL_TIMES = (4.0, 7.0, 10.0, 13.0, 15.0, 17.0)
POOL_BACK_TIMES = (15.0, 17.5, 20.0, 22.5, 25.0, 27.0)
POOL_CUTS = (0, 1, 2, 3, 5, 8)


def packed(values):
    width = 1024
    flat = [value.reshape(-1) for value in values]
    flat = [jnp.pad(value, (0, -value.shape[0] % width)).reshape(-1, width) for value in flat]
    rows = jnp.concatenate(flat, axis=0)
    return jnp.pad(rows, ((0, -rows.shape[0] % 16), (0, 0)))


def unpacked(rows, values):
    totals = []
    first = 0
    for value in values:
        count = -(-value.size // rows.shape[1])
        taken = rows[first : first + count].reshape(-1)
        totals.append(taken[: value.size].reshape(value.shape))
        first += count
    return totals


def per_device(
    char_ids,
    char_mask,
    word_lengths,
    char_table,
    conv_weight,
    conv_bias,
    highway_weight,
    highway_bias,
    proj_weight,
    qkv_weight,
    qv_bias,
    out_weight,
    up_weight,
    up_bias,
    down_weight,
    vector_biases,
    norm_gains,
    cotangent,
):
    f32 = jnp.float32
    bf16 = jnp.bfloat16
    own_filters = conv_weight.shape[1]
    widths = channel_widths(lax.axis_index("narrow") * own_filters, own_filters)
    tap_rows = jnp.arange(TAPS * CHAR_DIM, dtype=jnp.int32) // CHAR_DIM
    tap_mask = (tap_rows[:, None] < widths[None, :]).astype(bf16)
    tap_pad = ((0, LANES - TAPS * CHAR_DIM), (0, 0))
    masked_filters = jnp.pad(conv_weight * tap_mask, tap_pad)
    chan_scale = jnp.sqrt(TAPS / widths.astype(f32))
    word_count = char_ids.shape[0]
    seq_count = word_count // LENGTH
    places = jnp.arange(CHARS_MAX, dtype=jnp.int32)
    alive = (char_mask > 0) & (places[None, :] < word_lengths[:, None])
    picks = word_order(word_lengths)
    picks_low = picks.astype(bf16)
    told = jnp.concatenate(
        [jnp.where(alive, char_ids, -1), word_lengths[:, None]], axis=1
    ).astype(f32)
    told = jnp.dot(picks, told, precision=lax.Precision.HIGHEST)
    lens = told[:, CHARS_MAX:]
    tile_count = word_count // TILE
    longest = jnp.max(lens.astype(jnp.int32).reshape(tile_count, TILE), axis=1)
    tile_chunks = (longest + CHUNK - 1) // CHUNK
    spread_ids = jnp.pad(
        told[:, :CHARS_MAX].astype(jnp.int32),
        ((0, 0), (0, SLOTS - CHARS_MAX)),
        constant_values=-1,
    )
    spread_ids = spread_ids.reshape(tile_count, TILE, SLOTS // CHUNK, CHUNK)
    spread_ids = spread_ids.transpose(0, 2, 3, 1).reshape(-1, CHUNK * TILE)
    table_t = jnp.pad(
        jnp.tile(char_table.T, (TAPS, 1)), (tap_pad[0], (0, IDS - CHAR_VOCAB))
    )
    tap_lanes = (
        jnp.arange(LANES, dtype=jnp.int32)[None, :] // CHAR_DIM
        == jnp.arange(8, dtype=jnp.int32)[:, None]
    ).astype(f32)
    scale_row, bias_row = chan_scale[None, :], conv_bias[None, :]
    width_row = widths.astype(f32)[None, :]
    here = lax.axis_index("wide")
    core = lax.axis_index("narrow")
    routed = lax.axis_size("wide") == CHIPS
    width_proj, width_qkv, width_out = own_filters, 3 * qkv_weight.shape[2], out_weight.shape[0]
    width_up, width_down = up_weight.shape[1], down_weight.shape[0]
    feature_rows = qkv_weight.shape[0]
    first_rows = jnp.concatenate(
        [proj_weight.T, qkv_weight.reshape(feature_rows, width_qkv), out_weight.T], axis=1
    )
    second_rows = jnp.concatenate([up_weight, down_weight.T], axis=1)

    def whole_rows(shard):
        return lax.all_gather(shard, "wide", axis=0, tiled=True)

    def own_rows(terms):
        return lax.psum_scatter(terms.astype(f32), "wide", scatter_dimension=0, tiled=True)

    if routed:
        full, gather_plan = gather_matrices(
            {
                "highway0": [highway_weight[0, :, part] for part in range(2)],
                "highway1": [highway_weight[1, :, part] for part in range(2)],
                "encoder": [first_rows, second_rows],
            },
            GATHER_KINDS,
        )
        highway_full = [
            [full[f"highway{layer}", part] for part in "ab"] for layer in range(HW_LAYERS)
        ]
        gathered_blocks = {part: blocks_of(GATHER_KINDS["encoder"], part) for part in "ab"}
        scattered_blocks = {part: blocks_of(SCATTER_KINDS["encoder"], part) for part in "ab"}
        features = gathered_blocks["a"]
        first_full, second_full = [
            moved_blocks(
                [gather_plan.after_all(full["encoder", part][0], "encoder", part)]
                + full["encoder", part][1:],
                gathered_blocks[part],
                features,
                1,
            )[0]
            for part in "ab"
        ]
        feature_order = owners(features, here)
    else:
        highway_full = [
            [[whole_rows(highway_weight[layer, :, part])] for part in range(2)]
            for layer in range(HW_LAYERS)
        ]
        first_full, second_full = whole_rows(first_rows), whole_rows(second_rows)
        feature_order = jnp.arange(lax.axis_size("wide"), dtype=jnp.int32)
    cuts = [cut * tile_count // 16 for cut in POOL_CUTS] + [tile_count]
    pool_pieces = []
    for first, last, time in zip(cuts, cuts[1:], POOL_TIMES):
        rows = slice(first * TILE, last * TILE)
        id_rows = slice(first * (SLOTS // CHUNK), last * (SLOTS // CHUNK))
        chunks = tile_chunks[first:last]
        if routed:
            chunks = gather_plan.after(chunks, time)
        pool, pool_back = conv_calls((last - first) * TILE, own_filters)
        results = pool(
            chunks, spread_ids[id_rows], table_t, tap_lanes, masked_filters, scale_row, bias_row,
            lens[rows], width_row,
        )
        pool_pieces.append((rows, id_rows, first, last, pool_back, results))
    pooled = joined([results[1] for *_, results in pool_pieces])
    current = gelu_exact(pooled).astype(bf16)
    proj_t, qkv_full, out_t = jnp.split(
        first_full, [width_proj, width_proj + width_qkv], axis=1
    )
    up_full, down_t = jnp.split(second_full, [width_up], axis=1)
    feature_count = proj_t.shape[0]
    feature_picks = (
        feature_order[:, None] == jnp.arange(feature_order.shape[0], dtype=jnp.int32)[None, :]
    ).astype(f32)
    feature_places = (
        feature_order[:, None] * feature_rows + jnp.arange(feature_rows, dtype=jnp.int32)[None, :]
    ).reshape(-1)
    feature_moves = (
        feature_places[:, None] == jnp.arange(feature_count, dtype=jnp.int32)[None, :]
    ).astype(bf16)

    def pick_features(rows, picks):
        blocked = rows.reshape(rows.shape[0], -1, feature_rows)
        return jnp.einsum(
            "kwr,bw->kbr", blocked, picks, precision=lax.Precision.HIGHEST
        ).reshape(rows.shape)

    vector_biases = pick_features(vector_biases, feature_picks)
    norm_gains = pick_features(norm_gains, feature_picks)
    grad_output = jnp.dot(cotangent, feature_moves.T, preferred_element_type=f32).astype(bf16)
    grad_output = jnp.dot(picks_low, grad_output, preferred_element_type=f32)
    kept_layers = []
    block_count = 2 * own_filters // LANES
    for layer_index in range(HW_LAYERS):
        name = f"highway{layer_index}"
        orders = [jnp.arange(block_count, dtype=jnp.int32)] * 4
        if routed:
            orders = [
                owners(blocks_of(kinds[name], part), here)
                for kinds in (GATHER_KINDS, SCATTER_KINDS)
                for part in "ab"
            ]
        order = (jnp.stack(orders) - core * (block_count // 2)) % block_count
        *whole_input, rows_a, rows_b = permute_channels(order, current, swap(current))
        if routed:
            whole_input[0] = gather_plan.after_all(whole_input[0], name)
        pieces = highway_full[layer_index][0] + highway_full[layer_index][1]
        change, gate, mixed = mix_layer(whole_input, current, highway_bias[layer_index], pieces)
        kept_layers.append((order[:2], change, gate, current, pieces, (rows_a, rows_b)))
        current = mixed
    start_rows = (
        pair_sum(jnp.dot(current, proj_t.T, preferred_element_type=f32)) + vector_biases[0]
    )
    start_low = start_rows.astype(bf16)
    qkv_bias = jnp.concatenate([qv_bias[0], jnp.zeros_like(qv_bias[0]), qv_bias[1]])
    projected = (
        jnp.dot(start_low, qkv_full, preferred_element_type=f32) + qkv_bias
    ).astype(bf16)
    head_shape = (word_count, -1, HEAD_DIM)
    query, keys_here, values_here = [
        part.reshape(head_shape) for part in jnp.split(projected, 3, axis=1)
    ]
    attn_scale = HEAD_DIM ** (-0.5)
    sequence = jnp.arange(word_count, dtype=jnp.int32) // 8 % seq_count
    together = (sequence[:, None] == sequence[None, :])[None]
    scores = jnp.einsum("qhe,khe->hqk", query, keys_here, preferred_element_type=f32) * attn_scale
    scores = jnp.where(together, scores, -1e30)
    weights = jnp.exp(scores - jnp.max(scores, axis=-1, keepdims=True))
    probs = weights / jnp.sum(weights, axis=-1, keepdims=True)
    probs_low = probs.astype(bf16)
    context = (
        jnp.einsum("hqk,khe->qhe", probs_low, values_here, preferred_element_type=f32)
        .reshape(word_count, -1)
        .astype(bf16)
    )
    attended = pair_sum(jnp.dot(context, out_t.T, preferred_element_type=f32)) + vector_biases[1]
    before_one = start_rows + attended
    normed_one = layer_norm(before_one, norm_gains[0], vector_biases[3])
    normed_low = normed_one.astype(bf16)
    hidden_pre = jnp.dot(normed_low, up_full, preferred_element_type=f32) + up_bias
    hidden_low = gelu_exact(hidden_pre).astype(bf16)
    lowered = (
        pair_sum(jnp.dot(hidden_low, down_t.T, preferred_element_type=f32)) + vector_biases[2]
    )
    before_two = normed_one + lowered
    encoded = layer_norm(before_two, norm_gains[1], vector_biases[4]).astype(bf16)
    encoded = jnp.dot(encoded, feature_moves, preferred_element_type=f32).astype(bf16)
    encoded = jnp.dot(picks_low.T, encoded, preferred_element_type=f32).astype(bf16)
    if routed:
        scatter = Scatter(SCATTER_KINDS, READY)
    ln_two_back = jax.vjp(layer_norm, before_two, norm_gains[1], vector_biases[4])[1]
    grad_before_two, gain_two, bias_two = ln_two_back(grad_output)
    grad_lowered = grad_before_two.astype(bf16)
    down_grad_local = jnp.dot(grad_lowered.T, hidden_low, preferred_element_type=f32)
    bias_down = jnp.sum(grad_lowered.astype(f32), axis=0)
    grad_hidden = jnp.dot(grad_lowered, down_t, preferred_element_type=f32)
    grad_hidden_pre = jax.vjp(gelu_exact, hidden_pre)[1](grad_hidden)[0].astype(bf16)
    up_grad_local = jnp.dot(normed_low.T, grad_hidden_pre, preferred_element_type=f32)
    bias_up = jnp.sum(grad_hidden_pre.astype(f32), axis=0)
    grad_normed_one = grad_before_two + pair_grad_sum(
        jnp.dot(grad_hidden_pre, up_full.T, preferred_element_type=f32)
    )
    ln_one_back = jax.vjp(layer_norm, before_one, norm_gains[0], vector_biases[3])[1]
    grad_before_one, gain_one, bias_one = ln_one_back(grad_normed_one)
    grad_attended = grad_before_one.astype(bf16)
    out_grad_local = jnp.dot(grad_attended.T, context, preferred_element_type=f32)
    bias_attended = jnp.sum(grad_attended.astype(f32), axis=0)
    grad_context = (
        jnp.dot(grad_attended, out_t, preferred_element_type=f32)
        .astype(bf16)
        .reshape(head_shape)
    )
    grad_probs = jnp.einsum(
        "qhe,khe->hqk", grad_context, values_here, preferred_element_type=f32
    )
    grad_value = jnp.einsum("hqk,qhe->khe", probs_low, grad_context, preferred_element_type=f32)
    grad_scores = (
        probs * (grad_probs - jnp.sum(probs * grad_probs, axis=-1, keepdims=True))
    ).astype(bf16)
    grad_query = (
        jnp.einsum("hqk,khe->qhe", grad_scores, keys_here, preferred_element_type=f32) * attn_scale
    )
    grad_key = (
        jnp.einsum("hqk,qhe->khe", grad_scores, query, preferred_element_type=f32) * attn_scale
    )
    grad_projected = jnp.concatenate(
        [grad.reshape(word_count, -1).astype(bf16) for grad in (grad_query, grad_key, grad_value)],
        axis=1,
    )
    qkv_grad_local = jnp.dot(start_low.T, grad_projected, preferred_element_type=f32)
    bias_qkv = jnp.sum(grad_projected.astype(f32), axis=0).reshape(3, -1)
    bias_qv = bias_qkv[0::2]
    grad_start = grad_before_one + pair_grad_sum(
        jnp.dot(grad_projected, qkv_full.T, preferred_element_type=f32)
    )
    grad_start_low = grad_start.astype(bf16)
    proj_grad_local = jnp.dot(grad_start_low.T, current, preferred_element_type=f32)
    bias_start = jnp.sum(grad_start_low.astype(f32), axis=0)
    grad_current = jnp.dot(grad_start_low, proj_t, preferred_element_type=f32)
    first_grad_local = jnp.concatenate(
        [proj_grad_local, qkv_grad_local, out_grad_local], axis=1
    ).astype(bf16)
    second_grad_local = jnp.concatenate([up_grad_local, down_grad_local], axis=1).astype(bf16)
    if routed:
        for part, local in (("a", first_grad_local), ("b", second_grad_local)):
            scatter.terms["encoder", part] = moved_blocks([local], features, scattered_blocks[part], 4)
    highway_grads = []
    highway_bias_grads = []
    for layer_index in reversed(range(HW_LAYERS)):
        order, change, gate, carried, pieces, rows = kept_layers[layer_index]
        if routed:
            scatter.advance(READY[f"highway{layer_index}"])
            grad_current = scatter.plan.after(grad_current, BACK_TIMES[layer_index])
        part_grads, bias_sums, grad_own, grad_other = mix_layer_back(
            order, grad_current, change, gate, carried, pieces
        )
        terms = outer_products(rows, part_grads, len(pieces) // 2)
        if routed:
            scatter.terms.update(zip([(f"highway{layer_index}", part) for part in "ab"], terms))
        else:
            highway_grads.insert(0, jnp.stack([own_rows(joined(part)) for part in terms], axis=1))
        highway_bias_grads.insert(0, bias_sums)
        grad_current = add(grad_own, swap(grad_other))
    highway_bias_local = jnp.stack(highway_bias_grads)
    grad_pooled = jax.vjp(gelu_exact, pooled)[1](grad_current)[0]
    grad_filter = jnp.zeros((LANES, own_filters), f32)
    grad_marks = jnp.zeros((IDS, 2 * LANES), f32)
    for (rows, id_rows, first, last, pool_back, results), time in zip(pool_pieces, POOL_BACK_TIMES):
        chunks = tile_chunks[first:last]
        if routed:
            scatter.advance(time)
            chunks = scatter.plan.after(chunks, time - 1.0)
        grad_filter, grad_marks = pool_back(
            chunks, spread_ids[id_rows], tap_lanes, masked_filters, scale_row, lens[rows], width_row,
            results[0], results[2], grad_pooled[rows], grad_filter, grad_marks,
        )
    grad_filter = grad_filter[: TAPS * CHAR_DIM]
    grad_conv_bias = jnp.sum(grad_pooled, axis=0)
    grad_marks = grad_marks[:CHAR_VOCAB, :LANES] + grad_marks[:CHAR_VOCAB, LANES:]
    grad_chars = jnp.sum(
        grad_marks[:, : TAPS * CHAR_DIM].reshape(CHAR_VOCAB, TAPS, CHAR_DIM), axis=1
    )
    grad_filter = grad_filter * tap_mask.astype(f32)
    bias_local = pick_features(
        jnp.stack([bias_start, bias_attended, bias_down, bias_one, bias_two]), feature_picks.T
    )
    gain_local = pick_features(jnp.stack([gain_one, gain_two]), feature_picks.T)
    locals_small = (
        grad_filter,
        grad_conv_bias,
        highway_bias_local,
        bias_qv,
        bias_up,
        bias_local,
        gain_local,
        pair_sum(grad_chars),
    )
    if routed:
        scatter.small = packed(locals_small)
        scatter.advance(float("inf"))
        sums, small = scatter.sums()
        small_sums = unpacked(small, locals_small)
        highway_grads = [
            sums[f"highway{layer}"].reshape(highway_weight.shape[1:]) for layer in range(HW_LAYERS)
        ]
        first_grad, second_grad = jnp.split(sums["encoder"], [first_rows.shape[1]], axis=1)
    else:
        first_grad, second_grad = own_rows(first_grad_local), own_rows(second_grad_local)
        small_sums = lax.psum(locals_small, "wide")
    highway_grad = jnp.stack(highway_grads)
    proj_grad, qkv_grad, out_grad = jnp.split(
        first_grad, [width_proj, width_proj + width_qkv], axis=1
    )
    up_grad, down_grad = jnp.split(second_grad, [width_up], axis=1)
    proj_grad, out_grad, down_grad = proj_grad.T, out_grad.T, down_grad.T
    qkv_grad = qkv_grad.reshape(qkv_weight.shape)
    (
        conv_grad,
        conv_bias_grad,
        highway_bias_grad,
        qv_bias_grad,
        up_bias_grad,
        bias_grads,
        gain_grads,
        char_grad,
    ) = small_sums
    return (
        encoded,
        char_grad,
        conv_grad,
        conv_bias_grad,
        highway_grad,
        highway_bias_grad,
        proj_grad,
        qkv_grad,
        qv_bias_grad,
        out_grad,
        up_grad,
        up_bias_grad,
        down_grad,
        bias_grads,
        gain_grads,
    )


def solution(mesh):
    placed = (
        P("wide", None),
        P("wide", None),
        P("wide"),
        P(),
        P(None, "narrow"),
        P("narrow"),
        P(None, "wide", None, "narrow"),
        P(None, None, "narrow"),
        P("narrow", "wide"),
        P("wide", None, "narrow"),
        P(None, "narrow"),
        P("narrow", "wide"),
        P("wide", "narrow"),
        P("narrow"),
        P("narrow", "wide"),
        P(),
        P(),
        P("wide", None),
    )
    return jax.shard_map(
        per_device,
        mesh=mesh,
        in_specs=placed,
        out_specs=(
            P("wide", None),
            P(),
            P(None, "narrow"),
            P("narrow"),
            P(None, "wide", None, "narrow"),
            P(None, None, "narrow"),
            P("narrow", "wide"),
            P("wide", None, "narrow"),
            P(None, "narrow"),
            P("narrow", "wide"),
            P("wide", "narrow"),
            P("narrow"),
            P("narrow", "wide"),
            P(),
            P(),
        ),
        check_vma=False,
    )
```
